32 devices in a mesh: pages: 8 (over y, x, core), emb: 4 (over z).
Axes of the slice: x: 2, y: 2, z: 4, core: 2. Of those that a mesh axis runs over, the one named last changes fastest.
Arguments:
- text_embed: bfloat16 [16384, 1024], P(('pages', 'emb')), may hold values from -6 to 6
- boxes: int32 [4, 16384], P(None, ('pages', 'emb')), may hold values from 0 to 1000, as said below
- layout_tables: float32 [4, 1024, 1024], P('emb'), may hold values from -3 to 3
- emb_gain: float32 [1024], replicated, may hold values from 0.5 to 1.5
- emb_bias: float32 [1024], replicated, may hold values from -1.5 to 1.5
- w_qkv: bfloat16 [1024, 3072], replicated, may hold values from -0.1875 to 0.1875
- b_query: float32 [1024], replicated, may hold values from -1.5 to 1.5
- b_value: float32 [1024], replicated, may hold values from -1.5 to 1.5
- w_out: bfloat16 [1024, 1024], replicated, may hold values from -2 to 2
- b_out: float32 [1024], replicated, may hold values from -1.5 to 1.5
- attn_gain: float32 [1024], replicated, may hold values from 0.5 to 1.5
- attn_bias: float32 [1024], replicated, may hold values from -1.5 to 1.5
- w_in: bfloat16 [1024, 4096], replicated, may hold values from -0.1875 to 0.1875
- b_in: float32 [4096], replicated, may hold values from -1.5 to 1.5
- w_back: bfloat16 [4096, 1024], replicated, may hold values from -0.09375 to 0.09375
- b_back: float32 [1024], replicated, may hold values from -1.5 to 1.5
- ffn_gain: float32 [1024], replicated, may hold values from 0.5 to 1.5
- ffn_bias: float32 [1024], replicated, may hold values from -1.5 to 1.5
- cotangent: bfloat16 [16384, 1024], P(('pages', 'emb')), may hold values from -6 to 6
Outputs:
- output: bfloat16 [16384, 1024], P(('pages', 'emb'))
- grad_text: float32 [16384, 1024], P(('pages', 'emb'))
- grad_tables: float32 [4, 1024, 1024], P('emb', 'pages')
- grad_emb_gain: float32 [1024], P('pages')
- grad_emb_bias: float32 [1024], P('pages')
- grad_qkv: float32 [1024, 3072], P('pages')
- grad_query_bias: float32 [1024], P('pages')
- grad_value_bias: float32 [1024], P('pages')
- grad_out: float32 [1024, 1024], P('pages')
- grad_out_bias: float32 [1024], P('pages')
- grad_attn_gain: float32 [1024], P('pages')
- grad_attn_bias: float32 [1024], P('pages')
- grad_in: float32 [1024, 4096], P('pages')
- grad_in_bias: float32 [4096], P('pages')
- grad_back: float32 [4096, 1024], P('pages')
- grad_back_bias: float32 [1024], P('pages')
- grad_ffn_gain: float32 [1024], P('pages')
- grad_ffn_bias: float32 [1024], P('pages')
- rms_grad: float32 [], replicated
The draws below stay inside these ranges and needn't reach their ends.
Inputs may be any that keep to these rules, and one draw needn't show every extreme that they name: `boxes`: rows are left x, top y, right x, bottom y of each token's cell, with right >= left and bottom >= top.
All inputs are finite; a program needn't handle non-finite values.
Results may differ from the reference program's by a relative error of at most 0.014.
Values sent between devices are 32-bit elements; how exact they have to be, the bound alone decides.
No kernel may reach another device: no remote copies, remote signals or barrier semaphores. Data moves between devices by JAX's collectives and lax.ppermute only.
A program may use at most 256 MiB of HBM per device.

```python
import jax
import jax.numpy as jnp
from jax import lax

HEADS = 16
HEAD = 64
D = 1024
FF = 4096
TABLE = 1024
COORD = 1000
PAGE = 512
TOKENS = 16384


def draw_boxes(key, part):
    key = jax.random.fold_in(key, 11)
    subkeys = jax.random.split(key, 6)
    clusters = TOKENS // 16
    spread = max(COORD // 25, 1)
    centre_x = jax.random.randint(subkeys[0], (clusters, 1), 0, COORD + 1)
    centre_y = jax.random.randint(subkeys[1], (clusters, 1), 0, COORD + 1)
    left_x = jnp.clip(centre_x + jax.random.randint(subkeys[2], (clusters, 16), -spread, spread + 1), 0, COORD)
    top_y = jnp.clip(centre_y + jax.random.randint(subkeys[3], (clusters, 16), -spread, spread + 1), 0, COORD)
    reach_x = jax.random.randint(subkeys[4], (clusters, 16), 0, 4096)
    reach_y = jax.random.randint(subkeys[5], (clusters, 16), 0, 4096)
    right_x = left_x + reach_x * (COORD - left_x + 1) // 4096
    bottom_y = top_y + reach_y * (COORD - top_y + 1) // 4096
    stacked = jnp.stack([left_x, top_y, right_x, bottom_y]).reshape(4, TOKENS)
    stacked = stacked.at[0:2, 0].set(0).at[2:4, 1].set(COORD)
    return stacked.astype(jnp.int32)


def block_scale(stream_key, extent, shards, smallest, largest):
    loudness = 1.0
    for dim, shards_of in shards:
        heights = jax.random.uniform(jax.random.fold_in(jax.random.fold_in(stream_key, 6), dim), (shards_of,), jnp.float32, smallest / len(shards), largest / len(shards))
        loudness = loudness * jnp.repeat(jnp.exp(heights), extent[dim] // shards_of).reshape((-1,) + (1,) * (len(extent) - 1 - dim))
    return loudness


def bell_draw(rng, extent, scale, reach, cuts=(), kind=jnp.bfloat16):
    entries = jax.random.normal(rng, extent, jnp.float32) * scale
    if len(cuts) > 0:
        entries = block_scale(rng, extent, cuts, -0.22, 0.18) * entries
    return jnp.clip(entries, min=-reach, max=reach).astype(kind)


def setup_inputs(seed: int = 0) -> dict:
    arg_keys = jax.random.split(jax.random.key(seed), 20)
    text_embed = bell_draw(arg_keys[0], (TOKENS, D), 1.0, 6.0, ((0, 32),))
    boxes = draw_boxes(jax.random.fold_in(arg_keys[19], 71), 0)
    layout_tables = bell_draw(arg_keys[2], (4, TABLE, D), 0.5, 3.0, ((0, 4),), jnp.float32)
    emb_gain = jnp.clip(1.0 + 0.1 * jax.random.normal(arg_keys[3], (D,), jnp.float32), 0.5, 1.5)
    emb_bias = bell_draw(arg_keys[4], (D,), 0.3, 1.5, (), jnp.float32)
    w_qkv = bell_draw(arg_keys[5], (D, 3 * D), D ** -0.5, 0.1875)
    b_query = bell_draw(arg_keys[6], (D,), 0.3, 1.5, (), jnp.float32)
    b_value = bell_draw(arg_keys[7], (D,), 0.3, 1.5, (), jnp.float32)
    w_out = bell_draw(arg_keys[8], (D, D), (max(D // 128, 8)) ** -0.5, 2.0)
    b_out = bell_draw(arg_keys[9], (D,), 0.3, 1.5, (), jnp.float32)
    attn_gain = jnp.clip(1.0 + 0.1 * jax.random.normal(arg_keys[10], (D,), jnp.float32), 0.5, 1.5)
    attn_bias = bell_draw(arg_keys[11], (D,), 0.3, 1.5, (), jnp.float32)
    w_in = bell_draw(arg_keys[12], (D, FF), D ** -0.5, 0.1875)
    b_in = bell_draw(arg_keys[13], (FF,), 0.3, 1.5, (), jnp.float32)
    w_back = bell_draw(arg_keys[14], (FF, D), FF ** -0.5, 0.09375)
    b_back = bell_draw(arg_keys[15], (D,), 0.3, 1.5, (), jnp.float32)
    ffn_gain = jnp.clip(1.0 + 0.1 * jax.random.normal(arg_keys[16], (D,), jnp.float32), 0.5, 1.5)
    ffn_bias = bell_draw(arg_keys[17], (D,), 0.3, 1.5, (), jnp.float32)
    cotangent = bell_draw(arg_keys[18], (TOKENS, D), 1.0, 6.0, ((0, 32),))
    return dict(text_embed=text_embed, boxes=boxes, layout_tables=layout_tables, emb_gain=emb_gain, emb_bias=emb_bias, w_qkv=w_qkv, b_query=b_query, b_value=b_value, w_out=w_out, b_out=b_out, attn_gain=attn_gain, attn_bias=attn_bias, w_in=w_in, b_in=b_in, w_back=w_back, b_back=b_back, ffn_gain=ffn_gain, ffn_bias=ffn_bias, cotangent=cotangent)


EPSILON = 1e-05
HIGHEST = lax.Precision.HIGHEST

@jax.custom_vjp
def low(v):
    return lax.optimization_barrier(v.astype(jnp.bfloat16)).astype(jnp.float32)

@jax.custom_vjp
def low_back(v):
    return v

def low_keep(v):
    return (low(v), None)

def low_pass(kept, grad):
    return (grad,)

def back_keep(v):
    return (v, None)

def back_low(kept, grad):
    return (low(grad),)
low.defvjp(low_keep, low_pass)
low_back.defvjp(back_keep, back_low)

def layer_norm(values, gain, bias):
    averaged = lax.optimization_barrier(jnp.mean(values, -1, keepdims=True))
    centered = values - averaged
    variance = lax.optimization_barrier(jnp.mean(centered * centered, -1, keepdims=True))
    return centered * lax.rsqrt(variance + EPSILON) * gain + bias

def matmul(left, right):
    return jnp.dot(left, right, precision=HIGHEST, preferred_element_type=jnp.float32)

def page_group(params, text_rows, box_rows):
    tables, emb_gain, emb_bias, w_qkv, b_query, b_value, w_out, b_out, attn_gain, attn_bias, w_in, b_in, w_back, b_back, ffn_gain, ffn_bias = params
    left_x = box_rows[0]
    top_y = box_rows[1]
    right_x = box_rows[2]
    bottom_y = box_rows[3]
    layout = jnp.take(tables[0], left_x, axis=0) + jnp.take(tables[1], top_y, axis=0) + jnp.take(tables[0], right_x, axis=0) + jnp.take(tables[1], bottom_y, axis=0) + jnp.take(tables[2], right_x - left_x, axis=0) + jnp.take(tables[3], bottom_y - top_y, axis=0)
    hidden_emb = layer_norm(text_rows + layout, emb_gain, emb_bias)
    zeros_key = jnp.zeros_like(b_query)
    packed = low(low_back(matmul(low(hidden_emb), w_qkv) + jnp.concatenate([b_query, zeros_key, b_value])))
    split_heads = packed.reshape(-1, PAGE, 3, HEADS, HEAD)
    queries = split_heads[:, :, 0]
    key_rows = split_heads[:, :, 1]
    value_rows = split_heads[:, :, 2]
    scores = low_back(jnp.einsum('bqhe,bkhe->bhqk', queries, key_rows, precision=HIGHEST) * HEAD ** (-0.5))
    attn_probs = jax.nn.softmax(scores, axis=-1)
    context = jnp.einsum('bhqk,bkhe->bqhe', low(attn_probs), value_rows, precision=HIGHEST).reshape(-1, D)
    attended = low_back(matmul(low(low_back(context)), w_out) + b_out)
    hidden_attn = layer_norm(hidden_emb + attended, attn_gain, attn_bias)
    pre_act = low_back(matmul(low(hidden_attn), w_in) + b_in)
    expanded = low(jax.nn.gelu(pre_act, approximate=False))
    returned = low_back(matmul(expanded, w_back) + b_back)
    return layer_norm(hidden_attn + returned, ffn_gain, ffn_bias)

def reference(text_embed, boxes, layout_tables, emb_gain, emb_bias, w_qkv, b_query, b_value, w_out, b_out, attn_gain, attn_bias, w_in, b_in, w_back, b_back, ffn_gain, ffn_bias, cotangent):
    pages_total = TOKENS // PAGE
    group_pages = max((divisor for divisor in range(1, 9) if pages_total % divisor == 0))
    group_rows = group_pages * PAGE
    blocks = pages_total // group_pages
    wide = jnp.float32
    params = (layout_tables, emb_gain, emb_bias, w_qkv.astype(wide), b_query, b_value, w_out.astype(wide), b_out, attn_gain, attn_bias, w_in.astype(wide), b_in, w_back.astype(wide), b_back, ffn_gain, ffn_bias)
    text_blocks = text_embed.astype(wide).reshape(blocks, group_rows, D)
    box_blocks = jnp.transpose(boxes.reshape(4, blocks, group_rows), (1, 0, 2))
    checked = jax.checkpoint(page_group)

    def forward(weights, text_rows):
        return lax.map(lambda inputs: checked(weights, inputs[0], inputs[1]), (text_rows, box_blocks))
    result, pullback = jax.vjp(forward, params, text_blocks)
    grads, grad_text = pullback(cotangent.astype(wide).reshape(blocks, group_rows, D))
    output = result.reshape(TOKENS, D).astype(jnp.bfloat16)
    grad_flat = grad_text.reshape(TOKENS, D)
    rms_grad = jnp.sqrt(jnp.sum(grad_flat * grad_flat) / (TOKENS * D))
    return (output, grad_flat, grads[0], grads[1], grads[2], grads[3], grads[4], grads[5], grads[6], grads[7], grads[8], grads[9], grads[10], grads[11], grads[12], grads[13], grads[14], grads[15], rms_grad)
```

```python
import itertools

import jax
import jax.numpy as jnp
from jax import lax
from jax.sharding import PartitionSpec as P

HEADS = 16
HEAD = 64
PAGE = 512


EPSILON = 1e-05
SQRT_HALF = 0.7071067811865476
INV_ROOT_TAU = 0.3989422804014327


def normalize(values):
    averaged = jnp.mean(values, -1, keepdims=True)
    centered = values - averaged
    inverse = lax.rsqrt(jnp.mean(centered * centered, -1, keepdims=True) + EPSILON)
    return (centered * inverse, inverse)


def norm_back(incoming, normed, inverse, gain):
    scaled = incoming * gain
    offset_mean = jnp.mean(scaled, -1, keepdims=True)
    along_mean = jnp.mean(scaled * normed, -1, keepdims=True)
    return (
        inverse * (scaled - offset_mean - normed * along_mean),
        jnp.sum(incoming * normed, 0),
        jnp.sum(incoming, 0),
    )


def gelu_slope(pre_act):
    return (
        0.5 * (1.0 + lax.erf(pre_act * SQRT_HALF))
        + pre_act * jnp.exp(-0.5 * pre_act * pre_act) * INV_ROOT_TAU
    )


def matmul(left, right):
    return jnp.dot(left, right, preferred_element_type=jnp.float32)


def outer_sum(left, right):
    return jnp.einsum("ti,tj->ij", left, right, preferred_element_type=jnp.float32)


def back_mul(left, right):
    return jnp.einsum("tj,ij->ti", left, right, preferred_element_type=jnp.float32)


def owner_indices(box_rows, table_owner):
    left_x = box_rows[0]
    top_y = box_rows[1]
    right_x = box_rows[2]
    bottom_y = box_rows[3]
    first_idx = jnp.where(
        table_owner == 0,
        left_x,
        jnp.where(
            table_owner == 1, top_y, jnp.where(table_owner == 2, right_x - left_x, bottom_y - top_y)
        ),
    )
    second_idx = jnp.where(table_owner == 0, right_x, bottom_y)
    return (first_idx, second_idx)


def look_rows(table, first_idx, second_idx, table_owner):
    single = jnp.take(table, first_idx, axis=0)
    return lax.cond(
        table_owner < 2, lambda: single + jnp.take(table, second_idx, axis=0), lambda: single
    )


def segment_rows(incoming, index_rows, entries):
    return jax.ops.segment_sum(incoming, index_rows, num_segments=entries)


def table_rows_grad(incoming, first_idx, second_idx, table_owner, entries):
    single = segment_rows(incoming, first_idx, entries)
    return lax.cond(
        table_owner < 2,
        lambda: single + segment_rows(incoming, second_idx, entries),
        lambda: single,
    )


def relative(array, masks, me, lanes, first, last):
    blocks = []
    for flips in itertools.product((0, 1), repeat=len(masks)):
        offset = sum(mask for mask, flip in zip(masks, flips) if flip)
        start = jnp.bitwise_xor(me, offset) * lanes + first
        blocks.append(lax.dynamic_slice_in_dim(array, start, last - first, 1))
    return jnp.concatenate(blocks, 1)


def swap(array, mask):
    return lax.ppermute(
        array, "pages", [(one, one ^ mask) for one in range(lax.axis_size("pages"))]
    )


def halve(kept, masks):
    arrived = None
    for mask in masks:
        half = kept.shape[0] // 2
        sent = kept[half:] if arrived is None else kept[half:] + arrived[half:]
        kept = kept[:half] if arrived is None else kept[:half] + arrived[:half]
        arrived = swap(sent, mask)
    return kept if arrived is None else kept + arrived


def weight_share(left, right, masks):
    if len(masks) < 2:
        return halve(outer_sum(left, right), masks)
    half = left.shape[1] // 2
    quarter = half // 2
    from_core = swap(outer_sum(left[:, half:], right), masks[0])
    sent = outer_sum(left[:, quarter:half], right) + from_core[quarter:]
    arrived = swap(sent, masks[1])
    kept = outer_sum(left[:, :quarter], right) + from_core[:quarter]
    for mask in masks[2:]:
        half = kept.shape[0] // 2
        sent = kept[half:] + arrived[half:]
        kept = kept[:half] + arrived[:half]
        arrived = swap(sent, mask)
    return kept + arrived


def emb_total(share):
    if lax.axis_size("emb") != 4:
        return lax.psum(share, "emb")
    plane = lax.axis_index("emb")
    middle = jnp.logical_or(plane == 1, plane == 2)
    share = share + lax.ppermute(share, "emb", [(0, 1), (3, 2)])
    share = share + lax.ppermute(share, "emb", [(1, 2), (2, 1)])
    return jnp.where(middle, share, lax.ppermute(share, "emb", [(1, 0), (2, 3)]))


def on_device(
    text_embed,
    boxes,
    layout_tables,
    emb_gain,
    emb_bias,
    w_qkv,
    b_query,
    b_value,
    w_out,
    b_out,
    attn_gain,
    attn_bias,
    w_in,
    b_in,
    w_back,
    b_back,
    ffn_gain,
    ffn_bias,
    cotangent,
):
    wide = jnp.float32
    narrow = jnp.bfloat16
    token_rows = text_embed.shape[0]
    model_width = text_embed.shape[1]
    entries = layout_tables.shape[1]
    page_count = token_rows // PAGE
    score_scale = HEAD ** (-0.5)
    table_owner = lax.axis_index("emb")
    me = lax.axis_index("pages")
    devices = lax.axis_size("pages")
    outer_masks = [1 << bit for bit in range(1, devices.bit_length() - 1)]
    turn = len(outer_masks) // 2
    masks_one = [1] + outer_masks
    masks_two = [1] + outer_masks[turn:] + outer_masks[:turn]
    lanes = model_width // devices
    group_boxes = lax.all_gather(boxes, "emb", axis=1, tiled=True)
    first_idx, second_idx = owner_indices(group_boxes, table_owner)
    layout = lax.psum_scatter(
        look_rows(layout_tables[0], first_idx, second_idx, table_owner),
        "emb",
        scatter_dimension=0,
        tiled=True,
    )
    normed_emb, inverse_emb = normalize(text_embed.astype(wide) + layout)
    hidden_emb = normed_emb * emb_gain + emb_bias
    emb_low = hidden_emb.astype(narrow)
    bias_qkv = jnp.concatenate([b_query, jnp.zeros_like(b_query), b_value])
    packed = (matmul(emb_low, w_qkv) + bias_qkv).astype(narrow)
    split_heads = packed.reshape(page_count, PAGE, 3, HEADS, HEAD)
    queries = split_heads[:, :, 0]
    key_rows = split_heads[:, :, 1]
    value_rows = split_heads[:, :, 2]
    scores = (
        jnp.einsum("bqhe,bkhe->bhqk", queries, key_rows, preferred_element_type=wide) * score_scale
    )
    maxima = jnp.max(scores, -1, keepdims=True)
    exponent = jnp.exp(scores - maxima)
    summed = jnp.sum(exponent, -1, keepdims=True)
    attn_probs = exponent / summed
    log_total = maxima + jnp.log(summed)
    context = jnp.einsum(
        "bhqk,bkhe->bqhe", attn_probs.astype(narrow), value_rows, preferred_element_type=wide
    )
    context_low = context.reshape(token_rows, model_width).astype(narrow)
    attended = matmul(context_low, w_out) + b_out
    normed_attn, inverse_attn = normalize(hidden_emb + attended)
    hidden_attn = normed_attn * attn_gain + attn_bias
    attn_low = hidden_attn.astype(narrow)
    pre_act = matmul(attn_low, w_in) + b_in
    expanded = jax.nn.gelu(pre_act, approximate=False).astype(narrow)
    returned = matmul(expanded, w_back) + b_back
    normed_ffn, inverse_ffn = normalize(hidden_attn + returned)
    output = (normed_ffn * ffn_gain + ffn_bias).astype(narrow)
    d_r2, g_ffn_gain, g_ffn_bias = norm_back(
        cotangent.astype(wide), normed_ffn, inverse_ffn, ffn_gain
    )
    d_returned = d_r2.astype(narrow)
    wide_lanes = expanded.shape[1] // devices
    back_one = relative(expanded, masks_one, me, wide_lanes, 0, wide_lanes // 2)
    back_two = relative(expanded, masks_two, me, wide_lanes, wide_lanes // 2, wide_lanes)
    g_back = emb_total(
        jnp.concatenate(
            [
                weight_share(back_one, d_returned, masks_one),
                weight_share(back_two, d_returned, masks_two),
            ],
            0,
        )
    )
    g_back_bias = jnp.sum(d_returned.astype(wide), 0)
    d_pre = (back_mul(d_returned, w_back) * gelu_slope(pre_act)).astype(narrow)
    g_in = emb_total(
        jnp.concatenate(
            [
                weight_share(
                    relative(attn_low, masks_one, me, lanes, 0, lanes), d_pre[:, :2 * model_width], masks_one
                ),
                weight_share(
                    relative(attn_low, masks_two, me, lanes, 0, lanes), d_pre[:, 2 * model_width:], masks_two
                ),
            ],
            1,
        )
    )
    g_in_bias = jnp.sum(d_pre.astype(wide), 0)
    d_h1 = d_r2 + back_mul(d_pre, w_in)
    d_r1, g_attn_gain, g_attn_bias = norm_back(d_h1, normed_attn, inverse_attn, attn_gain)
    d_attended = d_r1.astype(narrow)
    g_out_bias = jnp.sum(d_attended.astype(wide), 0)
    d_context = back_mul(d_attended, w_out).astype(narrow).reshape(page_count, PAGE, HEADS, HEAD)
    scores_again = (
        jnp.einsum("bqhe,bkhe->bhqk", queries, key_rows, preferred_element_type=wide) * score_scale
    )
    probs_again = jnp.exp(scores_again - log_total)
    d_values = jnp.einsum(
        "bhqk,bqhe->bkhe", probs_again.astype(narrow), d_context, preferred_element_type=wide
    )
    d_probs = jnp.einsum("bqhe,bkhe->bhqk", d_context, value_rows, preferred_element_type=wide)
    d_scores = (probs_again * (d_probs - jnp.sum(probs_again * d_probs, -1, keepdims=True))).astype(
        narrow
    )
    d_queries = (
        jnp.einsum("bhqk,bkhe->bqhe", d_scores, key_rows, preferred_element_type=wide) * score_scale
    )
    d_keys = (
        jnp.einsum("bhqk,bqhe->bkhe", d_scores, queries, preferred_element_type=wide) * score_scale
    )
    d_packed = (
        jnp.stack([d_queries, d_keys, d_values], 2)
        .reshape(token_rows, 3 * model_width)
        .astype(narrow)
    )
    out_share = weight_share(
        relative(context_low, masks_one, me, lanes, 0, lanes), d_attended, masks_one
    )
    qkv_one = weight_share(
        relative(emb_low, masks_one, me, lanes, 0, lanes), d_packed[:, :model_width], masks_one
    )
    qkv_two = weight_share(
        relative(emb_low, masks_two, me, lanes, 0, lanes), d_packed[:, model_width:], masks_two
    )
    both = emb_total(jnp.concatenate([out_share, qkv_one, qkv_two], 1))
    g_out = both[:, :model_width]
    g_qkv = both[:, model_width:]
    g_query_bias = jnp.sum(d_packed[:, :model_width].astype(wide), 0)
    g_value_bias = jnp.sum(d_packed[:, 2 * model_width :].astype(wide), 0)
    d_h0 = d_r1 + back_mul(d_packed, w_qkv)
    d_embed, g_emb_gain, g_emb_bias = norm_back(d_h0, normed_emb, inverse_emb, emb_gain)
    vectors = [
        g_query_bias,
        g_value_bias,
        g_out_bias,
        g_attn_gain,
        g_attn_bias,
        g_in_bias,
        g_back_bias,
        g_ffn_gain,
        g_ffn_bias,
        g_emb_gain,
        g_emb_bias,
        jnp.full((devices,), jnp.sum(d_embed * d_embed)),
    ]
    stacked = jnp.concatenate([vector.reshape(devices, -1) for vector in vectors], 1)
    in_order = [
        lax.dynamic_slice_in_dim(
            stacked,
            jnp.bitwise_xor(me, sum(mask for mask, flip in zip(masks_one, flips) if flip)),
            1,
            0,
        )
        for flips in itertools.product((0, 1), repeat=len(masks_one))
    ]
    vector_share = emb_total(halve(jnp.concatenate(in_order, 0), masks_one))[0]
    totals = []
    first = 0
    for vector in vectors:
        length = vector.shape[0] // devices
        totals.append(vector_share[first : first + length])
        first += length
    entry_count = token_rows * model_width * lax.axis_size("pages") * lax.axis_size("emb")
    rms_grad = jnp.sqrt(totals[11][0] / entry_count)
    table_grad = table_rows_grad(
        lax.all_gather(d_embed, "emb", axis=0, tiled=True),
        first_idx,
        second_idx,
        table_owner,
        entries,
    )
    table_share = lax.psum_scatter(table_grad, "pages", scatter_dimension=0, tiled=True)
    return (
        output,
        d_embed,
        table_share[None],
        totals[9],
        totals[10],
        g_qkv,
        totals[0],
        totals[1],
        g_out,
        totals[2],
        totals[3],
        totals[4],
        g_in,
        totals[5],
        g_back,
        totals[6],
        totals[7],
        totals[8],
        rms_grad,
    )


def solution(mesh):
    return jax.shard_map(
        on_device,
        mesh=mesh,
        in_specs=(
            P(("pages", "emb"), None),
            P(None, ("pages", "emb")),
            P("emb", None, None),
            P(),
            P(),
            P(),
            P(),
            P(),
            P(),
            P(),
            P(),
            P(),
            P(),
            P(),
            P(),
            P(),
            P(),
            P(),
            P(("pages", "emb"), None),
        ),
        out_specs=(
            P(("pages", "emb"), None),
            P(("pages", "emb"), None),
            P("emb", "pages", None),
            P("pages"),
            P("pages"),
            P("pages", None),
            P("pages"),
            P("pages"),
            P("pages", None),
            P("pages"),
            P("pages"),
            P("pages"),
            P("pages", None),
            P("pages"),
            P("pages", None),
            P("pages"),
            P("pages"),
            P("pages"),
            P(),
        ),
        check_vma=False,
    )
```

```python
import itertools

import jax
import jax.numpy as jnp
from jax import lax
from jax.experimental import pallas as pl
from jax.experimental.pallas import tpu as pltpu
from jax.sharding import PartitionSpec as P

HEADS = 16
HEAD = 64
PAGE = 512


EPSILON = 1e-05
SQRT_HALF = 0.7071067811865476
INV_ROOT_TAU = 0.3989422804014327


def normalize(values):
    averaged = jnp.mean(values, -1, keepdims=True)
    centered = values - averaged
    inverse = lax.rsqrt(jnp.mean(centered * centered, -1, keepdims=True) + EPSILON)
    return (centered * inverse, inverse)


def norm_back(incoming, normed, inverse, gain):
    scaled = incoming * gain
    offset_mean = jnp.mean(scaled, -1, keepdims=True)
    along_mean = jnp.mean(scaled * normed, -1, keepdims=True)
    return (
        inverse * (scaled - offset_mean - normed * along_mean),
        jnp.sum(incoming * normed, 0),
        jnp.sum(incoming, 0),
    )


def gelu_slope(pre_act):
    return (
        0.5 * (1.0 + lax.erf(pre_act * SQRT_HALF))
        + pre_act * jnp.exp(-0.5 * pre_act * pre_act) * INV_ROOT_TAU
    )


def matmul(left, right):
    return jnp.dot(left, right, preferred_element_type=jnp.float32)


def outer_sum(left, right):
    return jnp.einsum("ti,tj->ij", left, right, preferred_element_type=jnp.float32)


def back_mul(left, right):
    return jnp.einsum("tj,ij->ti", left, right, preferred_element_type=jnp.float32)


def table_indices(box_rows, table):
    left_x, top_y, right_x, bottom_y = box_rows[0], box_rows[1], box_rows[2], box_rows[3]
    first = jnp.where(
        table == 0,
        left_x,
        jnp.where(table == 1, top_y, jnp.where(table == 2, right_x - left_x, bottom_y - top_y)),
    )
    second = jnp.where(table == 0, right_x, jnp.where(table == 1, bottom_y, -1))
    return first, second


def two_halves(values):
    high = values.astype(jnp.bfloat16)
    return high, (values - high.astype(jnp.float32)).astype(jnp.bfloat16)


def hits(entry, indices):
    return jnp.where(entry == indices, 1.0, 0.0)


def lookup_kernel(idx_ref, table_ref, total_ref, out_ref, halves):
    width = table_ref.shape[1]

    @pl.when(pl.program_id(0) == 0)
    def _():
        halves[:, :width], halves[:, width:] = two_halves(table_ref[...])

    entry = lax.broadcasted_iota(jnp.int32, (idx_ref.shape[0], table_ref.shape[0]), 1)
    counts = hits(entry, idx_ref[:, 0:1]) + hits(entry, idx_ref[:, 1:2])
    rows = jnp.dot(
        counts.astype(jnp.bfloat16), halves[...], preferred_element_type=jnp.float32
    )
    out_ref[...] = total_ref[...] + rows[:, :width] + rows[:, width:]


def add_rows(indices, table, total):
    tokens = total.shape[0]
    entries, width = table.shape
    block = PAGE
    return pl.pallas_call(
        lookup_kernel,
        grid=(tokens // block,),
        in_specs=[
            pl.BlockSpec((block, 2), lambda step: (step, 0)),
            pl.BlockSpec((entries, width), lambda step: (0, 0)),
            pl.BlockSpec((block, width), lambda step: (step, 0)),
        ],
        out_specs=pl.BlockSpec((block, width), lambda step: (step, 0)),
        out_shape=jax.ShapeDtypeStruct((tokens, width), jnp.float32),
        scratch_shapes=[pltpu.VMEM((entries, 2 * width), jnp.bfloat16)],
        input_output_aliases={2: 0},
        compiler_params=pltpu.CompilerParams(vmem_limit_bytes=32 * 2**20),
        cost_estimate=pl.CostEstimate(
            flops=4 * tokens * entries * width, bytes_accessed=12 * tokens * width, transcendentals=0
        ),
    )(indices, table, total)


def spread_kernel(idx_ref, rows_ref, out_ref):
    width = rows_ref.shape[1]
    entry = lax.broadcasted_iota(jnp.int32, (out_ref.shape[0], rows_ref.shape[0]), 0)
    counts = hits(entry, idx_ref[0:1, :]) + hits(entry, idx_ref[1:2, :])
    both = jnp.dot(
        counts.astype(jnp.bfloat16),
        jnp.concatenate(two_halves(rows_ref[...]), 1),
        preferred_element_type=jnp.float32,
    )
    share = both[:, :width] + both[:, width:]

    @pl.when(pl.program_id(0) == 0)
    def _():
        out_ref[...] = share

    @pl.when(pl.program_id(0) > 0)
    def _():
        out_ref[...] += share


def spread_rows(indices, rows, entries):
    tokens, width = rows.shape
    block = 2 * PAGE
    return pl.pallas_call(
        spread_kernel,
        grid=(tokens // block,),
        in_specs=[
            pl.BlockSpec((2, block), lambda step: (0, step)),
            pl.BlockSpec((block, width), lambda step: (step, 0)),
        ],
        out_specs=pl.BlockSpec((entries, width), lambda step: (0, 0)),
        out_shape=jax.ShapeDtypeStruct((entries, width), jnp.float32),
        compiler_params=pltpu.CompilerParams(vmem_limit_bytes=32 * 2**20),
        cost_estimate=pl.CostEstimate(
            flops=4 * tokens * entries * width, bytes_accessed=8 * tokens * width, transcendentals=0
        ),
    )(indices, rows)


def flips_of(masks):
    return [
        sum(mask for mask, flip in zip(masks, flips) if flip)
        for flips in itertools.product((0, 1), repeat=len(masks))
    ]


def relative(array, offsets, me, size, axis, first=0, last=None):
    last = size if last is None else last
    blocks = [
        lax.dynamic_slice_in_dim(
            array, jnp.bitwise_xor(me, offset) * size + first, last - first, axis
        )
        for offset in offsets
    ]
    return jnp.concatenate(blocks, axis)


def swap(array, mask):
    return lax.ppermute(
        array, "pages", [(one, one ^ mask) for one in range(lax.axis_size("pages"))]
    )


def fold(kept, arrived):
    half = kept.shape[0] // 2
    return kept[:half] + arrived[:half], kept[half:] + arrived[half:]


def halve(kept, masks):
    for mask in masks:
        half = kept.shape[0] // 2
        kept = kept[:half] + swap(kept[half:], mask)
    return kept


def in_order(*values):
    return lax.optimization_barrier(values)


class Share:
    def __init__(self, left, right, masks):
        self.left, self.right, self.masks = left, right, masks
        self.half = left.shape[1] // 2

    def send(self):
        return outer_sum(self.left[:, self.half :], self.right)

    def to_core(self, sent):
        self.arrived = swap(sent, self.masks[0])

    def next(self):
        quarter = self.half // 2
        sent = (
            outer_sum(self.left[:, quarter : self.half], self.right) + self.arrived[quarter:]
        )
        self.kept = outer_sum(self.left[:, :quarter], self.right) + self.arrived[:quarter]
        return sent

    def to_second(self, sent):
        self.arrived = swap(sent, self.masks[1])

    def third(self):
        for mask in self.masks[2:-1]:
            self.kept, sent = fold(self.kept, self.arrived)
            self.arrived = swap(sent, mask)
        self.kept, sent = fold(self.kept, self.arrived)
        return sent

    def to_last(self, sent):
        self.arrived = swap(sent, self.masks[-1])

    def result(self):
        return self.kept + self.arrived


def emb_total(share):
    if lax.axis_size("emb") != 4:
        return lax.psum(share, "emb")
    plane = lax.axis_index("emb")
    middle = jnp.logical_or(plane == 1, plane == 2)
    share = share + lax.ppermute(share, "emb", [(0, 1), (3, 2)])
    share = share + lax.ppermute(share, "emb", [(1, 2), (2, 1)])
    return jnp.where(middle, share, lax.ppermute(share, "emb", [(1, 0), (2, 3)]))


def on_device(
    text_embed,
    boxes,
    layout_tables,
    emb_gain,
    emb_bias,
    w_qkv,
    b_query,
    b_value,
    w_out,
    b_out,
    attn_gain,
    attn_bias,
    w_in,
    b_in,
    w_back,
    b_back,
    ffn_gain,
    ffn_bias,
    cotangent,
):
    wide = jnp.float32
    narrow = jnp.bfloat16
    token_rows = text_embed.shape[0]
    model_width = text_embed.shape[1]
    entries = layout_tables.shape[1]
    page_count = token_rows // PAGE
    score_scale = HEAD ** (-0.5)
    me = lax.axis_index("pages")
    plane = lax.axis_index("emb")
    devices = lax.axis_size("pages")
    planes = lax.axis_size("emb")
    outer_masks = [1 << bit for bit in range(1, devices.bit_length() - 1)]
    turn = len(outer_masks) // 2
    masks_one = [1] + outer_masks
    masks_two = [1] + outer_masks[turn:] + outer_masks[:turn]
    flips_one = flips_of(masks_one)
    flips_two = flips_of(masks_two)
    lanes = model_width // devices
    group = min(devices, 8)
    inner = me % group
    columns = model_width // group

    def around(array, offset):
        return lax.ppermute(
            array, "emb", [((one + offset) % planes, one) for one in range(planes)]
        )

    def exchange(blocks):
        return [blocks[0]] + [swap(blocks[offset], offset) for offset in range(1, group)]

    def in_columns(blocks):
        return relative(
            jnp.concatenate(blocks, 1), range(group), inner, blocks[0].shape[1], 1
        )

    own_columns = lax.dynamic_slice_in_dim(layout_tables[0], inner * columns, columns, 1)
    table_columns = [own_columns] + [around(own_columns, offset) for offset in range(1, planes)]
    group_boxes = lax.all_gather(
        boxes,
        "pages",
        axis=1,
        tiled=True,
        axis_index_groups=[
            list(range(first, first + group)) for first in range(0, devices, group)
        ],
    )
    group_boxes = relative(group_boxes, range(group), inner, token_rows, 1)
    table_uses = [
        jnp.stack(table_indices(group_boxes, (plane + offset) % planes))
        for offset in range(planes)
    ]
    looked_up = jnp.zeros((group * token_rows, columns), wide)
    for offset in [0, 1, planes - 1] + list(range(2, planes - 1)):
        looked_up = add_rows(table_uses[offset].T, table_columns[offset], looked_up)
    layout = in_columns(
        exchange(
            [looked_up[one * token_rows : (one + 1) * token_rows] for one in range(group)]
        )
    )
    normed_emb, inverse_emb = normalize(text_embed.astype(wide) + layout)
    hidden_emb = normed_emb * emb_gain + emb_bias
    emb_low = hidden_emb.astype(narrow)
    bias_qkv = jnp.concatenate([b_query, jnp.zeros_like(b_query), b_value])
    packed = (matmul(emb_low, w_qkv) + bias_qkv).astype(narrow)
    split_heads = packed.reshape(page_count, PAGE, 3, HEADS, HEAD)
    queries = split_heads[:, :, 0]
    key_rows = split_heads[:, :, 1]
    value_rows = split_heads[:, :, 2]
    scores = (
        jnp.einsum("bqhe,bkhe->bhqk", queries, key_rows, preferred_element_type=wide) * score_scale
    )
    maxima = jnp.max(scores, -1, keepdims=True)
    exponent = jnp.exp(scores - maxima)
    summed = jnp.sum(exponent, -1, keepdims=True)
    attn_probs = exponent / summed
    log_total = maxima + jnp.log(summed)
    context = jnp.einsum(
        "bhqk,bkhe->bqhe", attn_probs.astype(narrow), value_rows, preferred_element_type=wide
    )
    context_low = context.reshape(token_rows, model_width).astype(narrow)
    attended = matmul(context_low, w_out) + b_out
    normed_attn, inverse_attn = normalize(hidden_emb + attended)
    hidden_attn = normed_attn * attn_gain + attn_bias
    attn_low = hidden_attn.astype(narrow)
    pre_act = matmul(attn_low, w_in) + b_in
    expanded = jax.nn.gelu(pre_act, approximate=False).astype(narrow)
    returned = matmul(expanded, w_back) + b_back
    normed_ffn, inverse_ffn = normalize(hidden_attn + returned)
    output = (normed_ffn * ffn_gain + ffn_bias).astype(narrow)
    d_r2, g_ffn_gain, g_ffn_bias = norm_back(
        cotangent.astype(wide), normed_ffn, inverse_ffn, ffn_gain
    )
    d_returned = d_r2.astype(narrow)
    wide_lanes = expanded.shape[1] // devices
    half_lanes = wide_lanes // 2
    back_one = Share(
        relative(expanded, flips_one, me, wide_lanes, 1, 0, half_lanes), d_returned, masks_one
    )
    back_two = Share(
        relative(expanded, flips_two, me, wide_lanes, 1, half_lanes, wide_lanes),
        d_returned,
        masks_two,
    )
    sent_one, sent_two = back_one.send(), back_two.send()
    sent_one, sent_two, d_returned = in_order(sent_one, sent_two, d_returned)
    back_one.to_core(sent_one)
    back_two.to_core(sent_two)
    g_back_bias = jnp.sum(d_returned.astype(wide), 0)
    d_pre = (back_mul(d_returned, w_back) * gelu_slope(pre_act)).astype(narrow)
    attn_one = relative(attn_low, flips_one, me, lanes, 1)
    attn_two = relative(attn_low, flips_two, me, lanes, 1)
    in_one = Share(attn_one, d_pre[:, : 2 * model_width], masks_one)
    in_two = Share(attn_two, d_pre[:, 2 * model_width :], masks_two)
    sent_one, sent_two = in_one.send(), in_two.send()
    sent_one, sent_two, back_one.arrived, back_two.arrived = in_order(
        sent_one, sent_two, back_one.arrived, back_two.arrived
    )
    in_one.to_core(sent_one)
    in_two.to_core(sent_two)
    sent_one, sent_two = back_one.next(), back_two.next()
    sent_one, sent_two, in_one.arrived, in_two.arrived = in_order(
        sent_one, sent_two, in_one.arrived, in_two.arrived
    )
    back_one.to_second(sent_one)
    back_two.to_second(sent_two)
    sent_one, sent_two = in_one.next(), in_two.next()
    sent_one, sent_two, d_pre = in_order(sent_one, sent_two, d_pre)
    in_one.to_second(sent_one)
    in_two.to_second(sent_two)
    g_in_bias = jnp.sum(d_pre.astype(wide), 0)
    d_h1 = d_r2 + back_mul(d_pre, w_in)
    d_r1, g_attn_gain, g_attn_bias = norm_back(d_h1, normed_attn, inverse_attn, attn_gain)
    d_attended = d_r1.astype(narrow)
    g_out_bias = jnp.sum(d_attended.astype(wide), 0)
    out_one = Share(
        relative(context_low, flips_one, me, lanes, 1),
        d_attended[:, : model_width // 2],
        masks_one,
    )
    out_two = Share(
        relative(context_low, flips_two, me, lanes, 1),
        d_attended[:, model_width // 2 :],
        masks_two,
    )
    sent_one, sent_two = out_one.send(), out_two.send()
    sent_one, sent_two, d_attended = in_order(sent_one, sent_two, d_attended)
    out_one.to_core(sent_one)
    out_two.to_core(sent_two)
    d_context = back_mul(d_attended, w_out).astype(narrow).reshape(page_count, PAGE, HEADS, HEAD)
    d_probs = jnp.einsum("bqhe,bkhe->bhqk", d_context, value_rows, preferred_element_type=wide)
    sent_one, sent_two = back_one.third(), back_two.third()
    sent_one, sent_two, out_one.arrived, out_two.arrived, d_probs = in_order(
        sent_one, sent_two, out_one.arrived, out_two.arrived, d_probs
    )
    back_one.to_last(sent_one)
    back_two.to_last(sent_two)
    sent_one, sent_two = out_one.next(), out_two.next()
    sent_one, sent_two, d_probs = in_order(sent_one, sent_two, d_probs)
    out_one.to_second(sent_one)
    out_two.to_second(sent_two)
    scores_again = (
        jnp.einsum("bqhe,bkhe->bhqk", queries, key_rows, preferred_element_type=wide) * score_scale
    )
    probs_again = jnp.exp(scores_again - log_total)
    d_values = jnp.einsum(
        "bhqk,bqhe->bkhe", probs_again.astype(narrow), d_context, preferred_element_type=wide
    )
    d_scores = (probs_again * (d_probs - jnp.sum(probs_again * d_probs, -1, keepdims=True))).astype(
        narrow
    )
    d_queries = (
        jnp.einsum("bhqk,bkhe->bqhe", d_scores, key_rows, preferred_element_type=wide) * score_scale
    )
    d_keys = (
        jnp.einsum("bhqk,bqhe->bkhe", d_scores, queries, preferred_element_type=wide) * score_scale
    )
    d_packed = (
        jnp.stack([d_queries, d_keys, d_values], 2)
        .reshape(token_rows, 3 * model_width)
        .astype(narrow)
    )
    emb_one = relative(emb_low, flips_one, me, lanes, 1)
    emb_two = relative(emb_low, flips_two, me, lanes, 1)
    qkv_one = Share(emb_one, d_packed[:, : 3 * model_width // 2], masks_one)
    qkv_two = Share(emb_two, d_packed[:, 3 * model_width // 2 :], masks_two)
    sent_one, sent_two = qkv_one.send(), qkv_two.send()
    sent_one, sent_two, in_one.arrived, in_two.arrived, d_packed = in_order(
        sent_one, sent_two, in_one.arrived, in_two.arrived, d_packed
    )
    qkv_one.to_core(sent_one)
    qkv_two.to_core(sent_two)
    sent_one, sent_two = in_one.third(), in_two.third()
    back_share = jnp.concatenate([back_one.result(), back_two.result()], 0)
    sent_one, sent_two, d_packed, back_share = in_order(sent_one, sent_two, d_packed, back_share)
    in_one.to_last(sent_one)
    in_two.to_last(sent_two)
    g_back = emb_total(back_share)
    g_query_bias = jnp.sum(d_packed[:, :model_width].astype(wide), 0)
    g_value_bias = jnp.sum(d_packed[:, 2 * model_width :].astype(wide), 0)
    d_h0 = d_r1 + back_mul(d_packed, w_qkv)
    d_embed, g_emb_gain, g_emb_bias = norm_back(d_h0, normed_emb, inverse_emb, emb_gain)
    embed_blocks = [
        relative(d_embed, [offset], inner, columns, 1) for offset in range(group)
    ]
    embed_columns = jnp.concatenate(exchange(embed_blocks), 0)
    embed_columns, qkv_one.arrived, qkv_two.arrived = in_order(
        embed_columns, qkv_one.arrived, qkv_two.arrived
    )
    sent_one, sent_two = qkv_one.next(), qkv_two.next()
    qkv_one.to_second(sent_one)
    qkv_two.to_second(sent_two)
    table_total = None
    for offset in list(range(2, planes - 1)) + [1, planes - 1, 0]:
        part = spread_rows(table_uses[offset], embed_columns, entries)
        part = around(part, (planes - offset) % planes) if offset else part
        table_total = part if table_total is None else table_total + part
    row_masks = [mask for mask in masks_one if mask >= group]
    table_total = halve(
        relative(
            table_total,
            flips_of([mask // group for mask in row_masks]),
            me // group,
            entries * group // devices,
            0,
        ),
        row_masks,
    )
    table_share = in_columns(
        exchange(
            [
                relative(table_total, [offset], inner, entries // devices, 0)
                for offset in range(group)
            ]
        )
    )
    out_one.to_last(out_one.third())
    out_two.to_last(out_two.third())
    g_in = emb_total(jnp.concatenate([in_one.result(), in_two.result()], 1))
    g_out = emb_total(jnp.concatenate([out_one.result(), out_two.result()], 1))
    qkv_one.to_last(qkv_one.third())
    qkv_two.to_last(qkv_two.third())
    g_qkv = emb_total(jnp.concatenate([qkv_one.result(), qkv_two.result()], 1))
    vectors = [
        g_query_bias,
        g_value_bias,
        g_out_bias,
        g_attn_gain,
        g_attn_bias,
        g_in_bias,
        g_back_bias,
        g_ffn_gain,
        g_ffn_bias,
        g_emb_gain,
        g_emb_bias,
        jnp.full((devices,), jnp.sum(d_embed * d_embed)),
    ]
    stacked = jnp.concatenate([vector.reshape(devices, -1) for vector in vectors], 1)
    vector_share = emb_total(halve(relative(stacked, flips_one, me, 1, 0), masks_one))[0]
    totals = []
    first = 0
    for vector in vectors:
        length = vector.shape[0] // devices
        totals.append(vector_share[first : first + length])
        first += length
    entry_count = token_rows * model_width * devices * planes
    rms_grad = jnp.sqrt(totals[11][0] / entry_count)
    return (
        output,
        d_embed,
        table_share[None],
        totals[9],
        totals[10],
        g_qkv,
        totals[0],
        totals[1],
        g_out,
        totals[2],
        totals[3],
        totals[4],
        g_in,
        totals[5],
        g_back,
        totals[6],
        totals[7],
        totals[8],
        rms_grad,
    )


def solution(mesh):
    return jax.shard_map(
        on_device,
        mesh=mesh,
        in_specs=(
            P(("pages", "emb"), None),
            P(None, ("pages", "emb")),
            P("emb", None, None),
            P(),
            P(),
            P(),
            P(),
            P(),
            P(),
            P(),
            P(),
            P(),
            P(),
            P(),
            P(),
            P(),
            P(),
            P(),
            P(("pages", "emb"), None),
        ),
        out_specs=(
            P(("pages", "emb"), None),
            P(("pages", "emb"), None),
            P("emb", "pages", None),
            P("pages"),
            P("pages"),
            P("pages", None),
            P("pages"),
            P("pages"),
            P("pages", None),
            P("pages"),
            P("pages"),
            P("pages"),
            P("pages", None),
            P("pages"),
            P("pages", None),
            P("pages"),
            P("pages"),
            P("pages"),
            P(),
        ),
        check_vma=False,
    )
```

```python
import itertools

import jax
import jax.numpy as jnp
from jax import lax
from jax.experimental import pallas as pl
from jax.experimental.pallas import tpu as pltpu
from jax.sharding import PartitionSpec as P

HEADS = 16
HEAD = 64
PAGE = 512
PAIR = 2 * HEAD

EPSILON = 1e-05
SQRT_HALF = 0.7071067811865476
INV_ROOT_TAU = 0.3989422804014327

wide = jnp.float32
narrow = jnp.bfloat16
LITTLE = pl.CostEstimate(flops=1024, bytes_accessed=1024, transcendentals=0)
ROOM = pltpu.CompilerParams(vmem_limit_bytes=48 * 2**20)


def shape(dims, dtype=wide):
    return jax.ShapeDtypeStruct(dims, dtype)


def whole(*dims):
    return pl.BlockSpec(dims, lambda *_: (0,) * len(dims))


def normalize(values):
    averaged = jnp.mean(values, -1, keepdims=True)
    centered = values - averaged
    inverse = lax.rsqrt(jnp.mean(centered * centered, -1, keepdims=True) + EPSILON)
    return centered * inverse, inverse


def norm_back(incoming, normed, inverse, gain):
    scaled = incoming * gain
    offset_mean = jnp.mean(scaled, -1, keepdims=True)
    along_mean = jnp.mean(scaled * normed, -1, keepdims=True)
    return inverse * (scaled - offset_mean - normed * along_mean)


def down(values):
    return jnp.sum(values, 0, keepdims=True)


def mul(left, right):
    return jnp.dot(left, right, preferred_element_type=wide)


def mul_rows(left, right):
    return lax.dot_general(left, right, (((1,), (1,)), ((), ())), preferred_element_type=wide)


def mul_down(left, right):
    return lax.dot_general(left, right, (((0,), (0,)), ((), ())), preferred_element_type=wide)


def table_indices(box_rows, table):
    left_x, top_y, right_x, bottom_y = box_rows[0], box_rows[1], box_rows[2], box_rows[3]
    first = jnp.where(
        table == 0,
        left_x,
        jnp.where(table == 1, top_y, jnp.where(table == 2, right_x - left_x, bottom_y - top_y)),
    )
    second = jnp.where(table == 0, right_x, jnp.where(table == 1, bottom_y, -1))
    return first, second


def two_halves(values):
    high = values.astype(narrow)
    return high, (values - high.astype(wide)).astype(narrow)


def hits(entry, indices):
    return jnp.where(entry == indices, 1.0, 0.0)


def lookup_kernel(idx_ref, table_ref, total_ref, out_ref, halves):
    width = table_ref.shape[1]

    @pl.when(pl.program_id(0) == 0)
    def _():
        halves[:, :width], halves[:, width:] = two_halves(table_ref[...])

    entry = lax.broadcasted_iota(jnp.int32, (idx_ref.shape[0], table_ref.shape[0]), 1)
    counts = hits(entry, idx_ref[:, 0:1]) + hits(entry, idx_ref[:, 1:2])
    rows = mul(counts.astype(narrow), halves[...])
    out_ref[...] = total_ref[...] + rows[:, :width] + rows[:, width:]


def add_rows(indices, table, total):
    tokens = total.shape[0]
    entries, width = table.shape
    return pl.pallas_call(
        lookup_kernel,
        grid=(tokens // PAGE,),
        in_specs=[
            pl.BlockSpec((PAGE, 2), lambda step: (step, 0)),
            whole(entries, width),
            pl.BlockSpec((PAGE, width), lambda step: (step, 0)),
        ],
        out_specs=pl.BlockSpec((PAGE, width), lambda step: (step, 0)),
        out_shape=shape((tokens, width)),
        scratch_shapes=[pltpu.VMEM((entries, 2 * width), narrow)],
        input_output_aliases={2: 0},
        compiler_params=ROOM,
        cost_estimate=LITTLE,
        name="look_up",
    )(indices, table, total)


def spread_kernel(idx_ref, rows_ref, out_ref):
    width = rows_ref.shape[1]
    entry = lax.broadcasted_iota(jnp.int32, (out_ref.shape[0], rows_ref.shape[0]), 0)
    counts = hits(entry, idx_ref[0:1, :]) + hits(entry, idx_ref[1:2, :])
    both = mul(counts.astype(narrow), jnp.concatenate(two_halves(rows_ref[...]), 1))
    share = both[:, :width] + both[:, width:]

    @pl.when(pl.program_id(0) == 0)
    def _():
        out_ref[...] = share

    @pl.when(pl.program_id(0) > 0)
    def _():
        out_ref[...] += share


def spread_rows(indices, rows, entries):
    tokens, width = rows.shape
    block = 2 * PAGE
    return pl.pallas_call(
        spread_kernel,
        grid=(tokens // block,),
        in_specs=[
            pl.BlockSpec((2, block), lambda step: (0, step)),
            pl.BlockSpec((block, width), lambda step: (step, 0)),
        ],
        out_specs=whole(entries, width),
        out_shape=shape((entries, width)),
        compiler_params=ROOM,
        cost_estimate=LITTLE,
        name="spread",
    )(indices, rows)


def project_kernel(
    inner_ref, *refs
):
    group = len(refs) - 9
    parts = refs[:group]
    text, gain, bias, weight, weight_bias, packed, normed, inverse, low = refs[group:]
    width = parts[0].shape[1]

    @pl.when(pl.program_id(0) == 0)
    def _():
        for offset in range(group):
            place = pl.multiple_of(jnp.bitwise_xor(inner_ref[0], offset) * width, width)
            normed[:, pl.ds(place, width)] = parts[offset][...]
        normed[...], inverse[...] = normalize(normed[...] + text[...].astype(wide))
        low[...] = (normed[...] * gain[...] + bias[...]).astype(narrow)

    packed[...] = (mul(low[...], weight[...]) + weight_bias[...]).astype(narrow)


def embed_and_project(inner, parts, text, gain, bias, weight, weight_bias):
    tokens, width = text.shape
    block = width // 2
    steps = weight.shape[1] // block
    return pl.pallas_call(
        project_kernel,
        grid_spec=pltpu.PrefetchScalarGridSpec(
            num_scalar_prefetch=1,
            grid=(steps,),
            in_specs=[whole(*part.shape) for part in parts]
            + [
                whole(tokens, width),
                whole(1, width),
                whole(1, width),
                pl.BlockSpec((width, block), lambda step, *_: (0, step)),
                pl.BlockSpec((1, block), lambda step, *_: (0, step)),
            ],
            out_specs=[
                pl.BlockSpec((tokens, block), lambda step, *_: (0, step)),
                whole(tokens, width),
                whole(tokens, 1),
                whole(tokens, width),
            ],
        ),
        out_shape=[
            shape((tokens, weight.shape[1]), narrow),
            shape((tokens, width)),
            shape((tokens, 1)),
            shape((tokens, width), narrow),
        ],
        compiler_params=ROOM,
        cost_estimate=LITTLE,
        name="embed_and_project",
    )(inner, *parts, text, gain, bias, weight, weight_bias)


def one_head(rows, head):
    lane = lax.broadcasted_iota(jnp.int32, rows.shape, 1)
    return jnp.where((lane < HEAD) == (head == 0), rows, jnp.zeros_like(rows))


def head_probs(queries, keys, head):
    scores = mul_rows(one_head(queries, head), keys) * HEAD ** (-0.5)
    exponent = jnp.exp(scores - jnp.max(scores, -1, keepdims=True))
    return exponent * (1.0 / jnp.sum(exponent, -1, keepdims=True))


def attend_kernel(
    queries, keys, values, weight, weight_bias, normed_emb, emb_gain, emb_bias, gain, bias,
    context, normed, inverse, low, total,
):
    pair = pl.program_id(0)
    summed = None
    for head in range(2):
        probs = head_probs(queries[...], keys[...], head).astype(narrow)
        part = mul(probs, one_head(values[...], head))
        summed = part if summed is None else summed + part
    context[...] = summed.astype(narrow)
    share = mul(context[...], weight[...])

    @pl.when(pair == 0)
    def _():
        total[...] = share

    @pl.when(pair > 0)
    def _():
        total[...] += share

    @pl.when(pair == pl.num_programs(0) - 1)
    def _():
        hidden = normed_emb[...] * emb_gain[...] + emb_bias[...]
        normed[...], inverse[...] = normalize(hidden + (total[...] + weight_bias[...]))
        low[...] = (normed[...] * gain[...] + bias[...]).astype(narrow)


def attend(packed, weight, weight_bias, normed_emb, emb_gain, emb_bias, gain, bias):
    tokens, width = normed_emb.shape
    pairs = width // PAIR
    vector = whole(1, width)
    return pl.pallas_call(
        attend_kernel,
        grid=(pairs,),
        in_specs=[
            pl.BlockSpec((tokens, PAIR), lambda pair: (0, pair)),
            pl.BlockSpec((tokens, PAIR), lambda pair: (0, pairs + pair)),
            pl.BlockSpec((tokens, PAIR), lambda pair: (0, 2 * pairs + pair)),
            pl.BlockSpec((PAIR, width), lambda pair: (pair, 0)),
            vector,
            whole(tokens, width),
            vector,
            vector,
            vector,
            vector,
        ],
        out_specs=[
            pl.BlockSpec((tokens, PAIR), lambda pair: (0, pair)),
            whole(tokens, width),
            whole(tokens, 1),
            whole(tokens, width),
        ],
        out_shape=[
            shape((tokens, width), narrow),
            shape((tokens, width)),
            shape((tokens, 1)),
            shape((tokens, width), narrow),
        ],
        scratch_shapes=[pltpu.VMEM((tokens, width), wide)],
        compiler_params=ROOM,
        cost_estimate=LITTLE,
        name="attend",
    )(packed, packed, packed, weight, weight_bias, normed_emb, emb_gain, emb_bias, gain, bias)


def feed_kernel(
    low, w_in, b_in, w_back, b_back, normed_attn, attn_gain, attn_bias, gain, bias, cotangent,
    pre_act, expanded, output, d_r2, d_returned, g_gain, g_bias, g_back_bias, total,
):
    step = pl.program_id(0)
    pre = mul(low[...], w_in[...]) + b_in[...]
    pre_act[...] = pre
    expanded[...] = (pre * (0.5 * (1.0 + lax.erf(pre * SQRT_HALF)))).astype(narrow)
    share = mul(expanded[...], w_back[...])

    @pl.when(step == 0)
    def _():
        total[...] = share

    @pl.when(step > 0)
    def _():
        total[...] += share

    @pl.when(step == pl.num_programs(0) - 1)
    def _():
        hidden = normed_attn[...] * attn_gain[...] + attn_bias[...]
        normed, inverse = normalize(hidden + (total[...] + b_back[...]))
        output[...] = (normed * gain[...] + bias[...]).astype(narrow)
        incoming = cotangent[...].astype(wide)
        d_r2[...] = norm_back(incoming, normed, inverse, gain[...])
        g_gain[...] = down(incoming * normed)
        g_bias[...] = down(incoming)
        rounded = d_r2[...].astype(narrow)
        d_returned[...] = rounded
        g_back_bias[...] = down(rounded.astype(wide))


def feed(low, w_in, b_in, w_back, b_back, normed, attn_gain, attn_bias, gain, bias, cotangent):
    tokens, width = low.shape
    expand = w_in.shape[1]
    block = width // 2
    vector = whole(1, width)
    rows = whole(tokens, width)
    part = pl.BlockSpec((tokens, block), lambda step: (0, step))
    return pl.pallas_call(
        feed_kernel,
        grid=(expand // block,),
        in_specs=[
            rows,
            pl.BlockSpec((width, block), lambda step: (0, step)),
            pl.BlockSpec((1, block), lambda step: (0, step)),
            pl.BlockSpec((block, width), lambda step: (step, 0)),
            vector,
            rows,
            vector,
            vector,
            vector,
            vector,
            rows,
        ],
        out_specs=[part, part, rows, rows, rows, vector, vector, vector],
        out_shape=[
            shape((tokens, expand)),
            shape((tokens, expand), narrow),
            shape((tokens, width), narrow),
            shape((tokens, width)),
            shape((tokens, width), narrow),
            shape((1, width)),
            shape((1, width)),
            shape((1, width)),
        ],
        scratch_shapes=[pltpu.VMEM((tokens, width), wide)],
        compiler_params=ROOM,
        cost_estimate=LITTLE,
        name="feed",
    )(low, w_in, b_in, w_back, b_back, normed, attn_gain, attn_bias, gain, bias, cotangent)


def gelu_slope(pre_act):
    return (
        0.5 * (1.0 + lax.erf(pre_act * SQRT_HALF))
        + pre_act * jnp.exp(-0.5 * pre_act * pre_act) * INV_ROOT_TAU
    )


def feed_back_kernel(
    d_returned, w_back, pre_act, w_in, d_r2, normed, inverse, gain,
    d_pre, g_in_bias, d_r1, d_attended, g_gain, g_bias, g_out_bias, total,
):
    step = pl.program_id(0)
    rounded = (mul_rows(d_returned[...], w_back[...]) * gelu_slope(pre_act[...])).astype(narrow)
    d_pre[...] = rounded
    g_in_bias[...] = down(rounded.astype(wide))
    share = mul_rows(rounded, w_in[...])

    @pl.when(step == 0)
    def _():
        total[...] = share

    @pl.when(step > 0)
    def _():
        total[...] += share

    @pl.when(step == pl.num_programs(0) - 1)
    def _():
        incoming = d_r2[...] + total[...]
        d_r1[...] = norm_back(incoming, normed[...], inverse[...], gain[...])
        g_gain[...] = down(incoming * normed[...])
        g_bias[...] = down(incoming)
        d_attended[...] = d_r1[...].astype(narrow)
        g_out_bias[...] = down(d_attended[...].astype(wide))


def feed_back(d_returned, w_back, pre_act, w_in, d_r2, normed, inverse, gain):
    tokens, width = d_returned.shape
    expand = pre_act.shape[1]
    block = width // 2
    vector = whole(1, width)
    rows = whole(tokens, width)
    part = pl.BlockSpec((tokens, block), lambda step: (0, step))
    return pl.pallas_call(
        feed_back_kernel,
        grid=(expand // block,),
        in_specs=[
            rows,
            pl.BlockSpec((block, width), lambda step: (step, 0)),
            part,
            pl.BlockSpec((width, block), lambda step: (0, step)),
            rows,
            rows,
            whole(tokens, 1),
            vector,
        ],
        out_specs=[
            part,
            pl.BlockSpec((1, block), lambda step: (0, step)),
            rows,
            rows,
            vector,
            vector,
            vector,
        ],
        out_shape=[
            shape((tokens, expand), narrow),
            shape((1, expand)),
            shape((tokens, width)),
            shape((tokens, width), narrow),
            shape((1, width)),
            shape((1, width)),
            shape((1, width)),
        ],
        scratch_shapes=[pltpu.VMEM((tokens, width), wide)],
        compiler_params=ROOM,
        cost_estimate=LITTLE,
        name="feed_back",
    )(d_returned, w_back, pre_act, w_in, d_r2, normed, inverse, gain)


def attend_back_kernel(
    queries, keys, values, d_attended, weight, d_packed, g_query_bias, g_value_bias
):
    d_context = mul_rows(d_attended[...], weight[...]).astype(narrow)
    d_queries, d_keys, d_values = 0.0, 0.0, 0.0
    for head in range(2):
        probs = head_probs(queries[...], keys[...], head)
        own_context = one_head(d_context, head)
        d_values += mul_down(probs.astype(narrow), own_context)
        d_probs = mul_rows(own_context, values[...])
        along = jnp.sum(probs * d_probs, -1, keepdims=True)
        d_scores = (probs * (d_probs - along)).astype(narrow)
        d_queries += mul(d_scores, one_head(keys[...], head))
        d_keys += mul_down(d_scores, one_head(queries[...], head))
    d_queries = (d_queries * HEAD ** (-0.5)).astype(narrow)
    d_values = d_values.astype(narrow)
    d_packed[0] = d_queries
    d_packed[1] = (d_keys * HEAD ** (-0.5)).astype(narrow)
    d_packed[2] = d_values
    g_query_bias[...] = down(d_queries.astype(wide))
    g_value_bias[...] = down(d_values.astype(wide))


def attend_back(packed, d_attended, weight):
    tokens, width = d_attended.shape
    pairs = width // PAIR
    return pl.pallas_call(
        attend_back_kernel,
        grid=(pairs,),
        in_specs=[
            pl.BlockSpec((tokens, PAIR), lambda pair: (0, pair)),
            pl.BlockSpec((tokens, PAIR), lambda pair: (0, pairs + pair)),
            pl.BlockSpec((tokens, PAIR), lambda pair: (0, 2 * pairs + pair)),
            whole(tokens, width),
            pl.BlockSpec((PAIR, width), lambda pair: (pair, 0)),
        ],
        out_specs=[
            pl.BlockSpec((3, tokens, PAIR), lambda pair: (0, 0, pair)),
            pl.BlockSpec((1, PAIR), lambda pair: (0, pair)),
            pl.BlockSpec((1, PAIR), lambda pair: (0, pair)),
        ],
        out_shape=[shape((3, tokens, width), narrow), shape((1, width)), shape((1, width))],
        compiler_params=ROOM,
        cost_estimate=LITTLE,
        name="attend_back",
    )(packed, packed, packed, d_attended, weight)


def embed_back_kernel(inner_ref, d_packed, weight, d_r1, normed, inverse, gain, *refs):
    d_embed, g_gain, g_bias, squares = refs[:4]
    blocks, total = refs[4:-1], refs[-1]
    step = pl.program_id(0)
    share = mul_rows(d_packed[0], weight[...])

    @pl.when(step == 0)
    def _():
        total[...] = d_r1[...] + share

    @pl.when(step > 0)
    def _():
        total[...] += share

    @pl.when(step == pl.num_programs(0) - 1)
    def _():
        incoming = total[...]
        d_embed[...] = norm_back(incoming, normed[...], inverse[...], gain[...])
        g_gain[...] = down(incoming * normed[...])
        g_bias[...] = down(incoming)
        squares[...] = down(d_embed[...] * d_embed[...])
        columns = blocks[0].shape[1]
        for offset in range(len(blocks)):
            place = pl.multiple_of(jnp.bitwise_xor(inner_ref[0], offset) * columns, columns)
            blocks[offset][...] = d_embed[:, pl.ds(place, columns)]


def embed_back(inner, group, d_packed, weight, d_r1, normed, inverse, gain):
    tokens, width = d_r1.shape
    block = width // 2
    vector = whole(1, width)
    rows = whole(tokens, width)
    columns = width // group
    return pl.pallas_call(
        embed_back_kernel,
        grid_spec=pltpu.PrefetchScalarGridSpec(
            num_scalar_prefetch=1,
            grid=(3 * width // block,),
            in_specs=[
                pl.BlockSpec((1, tokens, block), lambda step, *_: (step // 2, 0, step % 2)),
                pl.BlockSpec((width, block), lambda step, *_: (0, step)),
                rows,
                rows,
                whole(tokens, 1),
                vector,
            ],
            out_specs=[rows, vector, vector, vector] + [whole(tokens, columns)] * group,
            scratch_shapes=[pltpu.VMEM((tokens, width), wide)],
        ),
        out_shape=[shape((tokens, width)), shape((1, width)), shape((1, width)), shape((1, width))]
        + [shape((tokens, columns))] * group,
        compiler_params=ROOM,
        cost_estimate=LITTLE,
        name="embed_back",
    )(inner, d_packed, weight, d_r1, normed, inverse, gain)


def outer_first_kernel(table_ref, *refs):
    half = len(refs) // 3
    for left, right, out in zip(refs[:half], refs[half : 2 * half], refs[2 * half :]):
        out[...] = mul(left[...], right[...].reshape(right.shape[-2:]))


def outer_next_kernel(table_ref, *refs):
    streams = len(refs) // 7
    for one in range(streams):
        right = refs[one][...]
        right = right.reshape(right.shape[-2:])
        for part in range(2):
            place = streams + 2 * one + part
            left, arrived, out = refs[place], refs[place + 2 * streams], refs[place + 4 * streams]
            out[...] = mul(left[...], right) + arrived[...]


class Shares:
    def __init__(self, me, streams):
        self.me, self.streams = me, streams
        self.devices = lax.axis_size("pages")
        self.tables = [
            jnp.bitwise_xor(me, jnp.array(flips_of(stream["masks"]), jnp.int32))
            * stream["units"]
            + stream["unit"]
            for stream in streams
        ]

    def right_spec(self, stream, splits):
        right, columns = stream["right"], stream["columns"] // splits
        first = stream["first"] * splits
        if right.ndim == 3:
            per = right.shape[2] // columns
            return pl.BlockSpec(
                (1, right.shape[1], columns),
                lambda row, col, *_: ((first + col) // per, 0, (first + col) % per),
            )
        return pl.BlockSpec((right.shape[0], columns), lambda row, col, *_: (0, first + col))

    def left_spec(self, stream, index, start):
        count = len(self.tables[0])
        return pl.BlockSpec(
            (stream["rows"], stream["left"].shape[1]),
            lambda row, col, table: (table[index * count + start + row], 0),
        )

    def first(self, splits=1):
        half = self.devices // 2
        streams = self.streams
        return pl.pallas_call(
            outer_first_kernel,
            grid_spec=pltpu.PrefetchScalarGridSpec(
                num_scalar_prefetch=1,
                grid=(half, splits),
                in_specs=[self.left_spec(one, i, half) for i, one in enumerate(streams)]
                + [self.right_spec(one, splits) for one in streams],
                out_specs=[
                    pl.BlockSpec(
                        (one["rows"], one["columns"] // splits), lambda row, col, *_: (row, col)
                    )
                    for one in streams
                ],
            ),
            out_shape=[shape((half * one["rows"], one["columns"])) for one in streams],
            compiler_params=ROOM,
            cost_estimate=LITTLE,
            name="outer_first",
        )(
            jnp.concatenate(self.tables),
            *[one["left"] for one in streams],
            *[one["right"] for one in streams],
        )

    def to_core(self, sent):
        self.arrived = [swap(one, 1) for one in sent]

    def next(self, splits=1):
        quarter = self.devices // 4
        streams = self.streams

        def block(one, start):
            return pl.BlockSpec(
                (one["rows"], one["columns"] // splits),
                lambda row, col, *_: (start + row, col),
            )

        results = pl.pallas_call(
            outer_next_kernel,
            grid_spec=pltpu.PrefetchScalarGridSpec(
                num_scalar_prefetch=1,
                grid=(quarter, splits),
                in_specs=[self.right_spec(one, splits) for one in streams]
                + [
                    self.left_spec(one, i, start)
                    for i, one in enumerate(streams)
                    for start in (0, quarter)
                ]
                + [block(one, start) for one in streams for start in (0, quarter)],
                out_specs=[block(one, 0) for one in streams for _ in range(2)],
            ),
            out_shape=[
                shape((quarter * one["rows"], one["columns"])) for one in streams for _ in range(2)
            ],
            compiler_params=ROOM,
            cost_estimate=LITTLE,
            name="outer_next",
        )(
            jnp.concatenate(self.tables),
            *[one["right"] for one in streams],
            *[one["left"] for one in streams for _ in range(2)],
            *[arrived for arrived in self.arrived for _ in range(2)],
        )
        self.kept = results[0::2]
        return results[1::2]

    def to_second(self, sent):
        self.arrived = [swap(one, s["masks"][1]) for one, s in zip(sent, self.streams)]

    def third(self):
        for step in range(2, len(self.streams[0]["masks"])):
            folded = [fold(kept, arrived) for kept, arrived in zip(self.kept, self.arrived)]
            self.kept = [one[0] for one in folded]
            sent = [one[1] for one in folded]
            if step == len(self.streams[0]["masks"]) - 1:
                return sent
            self.arrived = [swap(one, s["masks"][step]) for one, s in zip(sent, self.streams)]

    def to_last(self, sent):
        self.arrived = [swap(one, s["masks"][-1]) for one, s in zip(sent, self.streams)]

    def result(self):
        return [kept + arrived for kept, arrived in zip(self.kept, self.arrived)]


def flips_of(masks):
    return [
        sum(mask for mask, flip in zip(masks, flips) if flip)
        for flips in itertools.product((0, 1), repeat=len(masks))
    ]


def relative(array, offsets, me, size, axis):
    blocks = [
        lax.dynamic_slice_in_dim(array, jnp.bitwise_xor(me, offset) * size, size, axis)
        for offset in offsets
    ]
    return jnp.concatenate(blocks, axis)


def swap(array, mask):
    return lax.ppermute(
        array, "pages", [(one, one ^ mask) for one in range(lax.axis_size("pages"))]
    )


def fold(kept, arrived):
    half = kept.shape[0] // 2
    return kept[:half] + arrived[:half], kept[half:] + arrived[half:]


def halve(kept, masks):
    for mask in masks:
        half = kept.shape[0] // 2
        kept = kept[:half] + swap(kept[half:], mask)
    return kept


def in_order(*values):
    return lax.optimization_barrier(values)


def emb_total(share):
    if lax.axis_size("emb") != 4:
        return lax.psum(share, "emb")
    plane = lax.axis_index("emb")
    middle = jnp.logical_or(plane == 1, plane == 2)
    share = share + lax.ppermute(share, "emb", [(0, 1), (3, 2)])
    share = share + lax.ppermute(share, "emb", [(1, 2), (2, 1)])
    return jnp.where(middle, share, lax.ppermute(share, "emb", [(1, 0), (2, 3)]))


def on_device(
    text_embed,
    boxes,
    layout_tables,
    emb_gain,
    emb_bias,
    w_qkv,
    b_query,
    b_value,
    w_out,
    b_out,
    attn_gain,
    attn_bias,
    w_in,
    b_in,
    w_back,
    b_back,
    ffn_gain,
    ffn_bias,
    cotangent,
):
    token_rows = text_embed.shape[0]
    model_width = text_embed.shape[1]
    entries = layout_tables.shape[1]
    me = lax.axis_index("pages")
    plane = lax.axis_index("emb")
    devices = lax.axis_size("pages")
    planes = lax.axis_size("emb")
    outer_masks = [1 << bit for bit in range(1, devices.bit_length() - 1)]
    turn = len(outer_masks) // 2
    masks_one = [1] + outer_masks
    masks_two = [1] + outer_masks[turn:] + outer_masks[:turn]
    lanes = model_width // devices
    group = min(devices, 8)
    inner = me % group
    inner_list = inner.reshape(1).astype(jnp.int32)
    columns = model_width // group

    def row(vector):
        return vector.reshape(1, -1)

    def around(array, offset):
        return lax.ppermute(
            array, "emb", [((one + offset) % planes, one) for one in range(planes)]
        )

    def exchange(blocks):
        return [blocks[0]] + [swap(blocks[offset], offset) for offset in range(1, group)]

    own_columns = lax.dynamic_slice_in_dim(layout_tables[0], inner * columns, columns, 1)
    table_columns = [own_columns] + [around(own_columns, offset) for offset in range(1, planes)]
    group_boxes = lax.all_gather(
        boxes,
        "pages",
        axis=1,
        tiled=True,
        axis_index_groups=[
            list(range(first, first + group)) for first in range(0, devices, group)
        ],
    )
    group_boxes = relative(group_boxes, range(group), inner, token_rows, 1)
    table_uses = [
        jnp.stack(table_indices(group_boxes, (plane + offset) % planes))
        for offset in range(planes)
    ]
    looked_up = jnp.zeros((group * token_rows, columns), wide)
    for offset in [0, 1, planes - 1] + list(range(2, planes - 1)):
        looked_up = add_rows(table_uses[offset].T, table_columns[offset], looked_up)
    parts = exchange(
        [looked_up[one * token_rows : (one + 1) * token_rows] for one in range(group)]
    )

    bias_qkv = jnp.concatenate([b_query, jnp.zeros_like(b_query), b_value])
    packed, normed_emb, inverse_emb, emb_low = embed_and_project(
        inner_list, parts, text_embed, row(emb_gain), row(emb_bias), w_qkv, row(bias_qkv)
    )
    context_low, normed_attn, inverse_attn, attn_low = attend(
        packed,
        w_out,
        row(b_out),
        normed_emb,
        row(emb_gain),
        row(emb_bias),
        row(attn_gain),
        row(attn_bias),
    )
    pre_act, expanded, output, d_r2, d_returned, g_ffn_gain, g_ffn_bias, g_back_bias = feed(
        attn_low,
        w_in,
        row(b_in),
        w_back,
        row(b_back),
        normed_attn,
        row(attn_gain),
        row(attn_bias),
        row(ffn_gain),
        row(ffn_bias),
        cotangent,
    )

    def stream(left, right, masks, first=0, parts=1, units=1, unit=0):
        total = right.shape[-1] * (right.shape[0] if right.ndim == 3 else 1)
        return dict(
            left=left,
            rows=left.shape[0] // devices // units,
            units=units,
            unit=unit,
            right=right,
            columns=total // parts,
            first=first,
            masks=masks,
        )

    expanded_t = expanded.T
    back = Shares(
        me,
        [
            stream(expanded_t, d_returned, masks_one, units=2, unit=0),
            stream(expanded_t, d_returned, masks_two, units=2, unit=1),
        ],
    )
    sent = back.first()
    *sent, d_returned = in_order(*sent, d_returned)
    back.to_core(sent)
    d_pre, g_in_bias, d_r1, d_attended, g_attn_gain, g_attn_bias, g_out_bias = feed_back(
        d_returned, w_back, pre_act, w_in, d_r2, normed_attn, inverse_attn, row(attn_gain)
    )
    *back.arrived, d_pre = in_order(*back.arrived, d_pre)
    sent = back.next()
    *sent, d_pre = in_order(*sent, d_pre)
    back.to_second(sent)

    attn_t = attn_low.T
    inward = Shares(
        me,
        [
            stream(attn_t, d_pre, masks_one, 0, 2),
            stream(attn_t, d_pre, masks_two, 1, 2),
        ],
    )
    sent = inward.first()
    *sent, d_attended = in_order(*sent, d_attended)
    inward.to_core(sent)
    outward = Shares(
        me,
        [
            stream(context_low.T, d_attended, masks_one, 0, 2),
            stream(context_low.T, d_attended, masks_two, 1, 2),
        ],
    )
    sent = outward.first()
    *sent, d_attended = in_order(*sent, d_attended)
    outward.to_core(sent)
    *inward.arrived, d_attended = in_order(*inward.arrived, d_attended)
    sent = inward.next()
    *sent, d_attended = in_order(*sent, d_attended)
    inward.to_second(sent)

    d_packed, g_query_bias, g_value_bias = attend_back(packed, d_attended, w_out)

    *back.arrived, d_packed = in_order(*back.arrived, d_packed)
    sent = back.third()
    *sent, d_packed = in_order(*sent, d_packed)
    back.to_last(sent)
    *outward.arrived, d_packed = in_order(*outward.arrived, d_packed)
    sent = outward.next()
    *sent, d_packed = in_order(*sent, d_packed)
    outward.to_second(sent)

    emb_t = emb_low.T
    inmost = Shares(
        me,
        [
            stream(emb_t, d_packed, masks_one, 0, 2),
            stream(emb_t, d_packed, masks_two, 1, 2),
        ],
    )
    sent = inmost.first(3)
    *sent, d_packed = in_order(*sent, d_packed)
    inmost.to_core(sent)
    d_embed, g_emb_gain, g_emb_bias, squares, *embed_blocks = embed_back(
        inner_list, group, d_packed, w_qkv, d_r1, normed_emb, inverse_emb, row(emb_gain)
    )
    embed_columns = jnp.concatenate(exchange(embed_blocks), 0)

    *inward.arrived, embed_columns = in_order(*inward.arrived, embed_columns)
    sent = inward.third()
    *sent, embed_columns = in_order(*sent, embed_columns)
    inward.to_last(sent)
    *inmost.arrived, embed_columns = in_order(*inmost.arrived, embed_columns)
    sent = inmost.next(3)
    *sent, embed_columns = in_order(*sent, embed_columns)
    inmost.to_second(sent)
    back_share = jnp.concatenate(back.result(), 0)
    g_back = emb_total(back_share)

    table_total = None
    for offset in list(range(2, planes - 1)) + [1, planes - 1, 0]:
        part = spread_rows(table_uses[offset], embed_columns, entries)
        part = around(part, (planes - offset) % planes) if offset else part
        table_total = part if table_total is None else table_total + part
    row_masks = [mask for mask in masks_one if mask >= group]
    if row_masks:
        table_total = halve(
            relative(
                table_total,
                flips_of([mask // group for mask in row_masks]),
                me // group,
                entries * group // devices,
                0,
            ),
            row_masks,
        )
    table_parts = exchange(
        [relative(table_total, [offset], inner, entries // devices, 0) for offset in range(group)]
    )
    table_share = relative(jnp.concatenate(table_parts, 1), range(group), inner, columns, 1)

    outward.to_last(outward.third())
    g_in = emb_total(jnp.concatenate(inward.result(), 1))
    g_out = emb_total(jnp.concatenate(outward.result(), 1))
    inmost.to_last(inmost.third())
    g_qkv = emb_total(jnp.concatenate(inmost.result(), 1))

    vectors = [
        g_query_bias,
        g_value_bias,
        g_out_bias,
        g_attn_gain,
        g_attn_bias,
        g_in_bias,
        g_back_bias,
        g_ffn_gain,
        g_ffn_bias,
        g_emb_gain,
        g_emb_bias,
        jnp.full((devices,), jnp.sum(squares)),
    ]
    stacked = jnp.concatenate([vector.reshape(devices, -1) for vector in vectors], 1)
    vector_share = emb_total(
        halve(relative(stacked, flips_of(masks_one), me, 1, 0), masks_one)
    )[0]
    totals = []
    first = 0
    for vector in vectors:
        length = vector.size // devices
        totals.append(vector_share[first : first + length])
        first += length
    entry_count = token_rows * model_width * devices * planes
    rms_grad = jnp.sqrt(totals[11][0] / entry_count)
    return (
        output,
        d_embed,
        table_share[None],
        totals[9],
        totals[10],
        g_qkv,
        totals[0],
        totals[1],
        g_out,
        totals[2],
        totals[3],
        totals[4],
        g_in,
        totals[5],
        g_back,
        totals[6],
        totals[7],
        totals[8],
        rms_grad,
    )


def solution(mesh):
    return jax.shard_map(
        on_device,
        mesh=mesh,
        in_specs=(
            P(("pages", "emb"), None),
            P(None, ("pages", "emb")),
            P("emb", None, None),
            P(),
            P(),
            P(),
            P(),
            P(),
            P(),
            P(),
            P(),
            P(),
            P(),
            P(),
            P(),
            P(),
            P(),
            P(),
            P(("pages", "emb"), None),
        ),
        out_specs=(
            P(("pages", "emb"), None),
            P(("pages", "emb"), None),
            P("emb", "pages", None),
            P("pages"),
            P("pages"),
            P("pages", None),
            P("pages"),
            P("pages"),
            P("pages", None),
            P("pages"),
            P("pages"),
            P("pages"),
            P("pages", None),
            P("pages"),
            P("pages", None),
            P("pages"),
            P("pages"),
            P("pages"),
            P(),
        ),
        check_vma=False,
    )
```

```python
import functools
import itertools

import jax
import jax.numpy as jnp
from jax import lax
from jax.experimental import pallas as pl
from jax.experimental.pallas import tpu as pltpu
from jax.sharding import PartitionSpec as P

HEADS = 16
HEAD = 64
PAGE = 512
PAIR = 2 * HEAD

EPSILON = 1e-05
SQRT_HALF = 0.7071067811865476
INV_ROOT_TAU = 0.3989422804014327

wide = jnp.float32
narrow = jnp.bfloat16
ATTEND_PARTS = 4
ORDER = (
    "first back",
    "feed all",
    "first in",
    "attend all",
    "first q1",
    "first q2",
    "next in",
    "embed all",
    "next q1",
    "fold in",
    "finish back",
    "spread 0",
    "spread 1",
    "spread 2",
    "spread 3",
    "fold q1",
    "exchange back",
    "finish in",
    "next q2",
    "tables 0",
    "return back",
    "finish q1",
    "exchange in",
    "fold q2",
    "vector 0",
    "tables 1",
    "end back",
    "return in",
    "exchange q1",
    "finish q2",
    "vector 1",
    "return q1",
    "exchange q2",
    "vector 2",
    "end in",
    "return q2",
    "vector 3",
    "end q1",
    "end q2",
    "vector 4",
)
LITTLE = pl.CostEstimate(flops=1024, bytes_accessed=1024, transcendentals=0)
ROOM = pltpu.CompilerParams(vmem_limit_bytes=48 * 2**20)


def shape(dims, dtype=wide):
    return jax.ShapeDtypeStruct(dims, dtype)


def whole(*dims):
    return pl.BlockSpec(dims, lambda *_: (0,) * len(dims))


def normalize(values):
    averaged = jnp.mean(values, -1, keepdims=True)
    centered = values - averaged
    inverse = lax.rsqrt(jnp.mean(centered * centered, -1, keepdims=True) + EPSILON)
    return centered * inverse, inverse


def norm_back(incoming, normed, inverse, gain):
    scaled = incoming * gain
    offset_mean = jnp.mean(scaled, -1, keepdims=True)
    along_mean = jnp.mean(scaled * normed, -1, keepdims=True)
    return inverse * (scaled - offset_mean - normed * along_mean)


def down(values):
    return jnp.sum(values, 0, keepdims=True)


def mul(left, right):
    return jnp.dot(left, right, preferred_element_type=wide)


def mul_rows(left, right):
    return lax.dot_general(left, right, (((1,), (1,)), ((), ())), preferred_element_type=wide)


def mul_down(left, right):
    return lax.dot_general(left, right, (((0,), (0,)), ((), ())), preferred_element_type=wide)


def table_indices(box_rows, table):
    left_x, top_y, right_x, bottom_y = box_rows[0], box_rows[1], box_rows[2], box_rows[3]
    first = jnp.where(
        table == 0,
        left_x,
        jnp.where(table == 1, top_y, jnp.where(table == 2, right_x - left_x, bottom_y - top_y)),
    )
    second = jnp.where(table == 0, right_x, jnp.where(table == 1, bottom_y, -1))
    return first, second


def two_halves(values):
    high = values.astype(narrow)
    return high, (values - high.astype(wide)).astype(narrow)


def hits(entry, indices):
    return jnp.where(entry == indices, 1.0, 0.0)


def lookup_kernel(idx_ref, table_ref, total_ref, out_ref, halves):
    width = table_ref.shape[1]

    @pl.when(pl.program_id(0) == 0)
    def _():
        halves[:, :width], halves[:, width:] = two_halves(table_ref[...])

    entry = lax.broadcasted_iota(jnp.int32, (idx_ref.shape[0], table_ref.shape[0]), 1)
    counts = hits(entry, idx_ref[:, 0:1]) + hits(entry, idx_ref[:, 1:2])
    rows = mul(counts.astype(narrow), halves[...])
    out_ref[...] = total_ref[...] + rows[:, :width] + rows[:, width:]


def add_rows(indices, table, total):
    tokens = total.shape[0]
    entries, width = table.shape
    return pl.pallas_call(
        lookup_kernel,
        grid=(tokens // PAGE,),
        in_specs=[
            pl.BlockSpec((PAGE, 2), lambda step: (step, 0)),
            whole(entries, width),
            pl.BlockSpec((PAGE, width), lambda step: (step, 0)),
        ],
        out_specs=pl.BlockSpec((PAGE, width), lambda step: (step, 0)),
        out_shape=shape((tokens, width)),
        scratch_shapes=[pltpu.VMEM((entries, 2 * width), narrow)],
        input_output_aliases={2: 0},
        compiler_params=ROOM,
        cost_estimate=LITTLE,
        name="look_up",
    )(indices, table, total)


def spread_kernel(idx_ref, rows_ref, out_ref):
    width = rows_ref.shape[1]
    entry = lax.broadcasted_iota(jnp.int32, (out_ref.shape[0], rows_ref.shape[0]), 0)
    counts = hits(entry, idx_ref[0:1, :]) + hits(entry, idx_ref[1:2, :])
    both = mul(counts.astype(narrow), jnp.concatenate(two_halves(rows_ref[...]), 1))
    share = both[:, :width] + both[:, width:]

    @pl.when(pl.program_id(0) == 0)
    def _():
        out_ref[...] = share

    @pl.when(pl.program_id(0) > 0)
    def _():
        out_ref[...] += share


def spread_rows(indices, rows, entries):
    tokens, width = rows.shape
    block = 2 * PAGE
    return pl.pallas_call(
        spread_kernel,
        grid=(tokens // block,),
        in_specs=[
            pl.BlockSpec((2, block), lambda step: (0, step)),
            pl.BlockSpec((block, width), lambda step: (step, 0)),
        ],
        out_specs=whole(entries, width),
        out_shape=shape((entries, width)),
        compiler_params=ROOM,
        cost_estimate=LITTLE,
        name="spread",
    )(indices, rows)


def project_kernel(
    parts, text, gain, bias, weight, weight_bias, packed, normed, inverse, low
):
    group, _, width = parts.shape

    @pl.when(pl.program_id(0) == 0)
    def _():
        for one in range(group):
            normed[:, one * width : (one + 1) * width] = parts[one]
        normed[...], inverse[...] = normalize(normed[...] + text[...].astype(wide))
        low[...] = (normed[...] * gain[...] + bias[...]).astype(narrow)

    packed[...] = (mul(low[...], weight[...]) + weight_bias[...]).astype(narrow)


def embed_and_project(parts, text, gain, bias, weight, weight_bias):
    tokens, width = text.shape
    block = width // 2
    steps = weight.shape[1] // block
    return pl.pallas_call(
        project_kernel,
        grid=(steps,),
        in_specs=[
            whole(*parts.shape),
            whole(tokens, width),
            whole(1, width),
            whole(1, width),
            pl.BlockSpec((width, block), lambda step: (0, step)),
            pl.BlockSpec((1, block), lambda step: (0, step)),
        ],
        out_specs=[
            pl.BlockSpec((tokens, block), lambda step: (0, step)),
            whole(tokens, width),
            whole(tokens, 1),
            whole(tokens, width),
        ],
        out_shape=[
            shape((tokens, weight.shape[1]), narrow),
            shape((tokens, width)),
            shape((tokens, 1)),
            shape((tokens, width), narrow),
        ],
        compiler_params=ROOM,
        cost_estimate=LITTLE,
        name="embed_and_project",
    )(parts, text, gain, bias, weight, weight_bias)


def one_head(rows, head):
    lane = lax.broadcasted_iota(jnp.int32, rows.shape, 1)
    return jnp.where((lane < HEAD) == (head == 0), rows, jnp.zeros_like(rows))


def head_probs(queries, keys, head):
    scores = mul_rows(one_head(queries, head), keys) * HEAD ** (-0.5)
    exponent = jnp.exp(scores - jnp.max(scores, -1, keepdims=True))
    return exponent * (1.0 / jnp.sum(exponent, -1, keepdims=True))


def attend_kernel(
    queries, keys, values, weight, weight_bias, normed_emb, emb_gain, emb_bias, gain, bias,
    context, normed, inverse, low, total,
):
    pair = pl.program_id(0)
    summed = None
    for head in range(2):
        probs = head_probs(queries[...], keys[...], head).astype(narrow)
        part = mul(probs, one_head(values[...], head))
        summed = part if summed is None else summed + part
    context[...] = summed.astype(narrow)
    share = mul(context[...], weight[...])

    @pl.when(pair == 0)
    def _():
        total[...] = share

    @pl.when(pair > 0)
    def _():
        total[...] += share

    @pl.when(pair == pl.num_programs(0) - 1)
    def _():
        hidden = normed_emb[...] * emb_gain[...] + emb_bias[...]
        normed[...], inverse[...] = normalize(hidden + (total[...] + weight_bias[...]))
        low[...] = (normed[...] * gain[...] + bias[...]).astype(narrow)


def attend(packed, weight, weight_bias, normed_emb, emb_gain, emb_bias, gain, bias):
    tokens, width = normed_emb.shape
    pairs = width // PAIR
    vector = whole(1, width)
    return pl.pallas_call(
        attend_kernel,
        grid=(pairs,),
        in_specs=[
            pl.BlockSpec((tokens, PAIR), lambda pair: (0, pair)),
            pl.BlockSpec((tokens, PAIR), lambda pair: (0, pairs + pair)),
            pl.BlockSpec((tokens, PAIR), lambda pair: (0, 2 * pairs + pair)),
            pl.BlockSpec((PAIR, width), lambda pair: (pair, 0)),
            vector,
            whole(tokens, width),
            vector,
            vector,
            vector,
            vector,
        ],
        out_specs=[
            pl.BlockSpec((tokens, PAIR), lambda pair: (0, pair)),
            whole(tokens, width),
            whole(tokens, 1),
            whole(tokens, width),
        ],
        out_shape=[
            shape((tokens, width), narrow),
            shape((tokens, width)),
            shape((tokens, 1)),
            shape((tokens, width), narrow),
        ],
        scratch_shapes=[pltpu.VMEM((tokens, width), wide)],
        compiler_params=ROOM,
        cost_estimate=LITTLE,
        name="attend",
    )(packed, packed, packed, weight, weight_bias, normed_emb, emb_gain, emb_bias, gain, bias)


def feed_kernel(
    low, w_in, b_in, w_back, b_back, normed_attn, attn_gain, attn_bias, gain, bias, cotangent,
    pre_act, expanded, output, d_r2, d_returned, g_gain, g_bias, g_back_bias, total,
):
    step = pl.program_id(0)
    pre = mul(low[...], w_in[...]) + b_in[...]
    pre_act[...] = pre
    expanded[...] = (pre * (0.5 * (1.0 + lax.erf(pre * SQRT_HALF)))).astype(narrow)
    share = mul(expanded[...], w_back[...])

    @pl.when(step == 0)
    def _():
        total[...] = share

    @pl.when(step > 0)
    def _():
        total[...] += share

    @pl.when(step == pl.num_programs(0) - 1)
    def _():
        hidden = normed_attn[...] * attn_gain[...] + attn_bias[...]
        normed, inverse = normalize(hidden + (total[...] + b_back[...]))
        output[...] = (normed * gain[...] + bias[...]).astype(narrow)
        incoming = cotangent[...].astype(wide)
        d_r2[...] = norm_back(incoming, normed, inverse, gain[...])
        g_gain[...] = down(incoming * normed)
        g_bias[...] = down(incoming)
        rounded = d_r2[...].astype(narrow)
        d_returned[...] = rounded
        g_back_bias[...] = down(rounded.astype(wide))


def feed(low, w_in, b_in, w_back, b_back, normed, attn_gain, attn_bias, gain, bias, cotangent):
    tokens, width = low.shape
    expand = w_in.shape[1]
    block = width // 2
    vector = whole(1, width)
    rows = whole(tokens, width)
    part = pl.BlockSpec((tokens, block), lambda step: (0, step))
    return pl.pallas_call(
        feed_kernel,
        grid=(expand // block,),
        in_specs=[
            rows,
            pl.BlockSpec((width, block), lambda step: (0, step)),
            pl.BlockSpec((1, block), lambda step: (0, step)),
            pl.BlockSpec((block, width), lambda step: (step, 0)),
            vector,
            rows,
            vector,
            vector,
            vector,
            vector,
            rows,
        ],
        out_specs=[part, part, rows, rows, rows, vector, vector, vector],
        out_shape=[
            shape((tokens, expand)),
            shape((tokens, expand), narrow),
            shape((tokens, width), narrow),
            shape((tokens, width)),
            shape((tokens, width), narrow),
            shape((1, width)),
            shape((1, width)),
            shape((1, width)),
        ],
        scratch_shapes=[pltpu.VMEM((tokens, width), wide)],
        compiler_params=ROOM,
        cost_estimate=LITTLE,
        name="feed",
    )(low, w_in, b_in, w_back, b_back, normed, attn_gain, attn_bias, gain, bias, cotangent)


def gelu_slope(pre_act):
    return (
        0.5 * (1.0 + lax.erf(pre_act * SQRT_HALF))
        + pre_act * jnp.exp(-0.5 * pre_act * pre_act) * INV_ROOT_TAU
    )


def feed_back_kernel(
    d_returned, w_back, pre_act, w_in, d_r2, normed, inverse, gain,
    d_pre, g_in_bias, d_r1, d_attended, g_gain, g_bias, g_out_bias, total,
):
    step = pl.program_id(0)
    rounded = (mul_rows(d_returned[...], w_back[...]) * gelu_slope(pre_act[...])).astype(narrow)
    d_pre[...] = rounded
    g_in_bias[...] = down(rounded.astype(wide))
    share = mul_rows(rounded, w_in[...])

    @pl.when(step == 0)
    def _():
        total[...] = share

    @pl.when(step > 0)
    def _():
        total[...] += share

    @pl.when(step == pl.num_programs(0) - 1)
    def _():
        incoming = d_r2[...] + total[...]
        d_r1[...] = norm_back(incoming, normed[...], inverse[...], gain[...])
        g_gain[...] = down(incoming * normed[...])
        g_bias[...] = down(incoming)
        d_attended[...] = d_r1[...].astype(narrow)
        g_out_bias[...] = down(d_attended[...].astype(wide))


def feed_back(d_returned, w_back, pre_act, w_in, d_r2, normed, inverse, gain):
    tokens, width = d_returned.shape
    expand = pre_act.shape[1]
    block = width // 2
    vector = whole(1, width)
    rows = whole(tokens, width)
    part = pl.BlockSpec((tokens, block), lambda step: (0, step))
    return pl.pallas_call(
        feed_back_kernel,
        grid=(expand // block,),
        in_specs=[
            rows,
            pl.BlockSpec((block, width), lambda step: (step, 0)),
            part,
            pl.BlockSpec((width, block), lambda step: (0, step)),
            rows,
            rows,
            whole(tokens, 1),
            vector,
        ],
        out_specs=[
            part,
            pl.BlockSpec((1, block), lambda step: (0, step)),
            rows,
            rows,
            vector,
            vector,
            vector,
        ],
        out_shape=[
            shape((tokens, expand), narrow),
            shape((1, expand)),
            shape((tokens, width)),
            shape((tokens, width), narrow),
            shape((1, width)),
            shape((1, width)),
            shape((1, width)),
        ],
        scratch_shapes=[pltpu.VMEM((tokens, width), wide)],
        compiler_params=ROOM,
        cost_estimate=LITTLE,
        name="feed_back",
    )(d_returned, w_back, pre_act, w_in, d_r2, normed, inverse, gain)


def attend_back_kernel(
    queries, keys, values, d_attended, weight, d_packed, g_query_bias, g_value_bias
):
    d_context = mul_rows(d_attended[...], weight[...]).astype(narrow)
    d_queries, d_keys, d_values = 0.0, 0.0, 0.0
    for head in range(2):
        probs = head_probs(queries[...], keys[...], head)
        own_context = one_head(d_context, head)
        d_values += mul_down(probs.astype(narrow), own_context)
        d_probs = mul_rows(own_context, values[...])
        along = jnp.sum(probs * d_probs, -1, keepdims=True)
        d_scores = (probs * (d_probs - along)).astype(narrow)
        d_queries += mul(d_scores, one_head(keys[...], head))
        d_keys += mul_down(d_scores, one_head(queries[...], head))
    d_queries = (d_queries * HEAD ** (-0.5)).astype(narrow)
    d_values = d_values.astype(narrow)
    d_packed[0] = d_queries
    d_packed[1] = (d_keys * HEAD ** (-0.5)).astype(narrow)
    d_packed[2] = d_values
    g_query_bias[...] = down(d_queries.astype(wide))
    g_value_bias[...] = down(d_values.astype(wide))


def attend_back(packed, d_attended, weight):
    tokens, width = d_attended.shape
    pairs = width // PAIR
    return pl.pallas_call(
        attend_back_kernel,
        grid=(pairs,),
        in_specs=[
            pl.BlockSpec((tokens, PAIR), lambda pair: (0, pair)),
            pl.BlockSpec((tokens, PAIR), lambda pair: (0, pairs + pair)),
            pl.BlockSpec((tokens, PAIR), lambda pair: (0, 2 * pairs + pair)),
            whole(tokens, width),
            pl.BlockSpec((PAIR, width), lambda pair: (pair, 0)),
        ],
        out_specs=[
            pl.BlockSpec((3, tokens, PAIR), lambda pair: (0, 0, pair)),
            pl.BlockSpec((1, PAIR), lambda pair: (0, pair)),
            pl.BlockSpec((1, PAIR), lambda pair: (0, pair)),
        ],
        out_shape=[shape((3, tokens, width), narrow), shape((1, width)), shape((1, width))],
        compiler_params=ROOM,
        cost_estimate=LITTLE,
        name="attend_back",
    )(packed, packed, packed, d_attended, weight)


def embed_back_kernel(
    d_packed, weight, d_r1, normed, inverse, gain, d_embed, g_gain, g_bias, squares, blocks, total
):
    step = pl.program_id(0)
    share = mul_rows(d_packed[0], weight[...])

    @pl.when(step == 0)
    def _():
        total[...] = d_r1[...] + share

    @pl.when(step > 0)
    def _():
        total[...] += share

    @pl.when(step == pl.num_programs(0) - 1)
    def _():
        incoming = total[...]
        d_embed[...] = norm_back(incoming, normed[...], inverse[...], gain[...])
        g_gain[...] = down(incoming * normed[...])
        g_bias[...] = down(incoming)
        squares[...] = down(d_embed[...] * d_embed[...])
        columns = blocks.shape[2]
        for one in range(blocks.shape[0]):
            blocks[one] = d_embed[:, one * columns : (one + 1) * columns]


def embed_back(group, d_packed, weight, d_r1, normed, inverse, gain):
    tokens, width = d_r1.shape
    block = width // 2
    vector = whole(1, width)
    rows = whole(tokens, width)
    columns = width // group
    return pl.pallas_call(
        embed_back_kernel,
        grid=(3 * width // block,),
        in_specs=[
            pl.BlockSpec((1, tokens, block), lambda step: (step // 2, 0, step % 2)),
            pl.BlockSpec((width, block), lambda step: (0, step)),
            rows,
            rows,
            whole(tokens, 1),
            vector,
        ],
        out_specs=[rows, vector, vector, vector, whole(group, tokens, columns)],
        scratch_shapes=[pltpu.VMEM((tokens, width), wide)],
        out_shape=[
            shape((tokens, width)),
            shape((1, width)),
            shape((1, width)),
            shape((1, width)),
            shape((group, tokens, columns)),
        ],
        compiler_params=ROOM,
        cost_estimate=LITTLE,
        name="embed_back",
    )(d_packed, weight, d_r1, normed, inverse, gain)


def outer_kernel(left, right, out):
    out[...] = mul_down(left[...], right[...].reshape(right.shape[-2:]))


def outer(left, right):
    tokens, rows = left.shape
    width = right.shape[1]
    block = min(rows, 512)
    return pl.pallas_call(
        outer_kernel,
        grid=(rows // block,),
        in_specs=[pl.BlockSpec((tokens, block), lambda row: (0, row)), whole(tokens, width)],
        out_specs=pl.BlockSpec((block, width), lambda row: (row, 0)),
        out_shape=shape((rows, width)),
        compiler_params=ROOM,
        cost_estimate=LITTLE,
        name="outer",
    )(left, right)


def flat(ref):
    return ref[...].reshape(ref.shape[-2:])


def first_kernel(plan, table, *refs):
    count = len(plan)
    lefts, rights, out = refs[:count], refs[count : 2 * count], refs[-1]
    for one in range(count):
        out[one] = mul(lefts[one][...], flat(rights[one]))


def next_kernel(plan, table, *refs):
    count = len(plan)
    keeps, sends, rights = refs[:count], refs[count : 2 * count], refs[2 * count : 3 * count]
    arrived_keep, arrived_send, kept, sent_one, sent_two = refs[3 * count :]
    for one in range(count):
        right = flat(rights[one])
        kept[one] = mul(keeps[one][...], right) + arrived_keep[one]
        sent = sent_one if one < count // 2 else sent_two
        sent[one % (count // 2)] = mul(sends[one][...], right) + arrived_send[one]


class Halving:
    def __init__(self, me, masks_one, masks_two, streams, width):
        self.masks = (masks_one, masks_two)
        self.streams = streams
        self.devices = lax.axis_size("pages")
        self.width = width
        self.rows = streams[0][0].shape[0] // self.devices
        self.table = jnp.concatenate(
            [
                jnp.bitwise_xor(me, jnp.array(flips_of(masks), jnp.int32))
                for masks in self.masks
            ]
        )

    def left(self, one, start):
        place = (one >= len(self.streams) // 2) * self.devices + start
        return pl.BlockSpec(
            (self.rows, self.streams[one][0].shape[1]),
            lambda row, table: (table[place + row], 0),
        )

    def right(self, one):
        _, right, part, column = self.streams[one]
        if right.ndim == 3:
            return pl.BlockSpec((1, right.shape[1], self.width), lambda *_: (part, 0, column))
        return pl.BlockSpec((right.shape[0], self.width), lambda *_: (0, column))

    def block(self, count, start):
        return pl.BlockSpec((count, self.rows, self.width), lambda row, *_: (0, start + row, 0))

    def first(self, table):
        half = self.devices // 2
        count = len(self.streams)
        return pl.pallas_call(
            functools.partial(first_kernel, self.streams),
            grid_spec=pltpu.PrefetchScalarGridSpec(
                num_scalar_prefetch=1,
                grid=(half,),
                in_specs=[self.left(one, half) for one in range(count)]
                + [self.right(one) for one in range(count)],
                out_specs=self.block(count, 0),
            ),
            out_shape=shape((count, half * self.rows, self.width)),
            compiler_params=ROOM,
            cost_estimate=LITTLE,
            name="halving_first",
        )(table, *[one[0] for one in self.streams], *[one[1] for one in self.streams])

    def next(self, table, arrived):
        quarter = self.devices // 4
        count = len(self.streams)
        lefts = [one[0] for one in self.streams]
        return pl.pallas_call(
            functools.partial(next_kernel, self.streams),
            grid_spec=pltpu.PrefetchScalarGridSpec(
                num_scalar_prefetch=1,
                grid=(quarter,),
                in_specs=[self.left(one, 0) for one in range(count)]
                + [self.left(one, quarter) for one in range(count)]
                + [self.right(one) for one in range(count)]
                + [self.block(count, 0), self.block(count, quarter)],
                out_specs=[
                    self.block(count, 0),
                    self.block(count // 2, 0),
                    self.block(count // 2, 0),
                ],
            ),
            out_shape=[
                shape((part, quarter * self.rows, self.width))
                for part in (count, count // 2, count // 2)
            ],
            compiler_params=ROOM,
            cost_estimate=LITTLE,
            name="halving_next",
        )(table, *lefts, *lefts, *[one[1] for one in self.streams], arrived, arrived)

    def start(self, token):
        self.from_core = swap(token.after(self.first(token(self.table))), 1)

    def second(self, token):
        self.kept, *sent = token.after(*self.next(self.table, token(self.from_core)))
        self.arrived = [swap(one, masks[1]) for one, masks in zip(sent, self.masks)]

    def third(self, token):
        for at in range(2, len(self.masks[0])):
            arrived = jnp.concatenate(token(*self.arrived), 0)
            middle = self.kept.shape[1] // 2
            half = len(self.streams) // 2
            sent = self.kept[:, middle:] + arrived[:, middle:]
            sent = token.after(sent[:half], sent[half:])
            self.kept = self.kept[:, :middle] + arrived[:, :middle]
            self.arrived = [swap(one, masks[at]) for one, masks in zip(sent, self.masks)]

    def shares(self, token):
        return self.kept + jnp.concatenate(token(*self.arrived), 0)


class Token:
    def __init__(self, mark):
        self.mark = mark

    def __call__(self, *values):
        *values, self.mark = lax.optimization_barrier((*values, self.mark))
        return values[0] if len(values) == 1 else values

    after = __call__


def flips_of(masks):
    return [
        sum(mask for mask, flip in zip(masks, flips) if flip)
        for flips in itertools.product((0, 1), repeat=len(masks))
    ]


def relative(array, offsets, me, size, axis):
    blocks = [
        lax.dynamic_slice_in_dim(array, jnp.bitwise_xor(me, offset) * size, size, axis)
        for offset in offsets
    ]
    return jnp.concatenate(blocks, axis)


def swap(array, mask):
    return lax.ppermute(
        array, "pages", [(one, one ^ mask) for one in range(lax.axis_size("pages"))]
    )


def fold(kept, arrived):
    half = kept.shape[0] // 2
    return kept[:half] + arrived[:half], kept[half:] + arrived[half:]


def halve(kept, masks):
    for mask in masks:
        half = kept.shape[0] // 2
        kept = kept[:half] + swap(kept[half:], mask)
    return kept


def in_order(*values):
    return lax.optimization_barrier(values)


def emb_total(share):
    if lax.axis_size("emb") != 4:
        return lax.psum(share, "emb")
    plane = lax.axis_index("emb")
    middle = jnp.logical_or(plane == 1, plane == 2)
    share = share + lax.ppermute(share, "emb", [(0, 1), (3, 2)])
    share = share + lax.ppermute(share, "emb", [(1, 2), (2, 1)])
    return jnp.where(middle, share, lax.ppermute(share, "emb", [(1, 0), (2, 3)]))


def on_device(
    text_embed,
    boxes,
    layout_tables,
    emb_gain,
    emb_bias,
    w_qkv,
    b_query,
    b_value,
    w_out,
    b_out,
    attn_gain,
    attn_bias,
    w_in,
    b_in,
    w_back,
    b_back,
    ffn_gain,
    ffn_bias,
    cotangent,
):
    token_rows = text_embed.shape[0]
    model_width = text_embed.shape[1]
    entries = layout_tables.shape[1]
    me = lax.axis_index("pages")
    plane = lax.axis_index("emb")
    devices = lax.axis_size("pages")
    planes = lax.axis_size("emb")
    outer_masks = [1 << bit for bit in range(1, devices.bit_length() - 1)]
    turn = len(outer_masks) // 2
    masks_one = [1] + outer_masks
    masks_two = [1] + outer_masks[turn:] + outer_masks[:turn]
    group = min(devices, 8)
    inner = me % group
    columns = model_width // group
    groups = [list(range(first, first + group)) for first in range(0, devices, group)]

    def row(vector):
        return vector.reshape(1, -1)

    def around(array, offset):
        return lax.ppermute(
            array, "emb", [((one + offset) % planes, one) for one in range(planes)]
        )

    def exchange(blocks):
        return lax.all_to_all(blocks, "pages", 0, 0, tiled=True, axis_index_groups=groups)

    own_columns = lax.dynamic_slice_in_dim(layout_tables[0], inner * columns, columns, 1)
    table_columns = [own_columns] + [around(own_columns, offset) for offset in range(1, planes)]
    group_boxes = lax.all_gather(boxes, "pages", axis=1, tiled=True, axis_index_groups=groups)
    looked_up = jnp.zeros((group * token_rows, columns), wide)
    for offset in [0, 1, planes - 1] + list(range(2, planes - 1)):
        uses = jnp.stack(table_indices(group_boxes, (plane + offset) % planes))
        looked_up = add_rows(uses.T, table_columns[offset], looked_up)
    parts = exchange(looked_up.reshape(group, token_rows, columns))

    bias_qkv = jnp.concatenate([b_query, jnp.zeros_like(b_query), b_value])
    packed, normed_emb, inverse_emb, emb_low = embed_and_project(
        parts, text_embed, row(emb_gain), row(emb_bias), w_qkv, row(bias_qkv)
    )
    context_low, normed_attn, inverse_attn, attn_low = attend(
        packed,
        w_out,
        row(b_out),
        normed_emb,
        row(emb_gain),
        row(emb_bias),
        row(attn_gain),
        row(attn_bias),
    )
    pre_act, expanded, output, d_r2, d_returned, g_ffn_gain, g_ffn_bias, g_back_bias = feed(
        attn_low,
        w_in,
        row(b_in),
        w_back,
        row(b_back),
        normed_attn,
        row(attn_gain),
        row(attn_bias),
        row(ffn_gain),
        row(ffn_bias),
        cotangent,
    )

    token = Token(output)
    flight = {}

    def gather_pages(product):
        return lax.psum_scatter(product, "pages", scatter_dimension=0, tiled=True)

    def inward(share):
        return lax.ppermute(share, "emb", [(0, 1), (3, 2)])

    def across(share):
        return lax.ppermute(share, "emb", [(1, 2), (2, 1)])

    def outward(share):
        return lax.ppermute(share, "emb", [(1, 0), (2, 3)])

    def settled(share, arrived):
        return jnp.where(jnp.logical_or(plane == 1, plane == 2), share, arrived)

    shares, halvings = {}, {}
    for step in ORDER:
        kind, name = step.split()
        if step == "first back":
            flight[name] = gather_pages(token.after(outer(expanded, token(d_returned))))
        elif step == "feed all":
            d_pre, g_in_bias, d_r1, d_attended, g_attn_gain, g_attn_bias, g_out_bias = feed_back(
                d_returned,
                w_back,
                pre_act,
                w_in,
                d_r2,
                normed_attn,
                inverse_attn,
                token(row(attn_gain)),
            )
            d_pre, d_attended = token.after(d_pre, d_attended)
            attn_rows = attn_low.T
            halvings["in"] = Halving(
                me,
                masks_one,
                masks_two,
                [(attn_rows, d_pre, 0, one) for one in range(4)],
                model_width,
            )
        elif step == "attend all":
            d_packed, g_query_bias, g_value_bias = attend_back(packed, token(d_attended), w_out)
            d_packed = token.after(d_packed)
            emb_rows = emb_low.T
            context_rows = context_low.T
            quarter = model_width // 4
            for name, width, column in (("q1", 3 * quarter, 0), ("q2", quarter, 3)):
                halvings[name] = Halving(
                    me,
                    masks_one,
                    masks_two,
                    [(emb_rows, d_packed, one, column) for one in range(3)]
                    + [(context_rows, d_attended, 0, column)],
                    width,
                )
        elif kind == "first":
            halvings[name].start(token)
        elif kind == "next":
            halvings[name].second(token)
        elif kind == "fold":
            halvings[name].third(token)
        elif kind == "finish":
            shares[name] = halvings[name].shares(token) if name in halvings else flight[name]
            shares[name] = token.after(shares[name])
            flight[name] = inward(shares[name])
        elif kind == "exchange":
            shares[name] = token.after(shares[name] + token(flight[name]))
            flight[name] = across(shares[name])
        elif kind == "return":
            shares[name] = token.after(shares[name] + token(flight[name]))
            flight[name] = outward(shares[name])
        elif kind == "end":
            shares[name] = token.after(settled(shares[name], token(flight[name])))
        elif kind == "embed":
            d_embed, g_emb_gain, g_emb_bias, squares, embed_blocks = embed_back(
                group,
                d_packed,
                w_qkv,
                d_r1,
                normed_emb,
                inverse_emb,
                token(row(emb_gain)),
            )
            squares, embed_blocks = token.after(squares, embed_blocks)
            flight["h"] = exchange(embed_blocks)
        elif kind == "spread":
            if name == "0":
                embed_columns = token(flight["h"]).reshape(group * token_rows, columns)
            uses = jnp.stack(table_indices(group_boxes, int(name)))
            flight["t" + name] = token.after(spread_rows(token(uses), embed_columns, entries))
            if int(name) == planes - 1:
                table_shares = jnp.concatenate([flight["t" + str(one)] for one in range(planes)], 0)
                flight["t"] = lax.all_to_all(table_shares, "emb", 0, 0, tiled=True)
        elif step == "tables 0":
            owned = token(flight["t"]).reshape(planes, entries, columns)
            table_total = token.after(functools.reduce(jnp.add, list(owned)))
            row_masks = [mask for mask in masks_one if mask >= group]
            if row_masks:
                table_total = halve(
                    relative(
                        table_total,
                        flips_of([mask // group for mask in row_masks]),
                        me // group,
                        entries * group // devices,
                        0,
                    ),
                    row_masks,
                )
            flight["u"] = exchange(table_total.reshape(group, entries // devices, columns))
        elif step == "tables 1":
            table_share = jnp.concatenate(list(token(flight["u"])), 1)
            table_share = token.after(table_share)
        elif step == "vector 0":
            vectors = [
                g_query_bias,
                g_value_bias,
                g_out_bias,
                g_attn_gain,
                g_attn_bias,
                g_in_bias,
                g_back_bias,
                g_ffn_gain,
                g_ffn_bias,
                g_emb_gain,
                g_emb_bias,
                jnp.full((devices,), jnp.sum(squares)),
            ]
            stacked = jnp.concatenate([vector.reshape(devices, -1) for vector in vectors], 1)
            stacked = token.after(token(stacked))
            flight["v1"] = lax.all_to_all(stacked, "pages", 0, 0, tiled=True)
        elif step == "vector 1":
            vector_share = token.after(jnp.sum(token(flight["v1"]), 0, keepdims=True))
            flight["v2"] = lax.ppermute(vector_share, "emb", [(0, 1), (3, 2)])
        elif step == "vector 2":
            vector_share = token.after(vector_share + token(flight["v2"]))
            flight["v3"] = lax.ppermute(vector_share, "emb", [(1, 2), (2, 1)])
        elif step == "vector 3":
            vector_share = token.after(vector_share + token(flight["v3"]))
            flight["v4"] = lax.ppermute(vector_share, "emb", [(1, 0), (2, 3)])
        elif step == "vector 4":
            middle = jnp.logical_or(plane == 1, plane == 2)
            vector_share = jnp.where(middle, vector_share, token(flight["v4"]))[0]
    g_back = shares["back"]
    g_in = jnp.concatenate(list(shares["in"]), 1)
    g_four = jnp.concatenate([shares["q1"], shares["q2"]], 2)
    g_qkv = jnp.concatenate(list(g_four[:3]), 1)
    g_out = g_four[3]

    totals = []
    first = 0
    for vector in vectors:
        length = vector.size // devices
        totals.append(vector_share[first : first + length])
        first += length
    entry_count = token_rows * model_width * devices * planes
    rms_grad = jnp.sqrt(totals[11][0] / entry_count)
    return (
        token.mark,
        d_embed,
        table_share[None],
        totals[9],
        totals[10],
        g_qkv,
        totals[0],
        totals[1],
        g_out,
        totals[2],
        totals[3],
        totals[4],
        g_in,
        totals[5],
        g_back,
        totals[6],
        totals[7],
        totals[8],
        rms_grad,
    )


def solution(mesh):
    return jax.shard_map(
        on_device,
        mesh=mesh,
        in_specs=(
            P(("pages", "emb"), None),
            P(None, ("pages", "emb")),
            P("emb", None, None),
            P(),
            P(),
            P(),
            P(),
            P(),
            P(),
            P(),
            P(),
            P(),
            P(),
            P(),
            P(),
            P(),
            P(),
            P(),
            P(("pages", "emb"), None),
        ),
        out_specs=(
            P(("pages", "emb"), None),
            P(("pages", "emb"), None),
            P("emb", "pages", None),
            P("pages"),
            P("pages"),
            P("pages", None),
            P("pages"),
            P("pages"),
            P("pages", None),
            P("pages"),
            P("pages"),
            P("pages"),
            P("pages", None),
            P("pages"),
            P("pages", None),
            P("pages"),
            P("pages"),
            P("pages"),
            P(),
        ),
        check_vma=False,
    )
```

```python
import functools
import itertools

import jax
import jax.numpy as jnp
from jax import lax
from jax.experimental import pallas as pl
from jax.experimental.pallas import tpu as pltpu
from jax.sharding import PartitionSpec as P

HEADS = 16
HEAD = 64
PAGE = 512
PAIR = 2 * HEAD

EPSILON = 1e-05
SQRT_HALF = 0.7071067811865476
INV_ROOT_TAU = 0.3989422804014327

wide = jnp.float32
narrow = jnp.bfloat16
ATTEND_PARTS = 4
SPREAD = (2, 1, 3, 0)
SPLIT = {"back": ("backa", "backb"), "in": ("ina", "inb"), "q": ("qa", "qb")}
ORDER = (
    "first back",
    "feed all",
    "first in",
    "attend all",
    "embed all",
    "first q",
    "spread 0",
    "next in",
    "spread 1",
    "spread 2",
    "spread 3",
    "fold in",
    "tables 0",
    "next q",
    "finish back",
    "send backa",
    "finish in",
    "send backb",
    "tables 1",
    "exchange backa",
    "send ina",
    "vector 0",
    "exchange backb",
    "return backa",
    "fold q",
    "end backa",
    "send inb",
    "return backb",
    "exchange ina",
    "vector 1",
    "finish q",
    "send qa",
    "send qb",
    "end backb",
    "return ina",
    "exchange inb",
    "vector 2",
    "end ina",
    "return inb",
    "exchange qa",
    "vector 3",
    "end inb",
    "return qa",
    "exchange qb",
    "vector 4",
    "end qa",
    "return qb",
    "end qb",
)
PARTS = 1
LITTLE = pl.CostEstimate(flops=1024, bytes_accessed=1024, transcendentals=0)
ROOM = pltpu.CompilerParams(vmem_limit_bytes=32 * 2**20)
MOST = pltpu.CompilerParams(vmem_limit_bytes=32 * 2**20)


def shape(dims, dtype=wide):
    return jax.ShapeDtypeStruct(dims, dtype)


def whole(*dims):
    return pl.BlockSpec(dims, lambda *_: (0,) * len(dims))


def normalize(values):
    averaged = jnp.mean(values, -1, keepdims=True)
    centered = values - averaged
    inverse = lax.rsqrt(jnp.mean(centered * centered, -1, keepdims=True) + EPSILON)
    return centered * inverse, inverse


def norm_back(incoming, normed, inverse, gain):
    scaled = incoming * gain
    offset_mean = jnp.mean(scaled, -1, keepdims=True)
    along_mean = jnp.mean(scaled * normed, -1, keepdims=True)
    return inverse * (scaled - offset_mean - normed * along_mean)


def down(values):
    return jnp.sum(values, 0, keepdims=True)


def mul(left, right):
    return jnp.dot(left, right, preferred_element_type=wide)


def mul_rows(left, right):
    return lax.dot_general(left, right, (((1,), (1,)), ((), ())), preferred_element_type=wide)


def mul_down(left, right):
    return lax.dot_general(left, right, (((0,), (0,)), ((), ())), preferred_element_type=wide)


def table_indices(box_rows, table):
    left_x, top_y, right_x, bottom_y = box_rows[0], box_rows[1], box_rows[2], box_rows[3]
    first = jnp.where(
        table == 0,
        left_x,
        jnp.where(table == 1, top_y, jnp.where(table == 2, right_x - left_x, bottom_y - top_y)),
    )
    second = jnp.where(table == 0, right_x, jnp.where(table == 1, bottom_y, -1))
    return first, second


def two_halves(values):
    high = values.astype(narrow)
    return high, (values - high.astype(wide)).astype(narrow)


def hits(entry, indices):
    return jnp.where(entry == indices, 1.0, 0.0)


def lookup_kernel(twice_ref, idx_ref, *refs):
    tables, total_ref, out_ref, halves = refs[:-3], refs[-3], refs[-2], refs[-1]
    entries, width = tables[0].shape

    @pl.when(pl.program_id(0) == 0)
    def _():
        for one, table in enumerate(tables):
            halves[one, :, :width], halves[one, :, width:] = two_halves(table[...])

    entry = lax.broadcasted_iota(jnp.int32, (idx_ref.shape[0], entries), 1)

    def add(one, counts):
        rows = mul(counts.astype(narrow), halves[one])
        out_ref[...] += rows[:, :width] + rows[:, width:]

    out_ref[...] = total_ref[...]
    for one in range(len(tables)):
        first = idx_ref[:, 2 * one : 2 * one + 1]
        second = idx_ref[:, 2 * one + 1 : 2 * one + 2]

        @pl.when(twice_ref[one] == 1)
        def _():
            add(one, hits(entry, first) + hits(entry, second))

        @pl.when(twice_ref[one] == 0)
        def _():
            add(one, hits(entry, first))


def add_rows(twice, indices, tables, total, part, parts):
    tokens = total.shape[0]
    entries, width = tables[0].shape
    block = PAGE
    steps = tokens // block // parts
    return pl.pallas_call(
        lookup_kernel,
        grid_spec=pltpu.PrefetchScalarGridSpec(
            num_scalar_prefetch=1,
            grid=(steps,),
            in_specs=[
                pl.BlockSpec((block, indices.shape[1]), lambda step, *_: (steps * part + step, 0))
            ]
            + [whole(entries, width)] * len(tables)
            + [pl.BlockSpec((block, width), lambda step, *_: (steps * part + step, 0))],
            out_specs=pl.BlockSpec((block, width), lambda step, *_: (step, 0)),
            scratch_shapes=[pltpu.VMEM((len(tables), entries, 2 * width), narrow)],
        ),
        out_shape=shape((tokens // parts, width)),
        compiler_params=ROOM,
        cost_estimate=LITTLE,
        name="look_up",
    )(twice, indices, *tables, total)


def spread_kernel(idx_ref, rows_ref, out_ref):
    width = rows_ref.shape[1]
    entry = lax.broadcasted_iota(jnp.int32, (out_ref.shape[0], rows_ref.shape[0]), 0)
    counts = hits(entry, idx_ref[0:1, :]) + hits(entry, idx_ref[1:2, :])
    both = mul(counts.astype(narrow), jnp.concatenate(two_halves(rows_ref[...]), 1))
    share = both[:, :width] + both[:, width:]

    @pl.when(pl.program_id(0) == 0)
    def _():
        out_ref[...] = share

    @pl.when(pl.program_id(0) > 0)
    def _():
        out_ref[...] += share


def spread_rows(indices, rows, entries):
    tokens, width = rows.shape
    block = 2 * PAGE
    return pl.pallas_call(
        spread_kernel,
        grid=(tokens // block,),
        in_specs=[
            pl.BlockSpec((2, block), lambda step: (0, step)),
            pl.BlockSpec((block, width), lambda step: (step, 0)),
        ],
        out_specs=whole(entries, width),
        out_shape=shape((entries, width)),
        compiler_params=ROOM,
        cost_estimate=LITTLE,
        name="spread",
    )(indices, rows)


def project_kernel(*refs):
    parts, (text, gain, bias, weight, weight_bias) = refs[:-9], refs[-9:-4]
    packed, normed, inverse, low = refs[-4:]
    group, rows, width = parts[0].shape

    @pl.when(pl.program_id(0) == 0)
    def _():
        for at, part in enumerate(parts):
            for one in range(group):
                normed[at * rows : (at + 1) * rows, one * width : (one + 1) * width] = part[one]
        normed[...], inverse[...] = normalize(normed[...] + text[...].astype(wide))
        low[...] = (normed[...] * gain[...] + bias[...]).astype(narrow)

    packed[...] = (mul(low[...], weight[...]) + weight_bias[...]).astype(narrow)


def embed_and_project(parts, text, gain, bias, weight, weight_bias):
    tokens, width = text.shape
    block = width // 2
    steps = weight.shape[1] // block
    return pl.pallas_call(
        project_kernel,
        grid=(steps,),
        in_specs=[whole(*part.shape) for part in parts]
        + [
            whole(tokens, width),
            whole(1, width),
            whole(1, width),
            pl.BlockSpec((width, block), lambda step: (0, step)),
            pl.BlockSpec((1, block), lambda step: (0, step)),
        ],
        out_specs=[
            pl.BlockSpec((tokens, block), lambda step: (0, step)),
            whole(tokens, width),
            whole(tokens, 1),
            whole(tokens, width),
        ],
        out_shape=[
            shape((tokens, weight.shape[1]), narrow),
            shape((tokens, width)),
            shape((tokens, 1)),
            shape((tokens, width), narrow),
        ],
        compiler_params=ROOM,
        cost_estimate=LITTLE,
        name="embed_and_project",
    )(*parts, text, gain, bias, weight, weight_bias)


def one_head(rows, head):
    lane = lax.broadcasted_iota(jnp.int32, rows.shape, 1)
    return jnp.where((lane < HEAD) == (head == 0), rows, jnp.zeros_like(rows))


def head_probs(queries, keys, head):
    scores = mul_rows(one_head(queries, head), keys) * HEAD ** (-0.5)
    exponent = jnp.exp(scores - jnp.max(scores, -1, keepdims=True))
    return exponent * (1.0 / jnp.sum(exponent, -1, keepdims=True))


def attend_kernel(
    queries, keys, values, weight, weight_bias, normed_emb, emb_gain, emb_bias, gain, bias,
    context, normed, inverse, low,
):
    pair = pl.program_id(0)
    lane = lax.broadcasted_iota(jnp.int32, values.shape, 1)
    parts = []
    for head in range(2):
        scores = mul_rows(one_head(queries[...], head), keys[...]) * HEAD ** (-0.5)
        exponent = jnp.exp(scores - jnp.max(scores, -1, keepdims=True))
        probs = exponent * (1.0 / jnp.sum(exponent, -1, keepdims=True))
        parts.append(mul(probs.astype(narrow), values[...]))
    place = pl.multiple_of(pair * PAIR, PAIR)
    context[:, pl.ds(place, PAIR)] = jnp.where(lane < HEAD, parts[0], parts[1]).astype(narrow)

    @pl.when(pair == pl.num_programs(0) - 1)
    def _():
        hidden = normed_emb[...] * emb_gain[...] + emb_bias[...]
        attended = mul(context[...], weight[...]) + weight_bias[...]
        normed[...], inverse[...] = normalize(hidden + attended)
        low[...] = (normed[...] * gain[...] + bias[...]).astype(narrow)


def attend(packed, weight, weight_bias, normed_emb, emb_gain, emb_bias, gain, bias):
    tokens, width = normed_emb.shape
    pairs = width // PAIR
    vector = whole(1, width)
    return pl.pallas_call(
        attend_kernel,
        grid=(pairs,),
        in_specs=[
            pl.BlockSpec((tokens, PAIR), lambda pair: (0, pair)),
            pl.BlockSpec((tokens, PAIR), lambda pair: (0, pairs + pair)),
            pl.BlockSpec((tokens, PAIR), lambda pair: (0, 2 * pairs + pair)),
            whole(*weight.shape),
            vector,
            whole(tokens, width),
            vector,
            vector,
            vector,
            vector,
        ],
        out_specs=[
            whole(tokens, width),
            whole(tokens, width),
            whole(tokens, 1),
            whole(tokens, width),
        ],
        out_shape=[
            shape((tokens, width), narrow),
            shape((tokens, width)),
            shape((tokens, 1)),
            shape((tokens, width), narrow),
        ],
        compiler_params=ROOM,
        cost_estimate=LITTLE,
        name="attend",
    )(packed, packed, packed, weight, weight_bias, normed_emb, emb_gain, emb_bias, gain, bias)


def feed_kernel(
    low, w_in, b_in, w_back, b_back, normed_attn, attn_gain, attn_bias, gain, bias, cotangent,
    pre_act, expanded, output, d_r2, d_returned, g_gain, g_bias, g_back_bias, total,
):
    step = pl.program_id(0)
    pre = mul(low[...], w_in[...]) + b_in[...]
    pre_act[...] = pre
    expanded[...] = (pre * (0.5 * (1.0 + lax.erf(pre * SQRT_HALF)))).astype(narrow)
    share = mul(expanded[...], w_back[...])

    @pl.when(step == 0)
    def _():
        total[...] = share

    @pl.when(step > 0)
    def _():
        total[...] += share

    @pl.when(step == pl.num_programs(0) - 1)
    def _():
        hidden = normed_attn[...] * attn_gain[...] + attn_bias[...]
        normed, inverse = normalize(hidden + (total[...] + b_back[...]))
        output[...] = (normed * gain[...] + bias[...]).astype(narrow)
        incoming = cotangent[...].astype(wide)
        d_r2[...] = norm_back(incoming, normed, inverse, gain[...])
        g_gain[...] = down(incoming * normed)
        g_bias[...] = down(incoming)
        rounded = d_r2[...].astype(narrow)
        d_returned[...] = rounded
        g_back_bias[...] = down(rounded.astype(wide))


def feed(low, w_in, b_in, w_back, b_back, normed, attn_gain, attn_bias, gain, bias, cotangent):
    tokens, width = low.shape
    expand = w_in.shape[1]
    block = width // 2
    vector = whole(1, width)
    rows = whole(tokens, width)
    part = pl.BlockSpec((tokens, block), lambda step: (0, step))
    return pl.pallas_call(
        feed_kernel,
        grid=(expand // block,),
        in_specs=[
            rows,
            pl.BlockSpec((width, block), lambda step: (0, step)),
            pl.BlockSpec((1, block), lambda step: (0, step)),
            pl.BlockSpec((block, width), lambda step: (step, 0)),
            vector,
            rows,
            vector,
            vector,
            vector,
            vector,
            rows,
        ],
        out_specs=[part, part, rows, rows, rows, vector, vector, vector],
        out_shape=[
            shape((tokens, expand)),
            shape((tokens, expand), narrow),
            shape((tokens, width), narrow),
            shape((tokens, width)),
            shape((tokens, width), narrow),
            shape((1, width)),
            shape((1, width)),
            shape((1, width)),
        ],
        scratch_shapes=[pltpu.VMEM((tokens, width), wide)],
        compiler_params=ROOM,
        cost_estimate=LITTLE,
        name="feed",
    )(low, w_in, b_in, w_back, b_back, normed, attn_gain, attn_bias, gain, bias, cotangent)


def gelu_slope(pre_act):
    return (
        0.5 * (1.0 + lax.erf(pre_act * SQRT_HALF))
        + pre_act * jnp.exp(-0.5 * pre_act * pre_act) * INV_ROOT_TAU
    )


def feed_back_kernel(
    d_returned, w_back, pre_act, w_in, d_r2, normed, inverse, gain,
    d_pre, g_in_bias, d_r1, d_attended, g_gain, g_bias, g_out_bias, total,
):
    step = pl.program_id(0)
    rounded = (mul_rows(d_returned[...], w_back[...]) * gelu_slope(pre_act[...])).astype(narrow)
    d_pre[...] = rounded
    g_in_bias[...] = down(rounded.astype(wide))
    share = mul_rows(rounded, w_in[...])

    @pl.when(step == 0)
    def _():
        total[...] = share

    @pl.when(step > 0)
    def _():
        total[...] += share

    @pl.when(step == pl.num_programs(0) - 1)
    def _():
        incoming = d_r2[...] + total[...]
        d_r1[...] = norm_back(incoming, normed[...], inverse[...], gain[...])
        g_gain[...] = down(incoming * normed[...])
        g_bias[...] = down(incoming)
        d_attended[...] = d_r1[...].astype(narrow)
        g_out_bias[...] = down(d_attended[...].astype(wide))


def feed_back(d_returned, w_back, pre_act, w_in, d_r2, normed, inverse, gain):
    tokens, width = d_returned.shape
    expand = pre_act.shape[1]
    block = width // 2
    vector = whole(1, width)
    rows = whole(tokens, width)
    part = pl.BlockSpec((tokens, block), lambda step: (0, step))
    return pl.pallas_call(
        feed_back_kernel,
        grid=(expand // block,),
        in_specs=[
            rows,
            pl.BlockSpec((block, width), lambda step: (step, 0)),
            part,
            pl.BlockSpec((width, block), lambda step: (0, step)),
            rows,
            rows,
            whole(tokens, 1),
            vector,
        ],
        out_specs=[
            part,
            pl.BlockSpec((1, block), lambda step: (0, step)),
            rows,
            rows,
            vector,
            vector,
            vector,
        ],
        out_shape=[
            shape((tokens, expand), narrow),
            shape((1, expand)),
            shape((tokens, width)),
            shape((tokens, width), narrow),
            shape((1, width)),
            shape((1, width)),
            shape((1, width)),
        ],
        scratch_shapes=[pltpu.VMEM((tokens, width), wide)],
        compiler_params=MOST,
        cost_estimate=LITTLE,
        name="feed_back",
    )(d_returned, w_back, pre_act, w_in, d_r2, normed, inverse, gain)


def attend_back_kernel(
    queries, keys, values, d_attended, weight, d_packed, g_query_bias, g_value_bias
):
    d_context = mul_rows(d_attended[...], weight[...]).astype(narrow)
    d_queries, d_keys, d_values = 0.0, 0.0, 0.0
    for head in range(2):
        probs = head_probs(queries[...], keys[...], head)
        own_context = one_head(d_context, head)
        d_values += mul_down(probs.astype(narrow), own_context)
        d_probs = mul_rows(own_context, values[...])
        along = jnp.sum(probs * d_probs, -1, keepdims=True)
        d_scores = (probs * (d_probs - along)).astype(narrow)
        d_queries += mul(d_scores, one_head(keys[...], head))
        d_keys += mul_down(d_scores, one_head(queries[...], head))
    d_queries = (d_queries * HEAD ** (-0.5)).astype(narrow)
    d_values = d_values.astype(narrow)
    d_packed[0] = d_queries
    d_packed[1] = (d_keys * HEAD ** (-0.5)).astype(narrow)
    d_packed[2] = d_values
    g_query_bias[...] = down(d_queries.astype(wide))
    g_value_bias[...] = down(d_values.astype(wide))


def attend_back(packed, d_attended, weight):
    tokens, width = d_attended.shape
    pairs = width // PAIR
    return pl.pallas_call(
        attend_back_kernel,
        grid=(pairs,),
        in_specs=[
            pl.BlockSpec((tokens, PAIR), lambda pair: (0, pair)),
            pl.BlockSpec((tokens, PAIR), lambda pair: (0, pairs + pair)),
            pl.BlockSpec((tokens, PAIR), lambda pair: (0, 2 * pairs + pair)),
            whole(tokens, width),
            pl.BlockSpec((PAIR, width), lambda pair: (pair, 0)),
        ],
        out_specs=[
            pl.BlockSpec((3, tokens, PAIR), lambda pair: (0, 0, pair)),
            pl.BlockSpec((1, PAIR), lambda pair: (0, pair)),
            pl.BlockSpec((1, PAIR), lambda pair: (0, pair)),
        ],
        out_shape=[shape((3, tokens, width), narrow), shape((1, width)), shape((1, width))],
        compiler_params=MOST,
        cost_estimate=LITTLE,
        name="attend_back",
    )(packed, packed, packed, d_attended, weight)


def embed_back_kernel(
    d_packed, weight, d_r1, normed, inverse, gain, d_embed, g_gain, g_bias, squares, blocks, total
):
    step = pl.program_id(0)
    share = mul_rows(d_packed[0], weight[...])

    @pl.when(step == 0)
    def _():
        total[...] = d_r1[...] + share

    @pl.when(step > 0)
    def _():
        total[...] += share

    @pl.when(step == pl.num_programs(0) - 1)
    def _():
        incoming = total[...]
        d_embed[...] = norm_back(incoming, normed[...], inverse[...], gain[...])
        g_gain[...] = down(incoming * normed[...])
        g_bias[...] = down(incoming)
        squares[...] = down(d_embed[...] * d_embed[...])
        columns = blocks.shape[2]
        for one in range(blocks.shape[0]):
            blocks[one] = d_embed[:, one * columns : (one + 1) * columns]


def embed_back(group, d_packed, weight, d_r1, normed, inverse, gain):
    tokens, width = d_r1.shape
    block = width // 2
    vector = whole(1, width)
    rows = whole(tokens, width)
    columns = width // group
    return pl.pallas_call(
        embed_back_kernel,
        grid=(3 * width // block,),
        in_specs=[
            pl.BlockSpec((1, tokens, block), lambda step: (step // 2, 0, step % 2)),
            pl.BlockSpec((width, block), lambda step: (0, step)),
            rows,
            rows,
            whole(tokens, 1),
            vector,
        ],
        out_specs=[rows, vector, vector, vector, whole(group, tokens, columns)],
        scratch_shapes=[pltpu.VMEM((tokens, width), wide)],
        out_shape=[
            shape((tokens, width)),
            shape((1, width)),
            shape((1, width)),
            shape((1, width)),
            shape((group, tokens, columns)),
        ],
        compiler_params=MOST,
        cost_estimate=LITTLE,
        name="embed_back",
    )(d_packed, weight, d_r1, normed, inverse, gain)


def outer_kernel(left, right, out):
    out[...] = mul_down(left[...], right[...].reshape(right.shape[-2:]))


def outer(left, right):
    tokens, rows = left.shape
    width = right.shape[1]
    block = min(rows, 512)
    return pl.pallas_call(
        outer_kernel,
        grid=(rows // block,),
        in_specs=[pl.BlockSpec((tokens, block), lambda row: (0, row)), whole(tokens, width)],
        out_specs=pl.BlockSpec((block, width), lambda row: (row, 0)),
        out_shape=shape((rows, width)),
        compiler_params=MOST,
        cost_estimate=LITTLE,
        name="outer",
    )(left, right)


def flat(ref):
    return ref[...].reshape(ref.shape[-2:])


def first_kernel(plan, table, *refs):
    count = len(plan)
    lefts, rights, out = refs[:count], refs[count : 2 * count], refs[-1]
    for one in range(count):
        out[one] = mul(lefts[one][...], flat(rights[one]))


def next_kernel(plan, table, *refs):
    count = len(plan)
    keeps, sends, rights = refs[:count], refs[count : 2 * count], refs[2 * count : 3 * count]
    arrived_keep, arrived_send, kept, sent_one, sent_two = refs[3 * count :]
    for one in range(count):
        right = flat(rights[one])
        kept[one] = mul(keeps[one][...], right) + arrived_keep[one]
        sent = sent_one if one < count // 2 else sent_two
        sent[one % (count // 2)] = mul(sends[one][...], right) + arrived_send[one]


class Halving:
    def __init__(self, me, masks_one, masks_two, streams, width):
        self.masks = (masks_one, masks_two)
        self.streams = streams
        self.devices = lax.axis_size("pages")
        self.width = width
        self.rows = streams[0][0].shape[0] // self.devices
        self.table = jnp.concatenate(
            [
                jnp.bitwise_xor(me, jnp.array(flips_of(masks), jnp.int32))
                for masks in self.masks
            ]
        )

    def left(self, one, start):
        place = (one >= len(self.streams) // 2) * self.devices + start
        return pl.BlockSpec(
            (self.rows, self.streams[one][0].shape[1]),
            lambda row, table: (table[place + row], 0),
        )

    def right(self, one):
        _, right, part, column = self.streams[one]
        if right.ndim == 3:
            return pl.BlockSpec((1, right.shape[1], self.width), lambda *_: (part, 0, column))
        return pl.BlockSpec((right.shape[0], self.width), lambda *_: (0, column))

    def block(self, count, start):
        return pl.BlockSpec((count, self.rows, self.width), lambda row, *_: (0, start + row, 0))

    def first(self, table):
        half = self.devices // 2
        count = len(self.streams)
        return pl.pallas_call(
            functools.partial(first_kernel, self.streams),
            grid_spec=pltpu.PrefetchScalarGridSpec(
                num_scalar_prefetch=1,
                grid=(half,),
                in_specs=[self.left(one, half) for one in range(count)]
                + [self.right(one) for one in range(count)],
                out_specs=self.block(count, 0),
            ),
            out_shape=shape((count, half * self.rows, self.width)),
            compiler_params=MOST,
            cost_estimate=LITTLE,
            name="halving_first",
        )(table, *[one[0] for one in self.streams], *[one[1] for one in self.streams])

    def next(self, table, arrived):
        quarter = self.devices // 4
        count = len(self.streams)
        lefts = [one[0] for one in self.streams]
        return pl.pallas_call(
            functools.partial(next_kernel, self.streams),
            grid_spec=pltpu.PrefetchScalarGridSpec(
                num_scalar_prefetch=1,
                grid=(quarter,),
                in_specs=[self.left(one, 0) for one in range(count)]
                + [self.left(one, quarter) for one in range(count)]
                + [self.right(one) for one in range(count)]
                + [self.block(count, 0), self.block(count, quarter)],
                out_specs=[
                    self.block(count, 0),
                    self.block(count // 2, 0),
                    self.block(count // 2, 0),
                ],
            ),
            out_shape=[
                shape((part, quarter * self.rows, self.width))
                for part in (count, count // 2, count // 2)
            ],
            compiler_params=MOST,
            cost_estimate=LITTLE,
            name="halving_next",
        )(table, *lefts, *lefts, *[one[1] for one in self.streams], arrived, arrived)

    def start(self, token):
        self.from_core = swap(token.after(self.first(token(self.table))), 1)

    def second(self, token):
        self.kept, *sent = token.after(*self.next(self.table, token(self.from_core)))
        self.arrived = [swap(one, masks[1]) for one, masks in zip(sent, self.masks)]

    def third(self, token):
        for at in range(2, len(self.masks[0])):
            arrived = jnp.concatenate(token(*self.arrived), 0)
            middle = self.kept.shape[1] // 2
            half = len(self.streams) // 2
            sent = self.kept[:, middle:] + arrived[:, middle:]
            sent = token.after(sent[:half], sent[half:])
            self.kept = self.kept[:, :middle] + arrived[:, :middle]
            self.arrived = [swap(one, masks[at]) for one, masks in zip(sent, self.masks)]

    def shares(self, token):
        return self.kept + jnp.concatenate(token(*self.arrived), 0)


class Token:
    def __init__(self, mark):
        self.mark = mark

    def __call__(self, *values):
        *values, self.mark = lax.optimization_barrier((*values, self.mark))
        return values[0] if len(values) == 1 else values

    after = __call__


def flips_of(masks):
    return [
        sum(mask for mask, flip in zip(masks, flips) if flip)
        for flips in itertools.product((0, 1), repeat=len(masks))
    ]


def relative(array, offsets, me, size, axis):
    blocks = [
        lax.dynamic_slice_in_dim(array, jnp.bitwise_xor(me, offset) * size, size, axis)
        for offset in offsets
    ]
    return jnp.concatenate(blocks, axis)


def swap(array, mask):
    return lax.ppermute(
        array, "pages", [(one, one ^ mask) for one in range(lax.axis_size("pages"))]
    )


def fold(kept, arrived):
    half = kept.shape[0] // 2
    return kept[:half] + arrived[:half], kept[half:] + arrived[half:]


def halve(kept, masks):
    for mask in masks:
        half = kept.shape[0] // 2
        kept = kept[:half] + swap(kept[half:], mask)
    return kept


def in_order(*values):
    return lax.optimization_barrier(values)


def emb_total(share):
    if lax.axis_size("emb") != 4:
        return lax.psum(share, "emb")
    plane = lax.axis_index("emb")
    middle = jnp.logical_or(plane == 1, plane == 2)
    share = share + lax.ppermute(share, "emb", [(0, 1), (3, 2)])
    share = share + lax.ppermute(share, "emb", [(1, 2), (2, 1)])
    return jnp.where(middle, share, lax.ppermute(share, "emb", [(1, 0), (2, 3)]))


def on_device(
    text_embed,
    boxes,
    layout_tables,
    emb_gain,
    emb_bias,
    w_qkv,
    b_query,
    b_value,
    w_out,
    b_out,
    attn_gain,
    attn_bias,
    w_in,
    b_in,
    w_back,
    b_back,
    ffn_gain,
    ffn_bias,
    cotangent,
):
    token_rows = text_embed.shape[0]
    model_width = text_embed.shape[1]
    entries = layout_tables.shape[1]
    me = lax.axis_index("pages")
    plane = lax.axis_index("emb")
    devices = lax.axis_size("pages")
    planes = lax.axis_size("emb")
    outer_masks = [1 << bit for bit in range(1, devices.bit_length() - 1)]
    turn = len(outer_masks) // 2
    masks_one = [1] + outer_masks
    masks_two = [1] + outer_masks[turn:] + outer_masks[:turn]
    group = min(devices, 8)
    inner = me % group
    columns = model_width // group
    groups = [list(range(first, first + group)) for first in range(0, devices, group)]

    def row(vector):
        return vector.reshape(1, -1)

    def around(array, offset):
        return lax.ppermute(
            array, "emb", [((one + offset) % planes, one) for one in range(planes)]
        )

    def exchange(blocks):
        return lax.all_to_all(blocks, "pages", 0, 0, tiled=True, axis_index_groups=groups)

    own_columns = lax.dynamic_slice_in_dim(layout_tables[0], inner * columns, columns, 1)
    table_columns = [own_columns] + [around(own_columns, offset) for offset in range(1, planes)]
    group_boxes = lax.all_gather(boxes, "pages", axis=1, tiled=True, axis_index_groups=groups)
    tables = [(plane + offset) % planes for offset in range(planes)]
    twice = jnp.stack([jnp.where(table < 2, 1, 0) for table in tables]).astype(jnp.int32)
    split_boxes = group_boxes.reshape(4, group, PARTS, token_rows // PARTS).swapaxes(1, 2)
    split_boxes = split_boxes.reshape(4, group * token_rows)
    uses = jnp.stack([one for table in tables for one in table_indices(split_boxes, table)]).T
    looked_up = add_rows(
        twice[:1],
        uses[:, :2],
        table_columns[:1],
        jnp.zeros((group * token_rows, columns), wide),
        0,
        1,
    )
    parts = [
        exchange(
            add_rows(twice[1:], uses[:, 2:], table_columns[1:], looked_up, part, PARTS).reshape(
                group, token_rows // PARTS, columns
            )
        )
        for part in range(PARTS)
    ]

    bias_qkv = jnp.concatenate([b_query, jnp.zeros_like(b_query), b_value])
    packed, normed_emb, inverse_emb, emb_low = embed_and_project(
        parts, text_embed, row(emb_gain), row(emb_bias), w_qkv, row(bias_qkv)
    )
    context_low, normed_attn, inverse_attn, attn_low = attend(
        packed,
        w_out,
        row(b_out),
        normed_emb,
        row(emb_gain),
        row(emb_bias),
        row(attn_gain),
        row(attn_bias),
    )
    pre_act, expanded, output, d_r2, d_returned, g_ffn_gain, g_ffn_bias, g_back_bias = feed(
        attn_low,
        w_in,
        row(b_in),
        w_back,
        row(b_back),
        normed_attn,
        row(attn_gain),
        row(attn_bias),
        row(ffn_gain),
        row(ffn_bias),
        cotangent,
    )

    token = Token(output)
    flight = {}

    def gather_pages(product):
        return lax.psum_scatter(product, "pages", scatter_dimension=0, tiled=True)

    def inward(share):
        return lax.ppermute(share, "emb", [(0, 1), (3, 2)])

    def across(share):
        return lax.ppermute(share, "emb", [(1, 2), (2, 1)])

    def outward(share):
        return lax.ppermute(share, "emb", [(1, 0), (2, 3)])

    def settled(share, arrived):
        return jnp.where(jnp.logical_or(plane == 1, plane == 2), share, arrived)

    shares, halvings = {}, {}
    for step in ORDER:
        kind, name = step.split()
        if step == "first back":
            flight[name] = gather_pages(token.after(outer(expanded, token(d_returned))))
        elif step == "feed all":
            d_pre, g_in_bias, d_r1, d_attended, g_attn_gain, g_attn_bias, g_out_bias = feed_back(
                d_returned,
                w_back,
                pre_act,
                w_in,
                d_r2,
                normed_attn,
                inverse_attn,
                token(row(attn_gain)),
            )
            d_pre, d_attended = token.after(d_pre, d_attended)
            attn_rows = attn_low.T
            halvings["in"] = Halving(
                me,
                masks_one,
                masks_two,
                [(attn_rows, d_pre, 0, one) for one in range(4)],
                model_width,
            )
        elif step == "attend all":
            d_packed, g_query_bias, g_value_bias = attend_back(packed, token(d_attended), w_out)
            d_packed = token.after(d_packed)
            emb_rows = emb_low.T
            halvings["q"] = Halving(
                me,
                masks_one,
                masks_two,
                [(emb_rows, d_packed, one, 0) for one in range(3)]
                + [(context_low.T, d_attended, 0, 0)],
                model_width,
            )
        elif kind == "first":
            halvings[name].start(token)
        elif kind == "next":
            halvings[name].second(token)
        elif kind == "fold":
            halvings[name].third(token)
        elif kind == "finish":
            share = halvings[name].shares(token) if name in halvings else token(flight[name])
            pieces = SPLIT.get(name, (name,))
            size = share.shape[0] // len(pieces)
            share = token.after(
                *[share[at * size : (at + 1) * size] for at in range(len(pieces))]
            )
            shares.update(zip(pieces, share))
        elif kind == "send":
            shares[name] = token(shares[name])
            flight[name] = inward(shares[name])
        elif kind == "exchange":
            shares[name] = token.after(shares[name] + token(flight[name]))
            flight[name] = across(shares[name])
        elif kind == "return":
            shares[name] = token.after(shares[name] + token(flight[name]))
            flight[name] = outward(shares[name])
        elif kind == "end":
            shares[name] = token.after(settled(shares[name], token(flight[name])))
        elif kind == "embed":
            d_embed, g_emb_gain, g_emb_bias, squares, embed_blocks = embed_back(
                group,
                d_packed,
                w_qkv,
                d_r1,
                normed_emb,
                inverse_emb,
                token(row(emb_gain)),
            )
            squares, embed_blocks = token.after(squares, embed_blocks)
            flight["h"] = exchange(embed_blocks)
        elif kind == "spread":
            if name == "0":
                embed_columns = token(flight["h"]).reshape(group * token_rows, columns)
            offset = SPREAD[int(name)]
            uses = jnp.stack(table_indices(group_boxes, (plane + offset) % planes))
            part = token.after(spread_rows(token(uses), embed_columns, entries))
            flight["t" + name] = around(part, planes - offset) if offset else part
        elif step == "tables 0":
            owned = token(*[flight["t" + str(at)] for at in range(planes)])
            table_total = token.after(functools.reduce(jnp.add, owned))
            row_masks = [mask for mask in masks_one if mask >= group]
            if row_masks:
                table_total = halve(
                    relative(
                        table_total,
                        flips_of([mask // group for mask in row_masks]),
                        me // group,
                        entries * group // devices,
                        0,
                    ),
                    row_masks,
                )
            flight["u"] = exchange(table_total.reshape(group, entries // devices, columns))
        elif step == "tables 1":
            table_share = jnp.concatenate(list(token(flight["u"])), 1)
            table_share = token.after(table_share)
        elif step == "vector 0":
            vectors = [
                g_query_bias,
                g_value_bias,
                g_out_bias,
                g_attn_gain,
                g_attn_bias,
                g_in_bias,
                g_back_bias,
                g_ffn_gain,
                g_ffn_bias,
                g_emb_gain,
                g_emb_bias,
                jnp.full((devices,), jnp.sum(squares)),
            ]
            stacked = jnp.concatenate([vector.reshape(devices, -1) for vector in vectors], 1)
            stacked = token.after(token(stacked))
            flight["v1"] = lax.all_to_all(stacked, "pages", 0, 0, tiled=True)
        elif step == "vector 1":
            vector_share = token.after(jnp.sum(token(flight["v1"]), 0, keepdims=True))
            flight["v2"] = lax.ppermute(vector_share, "emb", [(0, 1), (3, 2)])
        elif step == "vector 2":
            vector_share = token.after(vector_share + token(flight["v2"]))
            flight["v3"] = lax.ppermute(vector_share, "emb", [(1, 2), (2, 1)])
        elif step == "vector 3":
            vector_share = token.after(vector_share + token(flight["v3"]))
            flight["v4"] = lax.ppermute(vector_share, "emb", [(1, 0), (2, 3)])
        elif step == "vector 4":
            middle = jnp.logical_or(plane == 1, plane == 2)
            vector_share = jnp.where(middle, vector_share, token(flight["v4"]))[0]
    for name, pieces in SPLIT.items():
        shares[name] = jnp.concatenate([shares[one] for one in pieces], 0)
    g_back = shares["back"]
    g_in = jnp.concatenate(list(shares["in"]), 1)
    g_qkv = jnp.concatenate(list(shares["q"][:3]), 1)
    g_out = shares["q"][3]

    totals = []
    first = 0
    for vector in vectors:
        length = vector.size // devices
        totals.append(vector_share[first : first + length])
        first += length
    entry_count = token_rows * model_width * devices * planes
    rms_grad = jnp.sqrt(totals[11][0] / entry_count)
    return (
        token.mark,
        d_embed,
        table_share[None],
        totals[9],
        totals[10],
        g_qkv,
        totals[0],
        totals[1],
        g_out,
        totals[2],
        totals[3],
        totals[4],
        g_in,
        totals[5],
        g_back,
        totals[6],
        totals[7],
        totals[8],
        rms_grad,
    )


def solution(mesh):
    return jax.shard_map(
        on_device,
        mesh=mesh,
        in_specs=(
            P(("pages", "emb"), None),
            P(None, ("pages", "emb")),
            P("emb", None, None),
            P(),
            P(),
            P(),
            P(),
            P(),
            P(),
            P(),
            P(),
            P(),
            P(),
            P(),
            P(),
            P(),
            P(),
            P(),
            P(("pages", "emb"), None),
        ),
        out_specs=(
            P(("pages", "emb"), None),
            P(("pages", "emb"), None),
            P("emb", "pages", None),
            P("pages"),
            P("pages"),
            P("pages", None),
            P("pages"),
            P("pages"),
            P("pages", None),
            P("pages"),
            P("pages"),
            P("pages"),
            P("pages", None),
            P("pages"),
            P("pages", None),
            P("pages"),
            P("pages"),
            P("pages"),
            P(),
        ),
        check_vma=False,
    )
```

```python
import functools
import itertools

import jax
import jax.numpy as jnp
from jax import lax
from jax.experimental import pallas as pl
from jax.experimental.pallas import tpu as pltpu
from jax.sharding import PartitionSpec as P

HEADS = 16
HEAD = 64
PAGE = 512
PAIR = 2 * HEAD

EPSILON = 1e-05
SQRT_HALF = 0.7071067811865476
INV_ROOT_TAU = 0.3989422804014327

wide = jnp.float32
narrow = jnp.bfloat16
SPREAD = (2, 1, 3, 0)
SPLIT = {"back": ("backa", "backb"), "in": ("ina", "inb"), "q": ("qa", "qb")}
ORDER = (
    "first back",
    "feed all",
    "first in",
    "attend all",
    "embed all",
    "first q",
    "spread 0",
    "next in",
    "spread 1",
    "spread 2",
    "spread 3",
    "fold in",
    "tables 0",
    "next q",
    "finish back",
    "send backa",
    "finish in",
    "send backb",
    "tables 1",
    "exchange backa",
    "send ina",
    "vector 0",
    "exchange backb",
    "return backa",
    "fold q",
    "end backa",
    "send inb",
    "return backb",
    "exchange ina",
    "vector 1",
    "finish q",
    "send qa",
    "send qb",
    "end backb",
    "return ina",
    "exchange inb",
    "vector 2",
    "end ina",
    "return inb",
    "exchange qa",
    "vector 3",
    "end inb",
    "return qa",
    "exchange qb",
    "vector 4",
    "end qa",
    "return qb",
    "end qb",
)
PARTS = 1
LITTLE = pl.CostEstimate(flops=1024, bytes_accessed=1024, transcendentals=0)
ROOM = pltpu.CompilerParams(vmem_limit_bytes=32 * 2**20)
MOST = pltpu.CompilerParams(vmem_limit_bytes=32 * 2**20)


def shape(dims, dtype=wide):
    return jax.ShapeDtypeStruct(dims, dtype)


def whole(*dims):
    return pl.BlockSpec(dims, lambda *_: (0,) * len(dims))


def normalize(values):
    averaged = jnp.mean(values, -1, keepdims=True)
    centered = values - averaged
    inverse = lax.rsqrt(jnp.mean(centered * centered, -1, keepdims=True) + EPSILON)
    return centered * inverse, inverse


def norm_back(incoming, normed, inverse, gain):
    scaled = incoming * gain
    offset_mean = jnp.mean(scaled, -1, keepdims=True)
    along_mean = jnp.mean(scaled * normed, -1, keepdims=True)
    return inverse * (scaled - offset_mean - normed * along_mean)


def down(values):
    return jnp.sum(values, 0, keepdims=True)


def mul(left, right):
    return jnp.dot(left, right, preferred_element_type=wide)


def mul_rows(left, right):
    return lax.dot_general(left, right, (((1,), (1,)), ((), ())), preferred_element_type=wide)


def mul_down(left, right):
    return lax.dot_general(left, right, (((0,), (0,)), ((), ())), preferred_element_type=wide)


def table_indices(box_rows, table):
    left_x, top_y, right_x, bottom_y = box_rows[0], box_rows[1], box_rows[2], box_rows[3]
    first = jnp.where(
        table == 0,
        left_x,
        jnp.where(table == 1, top_y, jnp.where(table == 2, right_x - left_x, bottom_y - top_y)),
    )
    second = jnp.where(table == 0, right_x, jnp.where(table == 1, bottom_y, -1))
    return first, second


def two_halves(values):
    high = values.astype(narrow)
    return high, (values - high.astype(wide)).astype(narrow)


def hits(entry, indices):
    return jnp.where(entry == indices, 1.0, 0.0)


def lookup_kernel(twice_ref, idx_ref, *refs):
    tables, total_ref, out_ref, halves = refs[:-3], refs[-3], refs[-2], refs[-1]
    entries, width = tables[0].shape

    @pl.when(pl.program_id(0) == 0)
    def _():
        for one, table in enumerate(tables):
            halves[one, :, :width], halves[one, :, width:] = two_halves(table[...])

    entry = lax.broadcasted_iota(jnp.int32, (idx_ref.shape[0], entries), 1)

    def add(one, counts):
        rows = mul(counts.astype(narrow), halves[one])
        out_ref[...] += rows[:, :width] + rows[:, width:]

    out_ref[...] = total_ref[...]
    for one in range(len(tables)):
        first = idx_ref[:, 2 * one : 2 * one + 1]
        second = idx_ref[:, 2 * one + 1 : 2 * one + 2]

        @pl.when(twice_ref[one] == 1)
        def _():
            add(one, hits(entry, first) + hits(entry, second))

        @pl.when(twice_ref[one] == 0)
        def _():
            add(one, hits(entry, first))


def add_rows(twice, indices, tables, total, part, parts):
    tokens = total.shape[0]
    entries, width = tables[0].shape
    block = PAGE
    steps = tokens // block // parts
    return pl.pallas_call(
        lookup_kernel,
        grid_spec=pltpu.PrefetchScalarGridSpec(
            num_scalar_prefetch=1,
            grid=(steps,),
            in_specs=[
                pl.BlockSpec((block, indices.shape[1]), lambda step, *_: (steps * part + step, 0))
            ]
            + [whole(entries, width)] * len(tables)
            + [pl.BlockSpec((block, width), lambda step, *_: (steps * part + step, 0))],
            out_specs=pl.BlockSpec((block, width), lambda step, *_: (step, 0)),
            scratch_shapes=[pltpu.VMEM((len(tables), entries, 2 * width), narrow)],
        ),
        out_shape=shape((tokens // parts, width)),
        compiler_params=ROOM,
        cost_estimate=LITTLE,
        name="look_up",
    )(twice, indices, *tables, total)


def spread_kernel(idx_ref, rows_ref, out_ref):
    width = rows_ref.shape[1]
    entry = lax.broadcasted_iota(jnp.int32, (out_ref.shape[0], rows_ref.shape[0]), 0)
    counts = hits(entry, idx_ref[0:1, :]) + hits(entry, idx_ref[1:2, :])
    both = mul(counts.astype(narrow), jnp.concatenate(two_halves(rows_ref[...]), 1))
    share = both[:, :width] + both[:, width:]

    @pl.when(pl.program_id(0) == 0)
    def _():
        out_ref[...] = share

    @pl.when(pl.program_id(0) > 0)
    def _():
        out_ref[...] += share


def spread_rows(indices, rows, entries):
    tokens, width = rows.shape
    block = 2 * PAGE
    return pl.pallas_call(
        spread_kernel,
        grid=(tokens // block,),
        in_specs=[
            pl.BlockSpec((2, block), lambda step: (0, step)),
            pl.BlockSpec((block, width), lambda step: (step, 0)),
        ],
        out_specs=whole(entries, width),
        out_shape=shape((entries, width)),
        compiler_params=ROOM,
        cost_estimate=LITTLE,
        name="spread",
    )(indices, rows)


def project_kernel(*refs):
    parts, (text, gain, bias, weight, weight_bias) = refs[:-9], refs[-9:-4]
    packed, normed, inverse, low = refs[-4:]
    group, rows, width = parts[0].shape

    @pl.when(pl.program_id(0) == 0)
    def _():
        for at, part in enumerate(parts):
            for one in range(group):
                normed[at * rows : (at + 1) * rows, one * width : (one + 1) * width] = part[one]
        normed[...], inverse[...] = normalize(normed[...] + text[...].astype(wide))
        low[...] = (normed[...] * gain[...] + bias[...]).astype(narrow)

    packed[...] = (mul(low[...], weight[...]) + weight_bias[...]).astype(narrow)


def embed_and_project(parts, text, gain, bias, weight, weight_bias):
    tokens, width = text.shape
    block = width // 2
    steps = weight.shape[1] // block
    return pl.pallas_call(
        project_kernel,
        grid=(steps,),
        in_specs=[whole(*part.shape) for part in parts]
        + [
            whole(tokens, width),
            whole(1, width),
            whole(1, width),
            pl.BlockSpec((width, block), lambda step: (0, step)),
            pl.BlockSpec((1, block), lambda step: (0, step)),
        ],
        out_specs=[
            pl.BlockSpec((tokens, block), lambda step: (0, step)),
            whole(tokens, width),
            whole(tokens, 1),
            whole(tokens, width),
        ],
        out_shape=[
            shape((tokens, weight.shape[1]), narrow),
            shape((tokens, width)),
            shape((tokens, 1)),
            shape((tokens, width), narrow),
        ],
        compiler_params=ROOM,
        cost_estimate=LITTLE,
        name="embed_and_project",
    )(*parts, text, gain, bias, weight, weight_bias)


def one_head(rows, head):
    lane = lax.broadcasted_iota(jnp.int32, rows.shape, 1)
    return jnp.where((lane < HEAD) == (head == 0), rows, jnp.zeros_like(rows))


def head_probs(queries, keys, head):
    scores = mul_rows(one_head(queries, head), keys) * HEAD ** (-0.5)
    exponent = jnp.exp(scores - jnp.max(scores, -1, keepdims=True))
    return exponent * (1.0 / jnp.sum(exponent, -1, keepdims=True))


def attend_kernel(
    queries, keys, values, weight, weight_bias, normed_emb, emb_gain, emb_bias, gain, bias,
    context, normed, inverse, low,
):
    pair = pl.program_id(0)
    lane = lax.broadcasted_iota(jnp.int32, values.shape, 1)
    parts = []
    for head in range(2):
        scores = mul_rows(one_head(queries[...], head), keys[...]) * HEAD ** (-0.5)
        exponent = jnp.exp(scores - jnp.max(scores, -1, keepdims=True))
        probs = exponent * (1.0 / jnp.sum(exponent, -1, keepdims=True))
        parts.append(mul(probs.astype(narrow), values[...]))
    place = pl.multiple_of(pair * PAIR, PAIR)
    context[:, pl.ds(place, PAIR)] = jnp.where(lane < HEAD, parts[0], parts[1]).astype(narrow)

    @pl.when(pair == pl.num_programs(0) - 1)
    def _():
        hidden = normed_emb[...] * emb_gain[...] + emb_bias[...]
        attended = mul(context[...], weight[...]) + weight_bias[...]
        normed[...], inverse[...] = normalize(hidden + attended)
        low[...] = (normed[...] * gain[...] + bias[...]).astype(narrow)


def attend(packed, weight, weight_bias, normed_emb, emb_gain, emb_bias, gain, bias):
    tokens, width = normed_emb.shape
    pairs = width // PAIR
    vector = whole(1, width)
    return pl.pallas_call(
        attend_kernel,
        grid=(pairs,),
        in_specs=[
            pl.BlockSpec((tokens, PAIR), lambda pair: (0, pair)),
            pl.BlockSpec((tokens, PAIR), lambda pair: (0, pairs + pair)),
            pl.BlockSpec((tokens, PAIR), lambda pair: (0, 2 * pairs + pair)),
            whole(*weight.shape),
            vector,
            whole(tokens, width),
            vector,
            vector,
            vector,
            vector,
        ],
        out_specs=[
            whole(tokens, width),
            whole(tokens, width),
            whole(tokens, 1),
            whole(tokens, width),
        ],
        out_shape=[
            shape((tokens, width), narrow),
            shape((tokens, width)),
            shape((tokens, 1)),
            shape((tokens, width), narrow),
        ],
        compiler_params=ROOM,
        cost_estimate=LITTLE,
        name="attend",
    )(packed, packed, packed, weight, weight_bias, normed_emb, emb_gain, emb_bias, gain, bias)


def feed_kernel(
    low, w_in, b_in, w_back, b_back, normed_attn, attn_gain, attn_bias, gain, bias, cotangent,
    pre_act, expanded, output, d_r2, d_returned, g_gain, g_bias, g_back_bias, total,
):
    step = pl.program_id(0)
    pre = mul(low[...], w_in[...]) + b_in[...]
    pre_act[...] = pre
    expanded[...] = (pre * (0.5 * (1.0 + lax.erf(pre * SQRT_HALF)))).astype(narrow)
    share = mul(expanded[...], w_back[...])

    @pl.when(step == 0)
    def _():
        total[...] = share

    @pl.when(step > 0)
    def _():
        total[...] += share

    @pl.when(step == pl.num_programs(0) - 1)
    def _():
        hidden = normed_attn[...] * attn_gain[...] + attn_bias[...]
        normed, inverse = normalize(hidden + (total[...] + b_back[...]))
        output[...] = (normed * gain[...] + bias[...]).astype(narrow)
        incoming = cotangent[...].astype(wide)
        d_r2[...] = norm_back(incoming, normed, inverse, gain[...])
        g_gain[...] = down(incoming * normed)
        g_bias[...] = down(incoming)
        rounded = d_r2[...].astype(narrow)
        d_returned[...] = rounded
        g_back_bias[...] = down(rounded.astype(wide))


def feed(low, w_in, b_in, w_back, b_back, normed, attn_gain, attn_bias, gain, bias, cotangent):
    tokens, width = low.shape
    expand = w_in.shape[1]
    block = width // 2
    vector = whole(1, width)
    rows = whole(tokens, width)
    part = pl.BlockSpec((tokens, block), lambda step: (0, step))
    return pl.pallas_call(
        feed_kernel,
        grid=(expand // block,),
        in_specs=[
            rows,
            pl.BlockSpec((width, block), lambda step: (0, step)),
            pl.BlockSpec((1, block), lambda step: (0, step)),
            pl.BlockSpec((block, width), lambda step: (step, 0)),
            vector,
            rows,
            vector,
            vector,
            vector,
            vector,
            rows,
        ],
        out_specs=[part, part, rows, rows, rows, vector, vector, vector],
        out_shape=[
            shape((tokens, expand)),
            shape((tokens, expand), narrow),
            shape((tokens, width), narrow),
            shape((tokens, width)),
            shape((tokens, width), narrow),
            shape((1, width)),
            shape((1, width)),
            shape((1, width)),
        ],
        scratch_shapes=[pltpu.VMEM((tokens, width), wide)],
        compiler_params=ROOM,
        cost_estimate=LITTLE,
        name="feed",
    )(low, w_in, b_in, w_back, b_back, normed, attn_gain, attn_bias, gain, bias, cotangent)


def gelu_slope(pre_act):
    return (
        0.5 * (1.0 + lax.erf(pre_act * SQRT_HALF))
        + pre_act * jnp.exp(-0.5 * pre_act * pre_act) * INV_ROOT_TAU
    )


def feed_back_kernel(
    d_returned, w_back, pre_act, w_in, d_r2, normed, inverse, gain,
    d_pre, g_in_bias, d_r1, d_attended, g_gain, g_bias, g_out_bias, total,
):
    step = pl.program_id(0)
    rounded = (mul_rows(d_returned[...], w_back[...]) * gelu_slope(pre_act[...])).astype(narrow)
    d_pre[...] = rounded
    g_in_bias[...] = down(rounded.astype(wide))
    share = mul_rows(rounded, w_in[...])

    @pl.when(step == 0)
    def _():
        total[...] = share

    @pl.when(step > 0)
    def _():
        total[...] += share

    @pl.when(step == pl.num_programs(0) - 1)
    def _():
        incoming = d_r2[...] + total[...]
        d_r1[...] = norm_back(incoming, normed[...], inverse[...], gain[...])
        g_gain[...] = down(incoming * normed[...])
        g_bias[...] = down(incoming)
        d_attended[...] = d_r1[...].astype(narrow)
        g_out_bias[...] = down(d_attended[...].astype(wide))


def feed_back(d_returned, w_back, pre_act, w_in, d_r2, normed, inverse, gain):
    tokens, width = d_returned.shape
    expand = pre_act.shape[1]
    block = width // 2
    vector = whole(1, width)
    rows = whole(tokens, width)
    part = pl.BlockSpec((tokens, block), lambda step: (0, step))
    return pl.pallas_call(
        feed_back_kernel,
        grid=(expand // block,),
        in_specs=[
            rows,
            pl.BlockSpec((block, width), lambda step: (step, 0)),
            part,
            pl.BlockSpec((width, block), lambda step: (0, step)),
            rows,
            rows,
            whole(tokens, 1),
            vector,
        ],
        out_specs=[
            part,
            pl.BlockSpec((1, block), lambda step: (0, step)),
            rows,
            rows,
            vector,
            vector,
            vector,
        ],
        out_shape=[
            shape((tokens, expand), narrow),
            shape((1, expand)),
            shape((tokens, width)),
            shape((tokens, width), narrow),
            shape((1, width)),
            shape((1, width)),
            shape((1, width)),
        ],
        scratch_shapes=[pltpu.VMEM((tokens, width), wide)],
        compiler_params=MOST,
        cost_estimate=LITTLE,
        name="feed_back",
    )(d_returned, w_back, pre_act, w_in, d_r2, normed, inverse, gain)


def attend_back_kernel(
    queries, keys, values, d_attended, weight, d_packed, g_query_bias, g_value_bias
):
    d_context = mul_rows(d_attended[...], weight[...]).astype(narrow)
    d_queries, d_keys, d_values = 0.0, 0.0, 0.0
    for head in range(2):
        probs = head_probs(queries[...], keys[...], head)
        own_context = one_head(d_context, head)
        d_values += mul_down(probs.astype(narrow), own_context)
        d_probs = mul_rows(own_context, values[...])
        along = jnp.sum(probs * d_probs, -1, keepdims=True)
        d_scores = (probs * (d_probs - along)).astype(narrow)
        d_queries += mul(d_scores, one_head(keys[...], head))
        d_keys += mul_down(d_scores, one_head(queries[...], head))
    d_queries = (d_queries * HEAD ** (-0.5)).astype(narrow)
    d_values = d_values.astype(narrow)
    d_packed[0] = d_queries
    d_packed[1] = (d_keys * HEAD ** (-0.5)).astype(narrow)
    d_packed[2] = d_values
    g_query_bias[...] = down(d_queries.astype(wide))
    g_value_bias[...] = down(d_values.astype(wide))


def attend_back(packed, d_attended, weight):
    tokens, width = d_attended.shape
    pairs = width // PAIR
    return pl.pallas_call(
        attend_back_kernel,
        grid=(pairs,),
        in_specs=[
            pl.BlockSpec((tokens, PAIR), lambda pair: (0, pair)),
            pl.BlockSpec((tokens, PAIR), lambda pair: (0, pairs + pair)),
            pl.BlockSpec((tokens, PAIR), lambda pair: (0, 2 * pairs + pair)),
            whole(tokens, width),
            pl.BlockSpec((PAIR, width), lambda pair: (pair, 0)),
        ],
        out_specs=[
            pl.BlockSpec((3, tokens, PAIR), lambda pair: (0, 0, pair)),
            pl.BlockSpec((1, PAIR), lambda pair: (0, pair)),
            pl.BlockSpec((1, PAIR), lambda pair: (0, pair)),
        ],
        out_shape=[shape((3, tokens, width), narrow), shape((1, width)), shape((1, width))],
        compiler_params=MOST,
        cost_estimate=LITTLE,
        name="attend_back",
    )(packed, packed, packed, d_attended, weight)


def embed_back_kernel(
    d_packed, weight, d_r1, normed, inverse, gain, d_embed, g_gain, g_bias, squares, blocks, total
):
    step = pl.program_id(0)
    share = mul_rows(d_packed[0], weight[...])

    @pl.when(step == 0)
    def _():
        total[...] = d_r1[...] + share

    @pl.when(step > 0)
    def _():
        total[...] += share

    @pl.when(step == pl.num_programs(0) - 1)
    def _():
        incoming = total[...]
        d_embed[...] = norm_back(incoming, normed[...], inverse[...], gain[...])
        g_gain[...] = down(incoming * normed[...])
        g_bias[...] = down(incoming)
        squares[...] = down(d_embed[...] * d_embed[...])
        columns = blocks.shape[2]
        for one in range(blocks.shape[0]):
            blocks[one] = d_embed[:, one * columns : (one + 1) * columns]


def embed_back(group, d_packed, weight, d_r1, normed, inverse, gain):
    tokens, width = d_r1.shape
    block = width // 2
    vector = whole(1, width)
    rows = whole(tokens, width)
    columns = width // group
    return pl.pallas_call(
        embed_back_kernel,
        grid=(3 * width // block,),
        in_specs=[
            pl.BlockSpec((1, tokens, block), lambda step: (step // 2, 0, step % 2)),
            pl.BlockSpec((width, block), lambda step: (0, step)),
            rows,
            rows,
            whole(tokens, 1),
            vector,
        ],
        out_specs=[rows, vector, vector, vector, whole(group, tokens, columns)],
        scratch_shapes=[pltpu.VMEM((tokens, width), wide)],
        out_shape=[
            shape((tokens, width)),
            shape((1, width)),
            shape((1, width)),
            shape((1, width)),
            shape((group, tokens, columns)),
        ],
        compiler_params=MOST,
        cost_estimate=LITTLE,
        name="embed_back",
    )(d_packed, weight, d_r1, normed, inverse, gain)


def outer_kernel(left, right, out):
    out[...] = mul_down(left[...], right[...].reshape(right.shape[-2:]))


def outer(left, right):
    tokens, rows = left.shape
    width = right.shape[1]
    block = min(rows, 512)
    return pl.pallas_call(
        outer_kernel,
        grid=(rows // block,),
        in_specs=[pl.BlockSpec((tokens, block), lambda row: (0, row)), whole(tokens, width)],
        out_specs=pl.BlockSpec((block, width), lambda row: (row, 0)),
        out_shape=shape((rows, width)),
        compiler_params=MOST,
        cost_estimate=LITTLE,
        name="outer",
    )(left, right)


def flat(ref):
    return ref[...].reshape(ref.shape[-2:])


def product(left, right):
    return mul_down(left, right) if left.shape[0] == right.shape[0] else mul(left, right)


def first_kernel(plan, table, *refs):
    count = len(plan)
    lefts, rights, out = refs[:count], refs[count : 2 * count], refs[-1]
    for one in range(count):
        out[one] = product(lefts[one][...], flat(rights[one]))


def next_kernel(plan, table, *refs):
    count = len(plan)
    keeps, sends, rights = refs[:count], refs[count : 2 * count], refs[2 * count : 3 * count]
    arrived_keep, arrived_send, kept, sent_one, sent_two = refs[3 * count :]
    for one in range(count):
        right = flat(rights[one])
        kept[one] = product(keeps[one][...], right) + arrived_keep[one]
        sent = sent_one if one < count // 2 else sent_two
        sent[one % (count // 2)] = product(sends[one][...], right) + arrived_send[one]


class Halving:
    def __init__(self, me, masks_one, masks_two, streams, width):
        self.masks = (masks_one, masks_two)
        self.devices = lax.axis_size("pages")
        self.width = width
        self.rows = streams[0][0].shape[1] // self.devices
        self.across = self.rows % 128 == 0
        self.streams = [
            (left if self.across else left.T, *rest) for left, *rest in streams
        ]
        self.table = jnp.concatenate(
            [
                jnp.bitwise_xor(me, jnp.array(flips_of(masks), jnp.int32))
                for masks in self.masks
            ]
        )

    def left(self, one, start):
        place = (one >= len(self.streams) // 2) * self.devices + start
        left = self.streams[one][0]
        if self.across:
            return pl.BlockSpec(
                (left.shape[0], self.rows), lambda row, table: (0, table[place + row])
            )
        return pl.BlockSpec(
            (self.rows, left.shape[1]), lambda row, table: (table[place + row], 0)
        )

    def right(self, one):
        _, right, part, column = self.streams[one]
        if right.ndim == 3:
            return pl.BlockSpec((1, right.shape[1], self.width), lambda *_: (part, 0, column))
        return pl.BlockSpec((right.shape[0], self.width), lambda *_: (0, column))

    def block(self, count, start):
        return pl.BlockSpec((count, self.rows, self.width), lambda row, *_: (0, start + row, 0))

    def first(self, table):
        half = self.devices // 2
        count = len(self.streams)
        return pl.pallas_call(
            functools.partial(first_kernel, self.streams),
            grid_spec=pltpu.PrefetchScalarGridSpec(
                num_scalar_prefetch=1,
                grid=(half,),
                in_specs=[self.left(one, half) for one in range(count)]
                + [self.right(one) for one in range(count)],
                out_specs=self.block(count, 0),
            ),
            out_shape=shape((count, half * self.rows, self.width)),
            compiler_params=MOST,
            cost_estimate=LITTLE,
            name="halving_first",
        )(table, *[one[0] for one in self.streams], *[one[1] for one in self.streams])

    def next(self, table, arrived):
        quarter = self.devices // 4
        count = len(self.streams)
        lefts = [one[0] for one in self.streams]
        return pl.pallas_call(
            functools.partial(next_kernel, self.streams),
            grid_spec=pltpu.PrefetchScalarGridSpec(
                num_scalar_prefetch=1,
                grid=(quarter,),
                in_specs=[self.left(one, 0) for one in range(count)]
                + [self.left(one, quarter) for one in range(count)]
                + [self.right(one) for one in range(count)]
                + [self.block(count, 0), self.block(count, quarter)],
                out_specs=[
                    self.block(count, 0),
                    self.block(count // 2, 0),
                    self.block(count // 2, 0),
                ],
            ),
            out_shape=[
                shape((part, quarter * self.rows, self.width))
                for part in (count, count // 2, count // 2)
            ],
            compiler_params=MOST,
            cost_estimate=LITTLE,
            name="halving_next",
        )(table, *lefts, *lefts, *[one[1] for one in self.streams], arrived, arrived)

    def start(self, token):
        self.from_core = swap(token.after(self.first(token(self.table))), 1)

    def second(self, token):
        self.kept, *sent = token.after(*self.next(self.table, token(self.from_core)))
        self.arrived = [swap(one, masks[1]) for one, masks in zip(sent, self.masks)]

    def third(self, token):
        for at in range(2, len(self.masks[0])):
            arrived = jnp.concatenate(token(*self.arrived), 0)
            middle = self.kept.shape[1] // 2
            half = len(self.streams) // 2
            sent = self.kept[:, middle:] + arrived[:, middle:]
            sent = token.after(sent[:half], sent[half:])
            self.kept = self.kept[:, :middle] + arrived[:, :middle]
            self.arrived = [swap(one, masks[at]) for one, masks in zip(sent, self.masks)]

    def shares(self, token):
        return self.kept + jnp.concatenate(token(*self.arrived), 0)


class Token:
    def __init__(self, mark):
        self.mark = mark

    def __call__(self, *values):
        *values, self.mark = lax.optimization_barrier((*values, self.mark))
        return values[0] if len(values) == 1 else values

    after = __call__


def flips_of(masks):
    return [
        sum(mask for mask, flip in zip(masks, flips) if flip)
        for flips in itertools.product((0, 1), repeat=len(masks))
    ]


def relative(array, offsets, me, size, axis):
    blocks = [
        lax.dynamic_slice_in_dim(array, jnp.bitwise_xor(me, offset) * size, size, axis)
        for offset in offsets
    ]
    return jnp.concatenate(blocks, axis)


def swap(array, mask):
    return lax.ppermute(
        array, "pages", [(one, one ^ mask) for one in range(lax.axis_size("pages"))]
    )


def fold(kept, arrived):
    half = kept.shape[0] // 2
    return kept[:half] + arrived[:half], kept[half:] + arrived[half:]


def halve(kept, masks):
    for mask in masks:
        half = kept.shape[0] // 2
        kept = kept[:half] + swap(kept[half:], mask)
    return kept


def in_order(*values):
    return lax.optimization_barrier(values)


def emb_total(share):
    if lax.axis_size("emb") != 4:
        return lax.psum(share, "emb")
    plane = lax.axis_index("emb")
    middle = jnp.logical_or(plane == 1, plane == 2)
    share = share + lax.ppermute(share, "emb", [(0, 1), (3, 2)])
    share = share + lax.ppermute(share, "emb", [(1, 2), (2, 1)])
    return jnp.where(middle, share, lax.ppermute(share, "emb", [(1, 0), (2, 3)]))


def on_device(
    text_embed,
    boxes,
    layout_tables,
    emb_gain,
    emb_bias,
    w_qkv,
    b_query,
    b_value,
    w_out,
    b_out,
    attn_gain,
    attn_bias,
    w_in,
    b_in,
    w_back,
    b_back,
    ffn_gain,
    ffn_bias,
    cotangent,
):
    token_rows = text_embed.shape[0]
    model_width = text_embed.shape[1]
    entries = layout_tables.shape[1]
    me = lax.axis_index("pages")
    plane = lax.axis_index("emb")
    devices = lax.axis_size("pages")
    planes = lax.axis_size("emb")
    outer_masks = [1 << bit for bit in range(1, devices.bit_length() - 1)]
    turn = len(outer_masks) // 2
    masks_one = [1] + outer_masks
    masks_two = [1] + outer_masks[turn:] + outer_masks[:turn]
    group = min(devices, 8)
    inner = me % group
    columns = model_width // group
    groups = [list(range(first, first + group)) for first in range(0, devices, group)]

    def row(vector):
        return vector.reshape(1, -1)

    def around(array, offset):
        return lax.ppermute(
            array, "emb", [((one + offset) % planes, one) for one in range(planes)]
        )

    def exchange(blocks):
        return lax.all_to_all(blocks, "pages", 0, 0, tiled=True, axis_index_groups=groups)

    own_columns = lax.dynamic_slice_in_dim(layout_tables[0], inner * columns, columns, 1)
    table_columns = [own_columns] + [around(own_columns, offset) for offset in range(1, planes)]
    group_boxes = lax.all_gather(boxes, "pages", axis=1, tiled=True, axis_index_groups=groups)
    tables = [(plane + offset) % planes for offset in range(planes)]
    twice = jnp.stack([jnp.where(table < 2, 1, 0) for table in tables]).astype(jnp.int32)
    split_boxes = group_boxes.reshape(4, group, PARTS, token_rows // PARTS).swapaxes(1, 2)
    split_boxes = split_boxes.reshape(4, group * token_rows)
    uses = jnp.stack([one for table in tables for one in table_indices(split_boxes, table)]).T
    def look_up(chosen, total, part, parts):
        return add_rows(
            jnp.stack([twice[one] for one in chosen]),
            jnp.concatenate([uses[:, 2 * one : 2 * one + 2] for one in chosen], 1),
            [table_columns[one] for one in chosen],
            total,
            part,
            parts,
        )

    looked_up = jnp.zeros((group * token_rows, columns), wide)
    near = sorted({1, planes - 1})
    for chosen in ([0], near):
        looked_up = look_up(chosen, looked_up, 0, 1)
    parts = [
        exchange(
            look_up(list(range(2, planes - 1)), looked_up, part, PARTS).reshape(group, token_rows // PARTS, columns)
        )
        for part in range(PARTS)
    ]

    bias_qkv = jnp.concatenate([b_query, jnp.zeros_like(b_query), b_value])
    packed, normed_emb, inverse_emb, emb_low = embed_and_project(
        parts, text_embed, row(emb_gain), row(emb_bias), w_qkv, row(bias_qkv)
    )
    context_low, normed_attn, inverse_attn, attn_low = attend(
        packed,
        w_out,
        row(b_out),
        normed_emb,
        row(emb_gain),
        row(emb_bias),
        row(attn_gain),
        row(attn_bias),
    )
    pre_act, expanded, output, d_r2, d_returned, g_ffn_gain, g_ffn_bias, g_back_bias = feed(
        attn_low,
        w_in,
        row(b_in),
        w_back,
        row(b_back),
        normed_attn,
        row(attn_gain),
        row(attn_bias),
        row(ffn_gain),
        row(ffn_bias),
        cotangent,
    )

    token = Token(output)
    flight = {}

    def gather_pages(product):
        return lax.psum_scatter(product, "pages", scatter_dimension=0, tiled=True)

    def inward(share):
        return lax.ppermute(share, "emb", [(0, 1), (3, 2)])

    def across(share):
        return lax.ppermute(share, "emb", [(1, 2), (2, 1)])

    def outward(share):
        return lax.ppermute(share, "emb", [(1, 0), (2, 3)])

    def settled(share, arrived):
        return jnp.where(jnp.logical_or(plane == 1, plane == 2), share, arrived)

    shares, halvings = {}, {}
    for step in ORDER:
        kind, name = step.split()
        if step == "first back":
            flight[name] = gather_pages(token.after(outer(expanded, token(d_returned))))
        elif step == "feed all":
            d_pre, g_in_bias, d_r1, d_attended, g_attn_gain, g_attn_bias, g_out_bias = feed_back(
                d_returned,
                w_back,
                pre_act,
                w_in,
                d_r2,
                normed_attn,
                inverse_attn,
                token(row(attn_gain)),
            )
            d_pre, d_attended = token.after(d_pre, d_attended)
            halvings["in"] = Halving(
                me,
                masks_one,
                masks_two,
                [(attn_low, d_pre, 0, one) for one in range(4)],
                model_width,
            )
        elif step == "attend all":
            d_packed, g_query_bias, g_value_bias = attend_back(packed, token(d_attended), w_out)
            d_packed = token.after(d_packed)
            halvings["q"] = Halving(
                me,
                masks_one,
                masks_two,
                [(emb_low, d_packed, one, 0) for one in range(3)]
                + [(context_low, d_attended, 0, 0)],
                model_width,
            )
        elif kind == "first":
            halvings[name].start(token)
        elif kind == "next":
            halvings[name].second(token)
        elif kind == "fold":
            halvings[name].third(token)
        elif kind == "finish":
            share = halvings[name].shares(token) if name in halvings else token(flight[name])
            pieces = SPLIT.get(name, (name,))
            size = share.shape[0] // len(pieces)
            share = token.after(
                *[share[at * size : (at + 1) * size] for at in range(len(pieces))]
            )
            shares.update(zip(pieces, share))
        elif kind == "send":
            shares[name] = token(shares[name])
            flight[name] = inward(shares[name])
        elif kind == "exchange":
            shares[name] = token.after(shares[name] + token(flight[name]))
            flight[name] = across(shares[name])
        elif kind == "return":
            shares[name] = token.after(shares[name] + token(flight[name]))
            flight[name] = outward(shares[name])
        elif kind == "end":
            shares[name] = token.after(settled(shares[name], token(flight[name])))
        elif kind == "embed":
            d_embed, g_emb_gain, g_emb_bias, squares, embed_blocks = embed_back(
                group,
                d_packed,
                w_qkv,
                d_r1,
                normed_emb,
                inverse_emb,
                token(row(emb_gain)),
            )
            squares, embed_blocks = token.after(squares, embed_blocks)
            flight["h"] = exchange(embed_blocks)
        elif kind == "spread":
            if name == "0":
                embed_columns = token(flight["h"]).reshape(group * token_rows, columns)
            offset = SPREAD[int(name)]
            uses = jnp.stack(table_indices(group_boxes, (plane + offset) % planes))
            part = token.after(spread_rows(token(uses), embed_columns, entries))
            flight["t" + name] = around(part, planes - offset) if offset else part
        elif step == "tables 0":
            owned = token(*[flight["t" + str(at)] for at in range(planes)])
            table_total = token.after(functools.reduce(jnp.add, owned))
            row_masks = [mask for mask in masks_one if mask >= group]
            if row_masks:
                table_total = halve(
                    relative(
                        table_total,
                        flips_of([mask // group for mask in row_masks]),
                        me // group,
                        entries * group // devices,
                        0,
                    ),
                    row_masks,
                )
            flight["u"] = exchange(table_total.reshape(group, entries // devices, columns))
        elif step == "tables 1":
            table_share = jnp.concatenate(list(token(flight["u"])), 1)
            table_share = token.after(table_share)
        elif step == "vector 0":
            vectors = [
                g_query_bias,
                g_value_bias,
                g_out_bias,
                g_attn_gain,
                g_attn_bias,
                g_in_bias,
                g_back_bias,
                g_ffn_gain,
                g_ffn_bias,
                g_emb_gain,
                g_emb_bias,
                jnp.full((devices,), jnp.sum(squares)),
            ]
            stacked = jnp.concatenate([vector.reshape(devices, -1) for vector in vectors], 1)
            stacked = token.after(token(stacked))
            flight["v1"] = lax.all_to_all(stacked, "pages", 0, 0, tiled=True)
        elif step == "vector 1":
            vector_share = token.after(jnp.sum(token(flight["v1"]), 0, keepdims=True))
            flight["v2"] = lax.ppermute(vector_share, "emb", [(0, 1), (3, 2)])
        elif step == "vector 2":
            vector_share = token.after(vector_share + token(flight["v2"]))
            flight["v3"] = lax.ppermute(vector_share, "emb", [(1, 2), (2, 1)])
        elif step == "vector 3":
            vector_share = token.after(vector_share + token(flight["v3"]))
            flight["v4"] = lax.ppermute(vector_share, "emb", [(1, 0), (2, 3)])
        elif step == "vector 4":
            middle = jnp.logical_or(plane == 1, plane == 2)
            vector_share = jnp.where(middle, vector_share, token(flight["v4"]))[0]
    for name, pieces in SPLIT.items():
        shares[name] = jnp.concatenate([shares[one] for one in pieces], 0)
    g_back = shares["back"]
    g_in = jnp.concatenate(list(shares["in"]), 1)
    g_qkv = jnp.concatenate(list(shares["q"][:3]), 1)
    g_out = shares["q"][3]

    totals = []
    first = 0
    for vector in vectors:
        length = vector.size // devices
        totals.append(vector_share[first : first + length])
        first += length
    entry_count = token_rows * model_width * devices * planes
    rms_grad = jnp.sqrt(totals[11][0] / entry_count)
    return (
        token.mark,
        d_embed,
        table_share[None],
        totals[9],
        totals[10],
        g_qkv,
        totals[0],
        totals[1],
        g_out,
        totals[2],
        totals[3],
        totals[4],
        g_in,
        totals[5],
        g_back,
        totals[6],
        totals[7],
        totals[8],
        rms_grad,
    )


def solution(mesh):
    return jax.shard_map(
        on_device,
        mesh=mesh,
        in_specs=(
            P(("pages", "emb"), None),
            P(None, ("pages", "emb")),
            P("emb", None, None),
            P(),
            P(),
            P(),
            P(),
            P(),
            P(),
            P(),
            P(),
            P(),
            P(),
            P(),
            P(),
            P(),
            P(),
            P(),
            P(("pages", "emb"), None),
        ),
        out_specs=(
            P(("pages", "emb"), None),
            P(("pages", "emb"), None),
            P("emb", "pages", None),
            P("pages"),
            P("pages"),
            P("pages", None),
            P("pages"),
            P("pages"),
            P("pages", None),
            P("pages"),
            P("pages"),
            P("pages"),
            P("pages", None),
            P("pages"),
            P("pages", None),
            P("pages"),
            P("pages"),
            P("pages"),
            P(),
        ),
        check_vma=False,
    )
```

```python
import functools
import itertools

import jax
import jax.numpy as jnp
from jax import lax
from jax.experimental import pallas as pl
from jax.experimental.pallas import tpu as pltpu
from jax.sharding import PartitionSpec as P

HEADS = 16
HEAD = 64
PAGE = 512
PAIR = 2 * HEAD

EPSILON = 1e-05
SQRT_HALF = 0.7071067811865476
INV_ROOT_TAU = 0.3989422804014327

wide = jnp.float32
narrow = jnp.bfloat16
SPREAD = (2, 1, 3, 0)
SPLIT = {"back": ("backa", "backb"), "in": ("ina", "inb"), "q": ("qa", "qb")}
ORDER = (
    "first back",
    "feed all",
    "first in",
    "attend all",
    "embed all",
    "first q",
    "spread 0",
    "next in",
    "spread 1",
    "spread 2",
    "spread 3",
    "fold in",
    "tables 0",
    "finish back",
    "send backa",
    "next q",
    "finish in",
    "send backb",
    "tables 1",
    "exchange backa",
    "send ina",
    "vector 0",
    "exchange backb",
    "return backa",
    "fold q",
    "end backa",
    "send inb",
    "return backb",
    "exchange ina",
    "vector 1",
    "finish q",
    "send qa",
    "send qb",
    "end backb",
    "return ina",
    "exchange inb",
    "vector 2",
    "end ina",
    "return inb",
    "exchange qa",
    "vector 3",
    "end inb",
    "return qa",
    "exchange qb",
    "vector 4",
    "end qa",
    "return qb",
    "end qb",
)
PARTS = 1
LITTLE = pl.CostEstimate(flops=1024, bytes_accessed=1024, transcendentals=0)
ROOM = pltpu.CompilerParams(vmem_limit_bytes=32 * 2**20)
MOST = pltpu.CompilerParams(vmem_limit_bytes=32 * 2**20)


def shape(dims, dtype=wide):
    return jax.ShapeDtypeStruct(dims, dtype)


def whole(*dims):
    return pl.BlockSpec(dims, lambda *_: (0,) * len(dims))


def normalize(values):
    averaged = jnp.mean(values, -1, keepdims=True)
    centered = values - averaged
    inverse = lax.rsqrt(jnp.mean(centered * centered, -1, keepdims=True) + EPSILON)
    return centered * inverse, inverse


def norm_back(incoming, normed, inverse, gain):
    scaled = incoming * gain
    offset_mean = jnp.mean(scaled, -1, keepdims=True)
    along_mean = jnp.mean(scaled * normed, -1, keepdims=True)
    return inverse * (scaled - offset_mean - normed * along_mean)


def down(values):
    return jnp.sum(values, 0, keepdims=True)


def mul(left, right):
    return jnp.dot(left, right, preferred_element_type=wide)


def mul_rows(left, right):
    return lax.dot_general(left, right, (((1,), (1,)), ((), ())), preferred_element_type=wide)


def mul_down(left, right):
    return lax.dot_general(left, right, (((0,), (0,)), ((), ())), preferred_element_type=wide)


def table_indices(box_rows, table):
    left_x, top_y, right_x, bottom_y = box_rows[0], box_rows[1], box_rows[2], box_rows[3]
    first = jnp.where(
        table == 0,
        left_x,
        jnp.where(table == 1, top_y, jnp.where(table == 2, right_x - left_x, bottom_y - top_y)),
    )
    second = jnp.where(table == 0, right_x, jnp.where(table == 1, bottom_y, -1))
    return first, second


def two_halves(values):
    high = values.astype(narrow)
    return high, (values - high.astype(wide)).astype(narrow)


def hits(entry, indices):
    return jnp.where(entry == indices, 1.0, 0.0)


def lookup_kernel(twice_ref, idx_ref, *refs):
    tables, total_ref, out_ref, halves = refs[:-3], refs[-3], refs[-2], refs[-1]
    entries, width = tables[0].shape

    @pl.when(pl.program_id(0) == 0)
    def _():
        for one, table in enumerate(tables):
            halves[one, :, :width], halves[one, :, width:] = two_halves(table[...])

    entry = lax.broadcasted_iota(jnp.int32, (idx_ref.shape[0], entries), 1)

    def add(one, counts):
        rows = mul(counts.astype(narrow), halves[one])
        out_ref[...] += rows[:, :width] + rows[:, width:]

    out_ref[...] = total_ref[...]
    for one in range(len(tables)):
        first = idx_ref[:, 2 * one : 2 * one + 1]
        second = idx_ref[:, 2 * one + 1 : 2 * one + 2]

        @pl.when(twice_ref[one] == 1)
        def _():
            add(one, hits(entry, first) + hits(entry, second))

        @pl.when(twice_ref[one] == 0)
        def _():
            add(one, hits(entry, first))


def add_rows(twice, indices, tables, total, part, parts):
    tokens = total.shape[0]
    entries, width = tables[0].shape
    block = PAGE
    steps = tokens // block // parts
    return pl.pallas_call(
        lookup_kernel,
        grid_spec=pltpu.PrefetchScalarGridSpec(
            num_scalar_prefetch=1,
            grid=(steps,),
            in_specs=[
                pl.BlockSpec((block, indices.shape[1]), lambda step, *_: (steps * part + step, 0))
            ]
            + [whole(entries, width)] * len(tables)
            + [pl.BlockSpec((block, width), lambda step, *_: (steps * part + step, 0))],
            out_specs=pl.BlockSpec((block, width), lambda step, *_: (step, 0)),
            scratch_shapes=[pltpu.VMEM((len(tables), entries, 2 * width), narrow)],
        ),
        out_shape=shape((tokens // parts, width)),
        compiler_params=ROOM,
        cost_estimate=LITTLE,
        name="look_up",
    )(twice, indices, *tables, total)


def spread_kernel(idx_ref, rows_ref, out_ref):
    width = rows_ref.shape[1]
    entry = lax.broadcasted_iota(jnp.int32, (out_ref.shape[0], rows_ref.shape[0]), 0)
    counts = hits(entry, idx_ref[0:1, :]) + hits(entry, idx_ref[1:2, :])
    both = mul(counts.astype(narrow), jnp.concatenate(two_halves(rows_ref[...]), 1))
    share = both[:, :width] + both[:, width:]

    @pl.when(pl.program_id(0) == 0)
    def _():
        out_ref[...] = share

    @pl.when(pl.program_id(0) > 0)
    def _():
        out_ref[...] += share


def spread_rows(indices, rows, entries):
    tokens, width = rows.shape
    block = 2 * PAGE
    return pl.pallas_call(
        spread_kernel,
        grid=(tokens // block,),
        in_specs=[
            pl.BlockSpec((2, block), lambda step: (0, step)),
            pl.BlockSpec((block, width), lambda step: (step, 0)),
        ],
        out_specs=whole(entries, width),
        out_shape=shape((entries, width)),
        compiler_params=ROOM,
        cost_estimate=LITTLE,
        name="spread",
    )(indices, rows)


def project_kernel(*refs):
    parts, (text, gain, bias, weight, weight_bias) = refs[:-9], refs[-9:-4]
    packed, normed, inverse, low = refs[-4:]
    group, rows, width = parts[0].shape

    @pl.when(pl.program_id(0) == 0)
    def _():
        for at, part in enumerate(parts):
            for one in range(group):
                normed[at * rows : (at + 1) * rows, one * width : (one + 1) * width] = part[one]
        normed[...], inverse[...] = normalize(normed[...] + text[...].astype(wide))
        low[...] = (normed[...] * gain[...] + bias[...]).astype(narrow)

    packed[...] = (mul(low[...], weight[...]) + weight_bias[...]).astype(narrow)


def embed_and_project(parts, text, gain, bias, weight, weight_bias):
    tokens, width = text.shape
    block = width // 2
    steps = weight.shape[1] // block
    return pl.pallas_call(
        project_kernel,
        grid=(steps,),
        in_specs=[whole(*part.shape) for part in parts]
        + [
            whole(tokens, width),
            whole(1, width),
            whole(1, width),
            pl.BlockSpec((width, block), lambda step: (0, step)),
            pl.BlockSpec((1, block), lambda step: (0, step)),
        ],
        out_specs=[
            pl.BlockSpec((tokens, block), lambda step: (0, step)),
            whole(tokens, width),
            whole(tokens, 1),
            whole(tokens, width),
        ],
        out_shape=[
            shape((tokens, weight.shape[1]), narrow),
            shape((tokens, width)),
            shape((tokens, 1)),
            shape((tokens, width), narrow),
        ],
        compiler_params=ROOM,
        cost_estimate=LITTLE,
        name="embed_and_project",
    )(*parts, text, gain, bias, weight, weight_bias)


def one_head(rows, head):
    lane = lax.broadcasted_iota(jnp.int32, rows.shape, 1)
    return jnp.where((lane < HEAD) == (head == 0), rows, jnp.zeros_like(rows))


def head_probs(queries, keys, head):
    scores = mul_rows(one_head(queries, head), keys) * HEAD ** (-0.5)
    exponent = jnp.exp(scores - jnp.max(scores, -1, keepdims=True))
    return exponent * (1.0 / jnp.sum(exponent, -1, keepdims=True))


def attend_kernel(
    queries, keys, values, weight, weight_bias, normed_emb, emb_gain, emb_bias, gain, bias,
    context, normed, inverse, low,
):
    pair = pl.program_id(0)
    lane = lax.broadcasted_iota(jnp.int32, values.shape, 1)
    parts = []
    for head in range(2):
        scores = mul_rows(one_head(queries[...], head), keys[...]) * HEAD ** (-0.5)
        exponent = jnp.exp(scores - jnp.max(scores, -1, keepdims=True))
        probs = exponent * (1.0 / jnp.sum(exponent, -1, keepdims=True))
        parts.append(mul(probs.astype(narrow), values[...]))
    place = pl.multiple_of(pair * PAIR, PAIR)
    context[:, pl.ds(place, PAIR)] = jnp.where(lane < HEAD, parts[0], parts[1]).astype(narrow)

    @pl.when(pair == pl.num_programs(0) - 1)
    def _():
        hidden = normed_emb[...] * emb_gain[...] + emb_bias[...]
        attended = mul(context[...], weight[...]) + weight_bias[...]
        normed[...], inverse[...] = normalize(hidden + attended)
        low[...] = (normed[...] * gain[...] + bias[...]).astype(narrow)


def attend(packed, weight, weight_bias, normed_emb, emb_gain, emb_bias, gain, bias):
    tokens, width = normed_emb.shape
    pairs = width // PAIR
    vector = whole(1, width)
    return pl.pallas_call(
        attend_kernel,
        grid=(pairs,),
        in_specs=[
            pl.BlockSpec((tokens, PAIR), lambda pair: (0, pair)),
            pl.BlockSpec((tokens, PAIR), lambda pair: (0, pairs + pair)),
            pl.BlockSpec((tokens, PAIR), lambda pair: (0, 2 * pairs + pair)),
            whole(*weight.shape),
            vector,
            whole(tokens, width),
            vector,
            vector,
            vector,
            vector,
        ],
        out_specs=[
            whole(tokens, width),
            whole(tokens, width),
            whole(tokens, 1),
            whole(tokens, width),
        ],
        out_shape=[
            shape((tokens, width), narrow),
            shape((tokens, width)),
            shape((tokens, 1)),
            shape((tokens, width), narrow),
        ],
        compiler_params=ROOM,
        cost_estimate=LITTLE,
        name="attend",
    )(packed, packed, packed, weight, weight_bias, normed_emb, emb_gain, emb_bias, gain, bias)


def feed_kernel(
    low, w_in, b_in, w_back, b_back, normed_attn, attn_gain, attn_bias, gain, bias, cotangent,
    pre_act, expanded, output, d_r2, d_returned, g_gain, g_bias, g_back_bias, total,
):
    step = pl.program_id(0)
    pre = mul(low[...], w_in[...]) + b_in[...]
    pre_act[...] = pre
    expanded[...] = (pre * (0.5 * (1.0 + lax.erf(pre * SQRT_HALF)))).astype(narrow)
    share = mul(expanded[...], w_back[...])

    @pl.when(step == 0)
    def _():
        total[...] = share

    @pl.when(step > 0)
    def _():
        total[...] += share

    @pl.when(step == pl.num_programs(0) - 1)
    def _():
        hidden = normed_attn[...] * attn_gain[...] + attn_bias[...]
        normed, inverse = normalize(hidden + (total[...] + b_back[...]))
        output[...] = (normed * gain[...] + bias[...]).astype(narrow)
        incoming = cotangent[...].astype(wide)
        d_r2[...] = norm_back(incoming, normed, inverse, gain[...])
        g_gain[...] = down(incoming * normed)
        g_bias[...] = down(incoming)
        rounded = d_r2[...].astype(narrow)
        d_returned[...] = rounded
        g_back_bias[...] = down(rounded.astype(wide))


def feed(low, w_in, b_in, w_back, b_back, normed, attn_gain, attn_bias, gain, bias, cotangent):
    tokens, width = low.shape
    expand = w_in.shape[1]
    block = width // 2
    vector = whole(1, width)
    rows = whole(tokens, width)
    part = pl.BlockSpec((tokens, block), lambda step: (0, step))
    return pl.pallas_call(
        feed_kernel,
        grid=(expand // block,),
        in_specs=[
            rows,
            pl.BlockSpec((width, block), lambda step: (0, step)),
            pl.BlockSpec((1, block), lambda step: (0, step)),
            pl.BlockSpec((block, width), lambda step: (step, 0)),
            vector,
            rows,
            vector,
            vector,
            vector,
            vector,
            rows,
        ],
        out_specs=[part, part, rows, rows, rows, vector, vector, vector],
        out_shape=[
            shape((tokens, expand)),
            shape((tokens, expand), narrow),
            shape((tokens, width), narrow),
            shape((tokens, width)),
            shape((tokens, width), narrow),
            shape((1, width)),
            shape((1, width)),
            shape((1, width)),
        ],
        scratch_shapes=[pltpu.VMEM((tokens, width), wide)],
        compiler_params=ROOM,
        cost_estimate=LITTLE,
        name="feed",
    )(low, w_in, b_in, w_back, b_back, normed, attn_gain, attn_bias, gain, bias, cotangent)


def gelu_slope(pre_act):
    return (
        0.5 * (1.0 + lax.erf(pre_act * SQRT_HALF))
        + pre_act * jnp.exp(-0.5 * pre_act * pre_act) * INV_ROOT_TAU
    )


def feed_back_kernel(
    d_returned, w_back, pre_act, w_in, d_r2, normed, inverse, gain,
    d_pre, g_in_bias, d_r1, d_attended, g_gain, g_bias, g_out_bias, total,
):
    step = pl.program_id(0)
    rounded = (mul_rows(d_returned[...], w_back[...]) * gelu_slope(pre_act[...])).astype(narrow)
    d_pre[...] = rounded
    g_in_bias[...] = down(rounded.astype(wide))
    share = mul_rows(rounded, w_in[...])

    @pl.when(step == 0)
    def _():
        total[...] = share

    @pl.when(step > 0)
    def _():
        total[...] += share

    @pl.when(step == pl.num_programs(0) - 1)
    def _():
        incoming = d_r2[...] + total[...]
        d_r1[...] = norm_back(incoming, normed[...], inverse[...], gain[...])
        g_gain[...] = down(incoming * normed[...])
        g_bias[...] = down(incoming)
        d_attended[...] = d_r1[...].astype(narrow)
        g_out_bias[...] = down(d_attended[...].astype(wide))


def feed_back(d_returned, w_back, pre_act, w_in, d_r2, normed, inverse, gain):
    tokens, width = d_returned.shape
    expand = pre_act.shape[1]
    block = width // 2
    vector = whole(1, width)
    rows = whole(tokens, width)
    part = pl.BlockSpec((tokens, block), lambda step: (0, step))
    return pl.pallas_call(
        feed_back_kernel,
        grid=(expand // block,),
        in_specs=[
            rows,
            pl.BlockSpec((block, width), lambda step: (step, 0)),
            part,
            pl.BlockSpec((width, block), lambda step: (0, step)),
            rows,
            rows,
            whole(tokens, 1),
            vector,
        ],
        out_specs=[
            part,
            pl.BlockSpec((1, block), lambda step: (0, step)),
            rows,
            rows,
            vector,
            vector,
            vector,
        ],
        out_shape=[
            shape((tokens, expand), narrow),
            shape((1, expand)),
            shape((tokens, width)),
            shape((tokens, width), narrow),
            shape((1, width)),
            shape((1, width)),
            shape((1, width)),
        ],
        scratch_shapes=[pltpu.VMEM((tokens, width), wide)],
        compiler_params=MOST,
        cost_estimate=LITTLE,
        name="feed_back",
    )(d_returned, w_back, pre_act, w_in, d_r2, normed, inverse, gain)


def attend_back_kernel(
    queries, keys, values, d_attended, weight, d_packed, g_query_bias, g_value_bias
):
    d_context = mul_rows(d_attended[...], weight[...]).astype(narrow)
    d_queries, d_keys, d_values = 0.0, 0.0, 0.0
    for head in range(2):
        probs = head_probs(queries[...], keys[...], head)
        own_context = one_head(d_context, head)
        d_values += mul_down(probs.astype(narrow), own_context)
        d_probs = mul_rows(own_context, values[...])
        along = jnp.sum(probs * d_probs, -1, keepdims=True)
        d_scores = (probs * (d_probs - along)).astype(narrow)
        d_queries += mul(d_scores, one_head(keys[...], head))
        d_keys += mul_down(d_scores, one_head(queries[...], head))
    d_queries = (d_queries * HEAD ** (-0.5)).astype(narrow)
    d_values = d_values.astype(narrow)
    d_packed[0] = d_queries
    d_packed[1] = (d_keys * HEAD ** (-0.5)).astype(narrow)
    d_packed[2] = d_values
    g_query_bias[...] = down(d_queries.astype(wide))
    g_value_bias[...] = down(d_values.astype(wide))


def attend_back(packed, d_attended, weight):
    tokens, width = d_attended.shape
    pairs = width // PAIR
    return pl.pallas_call(
        attend_back_kernel,
        grid=(pairs,),
        in_specs=[
            pl.BlockSpec((tokens, PAIR), lambda pair: (0, pair)),
            pl.BlockSpec((tokens, PAIR), lambda pair: (0, pairs + pair)),
            pl.BlockSpec((tokens, PAIR), lambda pair: (0, 2 * pairs + pair)),
            whole(tokens, width),
            pl.BlockSpec((PAIR, width), lambda pair: (pair, 0)),
        ],
        out_specs=[
            pl.BlockSpec((3, tokens, PAIR), lambda pair: (0, 0, pair)),
            pl.BlockSpec((1, PAIR), lambda pair: (0, pair)),
            pl.BlockSpec((1, PAIR), lambda pair: (0, pair)),
        ],
        out_shape=[shape((3, tokens, width), narrow), shape((1, width)), shape((1, width))],
        compiler_params=MOST,
        cost_estimate=LITTLE,
        name="attend_back",
    )(packed, packed, packed, d_attended, weight)


def embed_back_kernel(
    d_packed, weight, d_r1, normed, inverse, gain, d_embed, g_gain, g_bias, squares, blocks, total
):
    step = pl.program_id(0)
    share = mul_rows(d_packed[0], weight[...])

    @pl.when(step == 0)
    def _():
        total[...] = d_r1[...] + share

    @pl.when(step > 0)
    def _():
        total[...] += share

    @pl.when(step == pl.num_programs(0) - 1)
    def _():
        incoming = total[...]
        d_embed[...] = norm_back(incoming, normed[...], inverse[...], gain[...])
        g_gain[...] = down(incoming * normed[...])
        g_bias[...] = down(incoming)
        squares[...] = down(d_embed[...] * d_embed[...])
        columns = blocks.shape[2]
        for one in range(blocks.shape[0]):
            blocks[one] = d_embed[:, one * columns : (one + 1) * columns]


def embed_back(group, d_packed, weight, d_r1, normed, inverse, gain):
    tokens, width = d_r1.shape
    block = width // 2
    vector = whole(1, width)
    rows = whole(tokens, width)
    columns = width // group
    return pl.pallas_call(
        embed_back_kernel,
        grid=(3 * width // block,),
        in_specs=[
            pl.BlockSpec((1, tokens, block), lambda step: (step // 2, 0, step % 2)),
            pl.BlockSpec((width, block), lambda step: (0, step)),
            rows,
            rows,
            whole(tokens, 1),
            vector,
        ],
        out_specs=[rows, vector, vector, vector, whole(group, tokens, columns)],
        scratch_shapes=[pltpu.VMEM((tokens, width), wide)],
        out_shape=[
            shape((tokens, width)),
            shape((1, width)),
            shape((1, width)),
            shape((1, width)),
            shape((group, tokens, columns)),
        ],
        compiler_params=MOST,
        cost_estimate=LITTLE,
        name="embed_back",
    )(d_packed, weight, d_r1, normed, inverse, gain)


def outer_kernel(left, right, out):
    out[...] = mul_down(left[...], right[...].reshape(right.shape[-2:]))


def outer(left, right):
    tokens, rows = left.shape
    width = right.shape[1]
    block = min(rows, 512)
    return pl.pallas_call(
        outer_kernel,
        grid=(rows // block,),
        in_specs=[pl.BlockSpec((tokens, block), lambda row: (0, row)), whole(tokens, width)],
        out_specs=pl.BlockSpec((block, width), lambda row: (row, 0)),
        out_shape=shape((rows, width)),
        compiler_params=MOST,
        cost_estimate=LITTLE,
        name="outer",
    )(left, right)


def flat(ref):
    return ref[...].reshape(ref.shape[-2:])


def product(left, right):
    return mul_down(left, right) if left.shape[0] == right.shape[0] else mul(left, right)


def first_kernel(plan, table, *refs):
    count = len(plan)
    lefts, rights, out = refs[:count], refs[count : 2 * count], refs[-1]
    for one in range(count):
        out[one] = product(lefts[one][...], flat(rights[one]))


def next_kernel(plan, table, *refs):
    count = len(plan)
    keeps, sends, rights = refs[:count], refs[count : 2 * count], refs[2 * count : 3 * count]
    arrived_keep, arrived_send, kept, sent_one, sent_two = refs[3 * count :]
    for one in range(count):
        right = flat(rights[one])
        kept[one] = product(keeps[one][...], right) + arrived_keep[one]
        sent = sent_one if one < count // 2 else sent_two
        sent[one % (count // 2)] = product(sends[one][...], right) + arrived_send[one]


class Halving:
    def __init__(self, me, masks_one, masks_two, streams, width):
        self.masks = (masks_one, masks_two)
        self.devices = lax.axis_size("pages")
        self.width = width
        self.rows = streams[0][0].shape[1] // self.devices
        self.across = self.rows % 128 == 0
        self.streams = [
            (left if self.across else left.T, *rest) for left, *rest in streams
        ]
        self.table = jnp.concatenate(
            [
                jnp.bitwise_xor(me, jnp.array(flips_of(masks), jnp.int32))
                for masks in self.masks
            ]
        )

    def left(self, one, start):
        place = (one >= len(self.streams) // 2) * self.devices + start
        left = self.streams[one][0]
        if self.across:
            return pl.BlockSpec(
                (left.shape[0], self.rows), lambda row, table: (0, table[place + row])
            )
        return pl.BlockSpec(
            (self.rows, left.shape[1]), lambda row, table: (table[place + row], 0)
        )

    def right(self, one):
        _, right, part, column = self.streams[one]
        if right.ndim == 3:
            return pl.BlockSpec((1, right.shape[1], self.width), lambda *_: (part, 0, column))
        return pl.BlockSpec((right.shape[0], self.width), lambda *_: (0, column))

    def block(self, count, start):
        return pl.BlockSpec((count, self.rows, self.width), lambda row, *_: (0, start + row, 0))

    def first(self, table):
        half = self.devices // 2
        count = len(self.streams)
        return pl.pallas_call(
            functools.partial(first_kernel, self.streams),
            grid_spec=pltpu.PrefetchScalarGridSpec(
                num_scalar_prefetch=1,
                grid=(half,),
                in_specs=[self.left(one, half) for one in range(count)]
                + [self.right(one) for one in range(count)],
                out_specs=self.block(count, 0),
            ),
            out_shape=shape((count, half * self.rows, self.width)),
            compiler_params=MOST,
            cost_estimate=LITTLE,
            name="halving_first",
        )(table, *[one[0] for one in self.streams], *[one[1] for one in self.streams])

    def next(self, table, arrived):
        quarter = self.devices // 4
        count = len(self.streams)
        lefts = [one[0] for one in self.streams]
        return pl.pallas_call(
            functools.partial(next_kernel, self.streams),
            grid_spec=pltpu.PrefetchScalarGridSpec(
                num_scalar_prefetch=1,
                grid=(quarter,),
                in_specs=[self.left(one, 0) for one in range(count)]
                + [self.left(one, quarter) for one in range(count)]
                + [self.right(one) for one in range(count)]
                + [self.block(count, 0), self.block(count, quarter)],
                out_specs=[
                    self.block(count, 0),
                    self.block(count // 2, 0),
                    self.block(count // 2, 0),
                ],
            ),
            out_shape=[
                shape((part, quarter * self.rows, self.width))
                for part in (count, count // 2, count // 2)
            ],
            compiler_params=MOST,
            cost_estimate=LITTLE,
            name="halving_next",
        )(table, *lefts, *lefts, *[one[1] for one in self.streams], arrived, arrived)

    def start(self, token):
        self.from_core = swap(token.after(self.first(token(self.table))), 1)

    def second(self, token):
        self.kept, *sent = token.after(*self.next(self.table, token(self.from_core)))
        self.arrived = [swap(one, masks[1]) for one, masks in zip(sent, self.masks)]

    def third(self, token):
        for at in range(2, len(self.masks[0])):
            arrived = jnp.concatenate(token(*self.arrived), 0)
            middle = self.kept.shape[1] // 2
            half = len(self.streams) // 2
            sent = self.kept[:, middle:] + arrived[:, middle:]
            sent = token.after(sent[:half], sent[half:])
            self.kept = self.kept[:, :middle] + arrived[:, :middle]
            self.arrived = [swap(one, masks[at]) for one, masks in zip(sent, self.masks)]

    def shares(self, token):
        return self.kept + jnp.concatenate(token(*self.arrived), 0)


class Token:
    def __init__(self, mark):
        self.mark = mark

    def __call__(self, *values):
        *values, self.mark = lax.optimization_barrier((*values, self.mark))
        return values[0] if len(values) == 1 else values

    after = __call__


def flips_of(masks):
    return [
        sum(mask for mask, flip in zip(masks, flips) if flip)
        for flips in itertools.product((0, 1), repeat=len(masks))
    ]


def relative(array, offsets, me, size, axis):
    blocks = [
        lax.dynamic_slice_in_dim(array, jnp.bitwise_xor(me, offset) * size, size, axis)
        for offset in offsets
    ]
    return jnp.concatenate(blocks, axis)


def swap(array, mask):
    return lax.ppermute(
        array, "pages", [(one, one ^ mask) for one in range(lax.axis_size("pages"))]
    )


def fold(kept, arrived):
    half = kept.shape[0] // 2
    return kept[:half] + arrived[:half], kept[half:] + arrived[half:]


def halve(kept, masks):
    for mask in masks:
        half = kept.shape[0] // 2
        kept = kept[:half] + swap(kept[half:], mask)
    return kept


def in_order(*values):
    return lax.optimization_barrier(values)


def emb_total(share):
    if lax.axis_size("emb") != 4:
        return lax.psum(share, "emb")
    plane = lax.axis_index("emb")
    middle = jnp.logical_or(plane == 1, plane == 2)
    share = share + lax.ppermute(share, "emb", [(0, 1), (3, 2)])
    share = share + lax.ppermute(share, "emb", [(1, 2), (2, 1)])
    return jnp.where(middle, share, lax.ppermute(share, "emb", [(1, 0), (2, 3)]))


def on_device(
    text_embed,
    boxes,
    layout_tables,
    emb_gain,
    emb_bias,
    w_qkv,
    b_query,
    b_value,
    w_out,
    b_out,
    attn_gain,
    attn_bias,
    w_in,
    b_in,
    w_back,
    b_back,
    ffn_gain,
    ffn_bias,
    cotangent,
):
    token_rows = text_embed.shape[0]
    model_width = text_embed.shape[1]
    entries = layout_tables.shape[1]
    me = lax.axis_index("pages")
    plane = lax.axis_index("emb")
    devices = lax.axis_size("pages")
    planes = lax.axis_size("emb")
    outer_masks = [1 << bit for bit in range(1, devices.bit_length() - 1)]
    turn = len(outer_masks) // 2
    masks_one = [1] + outer_masks
    masks_two = [1] + outer_masks[turn:] + outer_masks[:turn]
    group = min(devices, 8)
    inner = me % group
    columns = model_width // group
    groups = [list(range(first, first + group)) for first in range(0, devices, group)]

    def row(vector):
        return vector.reshape(1, -1)

    def around(array, offset):
        return lax.ppermute(
            array, "emb", [((one + offset) % planes, one) for one in range(planes)]
        )

    def exchange(blocks):
        return lax.all_to_all(blocks, "pages", 0, 0, tiled=True, axis_index_groups=groups)

    own_columns = lax.dynamic_slice_in_dim(layout_tables[0], inner * columns, columns, 1)
    table_columns = [own_columns] + [around(own_columns, offset) for offset in range(1, planes)]
    group_boxes = lax.all_gather(boxes, "pages", axis=1, tiled=True, axis_index_groups=groups)
    tables = [(plane + offset) % planes for offset in range(planes)]
    twice = jnp.stack([jnp.where(table < 2, 1, 0) for table in tables]).astype(jnp.int32)
    split_boxes = group_boxes.reshape(4, group, PARTS, token_rows // PARTS).swapaxes(1, 2)
    split_boxes = split_boxes.reshape(4, group * token_rows)
    uses = jnp.stack([one for table in tables for one in table_indices(split_boxes, table)]).T
    def look_up(chosen, total, part, parts):
        return add_rows(
            jnp.stack([twice[one] for one in chosen]),
            jnp.concatenate([uses[:, 2 * one : 2 * one + 2] for one in chosen], 1),
            [table_columns[one] for one in chosen],
            total,
            part,
            parts,
        )

    looked_up = jnp.zeros((group * token_rows, columns), wide)
    near = sorted({1, planes - 1})
    for chosen in ([0], near):
        looked_up = look_up(chosen, looked_up, 0, 1)
    parts = [
        exchange(
            look_up(list(range(2, planes - 1)), looked_up, part, PARTS).reshape(group, token_rows // PARTS, columns)
        )
        for part in range(PARTS)
    ]

    bias_qkv = jnp.concatenate([b_query, jnp.zeros_like(b_query), b_value])
    packed, normed_emb, inverse_emb, emb_low = embed_and_project(
        parts, text_embed, row(emb_gain), row(emb_bias), w_qkv, row(bias_qkv)
    )
    context_low, normed_attn, inverse_attn, attn_low = attend(
        packed,
        w_out,
        row(b_out),
        normed_emb,
        row(emb_gain),
        row(emb_bias),
        row(attn_gain),
        row(attn_bias),
    )
    pre_act, expanded, output, d_r2, d_returned, g_ffn_gain, g_ffn_bias, g_back_bias = feed(
        attn_low,
        w_in,
        row(b_in),
        w_back,
        row(b_back),
        normed_attn,
        row(attn_gain),
        row(attn_bias),
        row(ffn_gain),
        row(ffn_bias),
        cotangent,
    )

    token = Token(output)
    flight = {}

    def gather_pages(product):
        return lax.psum_scatter(product, "pages", scatter_dimension=0, tiled=True)

    def inward(share):
        return lax.ppermute(share, "emb", [(0, 1), (3, 2)])

    def across(share):
        return lax.ppermute(share, "emb", [(1, 2), (2, 1)])

    def outward(share):
        return lax.ppermute(share, "emb", [(1, 0), (2, 3)])

    def settled(share, arrived):
        return jnp.where(jnp.logical_or(plane == 1, plane == 2), share, arrived)

    shares, halvings = {}, {}
    for step in ORDER:
        kind, name = step.split()
        if step == "first back":
            flight[name] = gather_pages(token.after(outer(expanded, token(d_returned))))
        elif step == "feed all":
            d_pre, g_in_bias, d_r1, d_attended, g_attn_gain, g_attn_bias, g_out_bias = feed_back(
                d_returned,
                w_back,
                pre_act,
                w_in,
                d_r2,
                normed_attn,
                inverse_attn,
                token(row(attn_gain)),
            )
            d_pre, d_attended = token.after(d_pre, d_attended)
            halvings["in"] = Halving(
                me,
                masks_one,
                masks_two,
                [(attn_low, d_pre, 0, one) for one in range(4)],
                model_width,
            )
        elif step == "attend all":
            d_packed, g_query_bias, g_value_bias = attend_back(packed, token(d_attended), w_out)
            d_packed = token.after(d_packed)
            halvings["q"] = Halving(
                me,
                masks_one,
                masks_two,
                [(emb_low, d_packed, one, 0) for one in range(3)]
                + [(context_low, d_attended, 0, 0)],
                model_width,
            )
        elif kind == "first":
            halvings[name].start(token)
        elif kind == "next":
            halvings[name].second(token)
        elif kind == "fold":
            halvings[name].third(token)
        elif kind == "finish":
            share = halvings[name].shares(token) if name in halvings else token(flight[name])
            pieces = SPLIT.get(name, (name,))
            size = share.shape[0] // len(pieces)
            share = token.after(
                *[share[at * size : (at + 1) * size] for at in range(len(pieces))]
            )
            shares.update(zip(pieces, share))
        elif kind == "send":
            shares[name] = token(shares[name])
            flight[name] = inward(shares[name])
        elif kind == "exchange":
            shares[name] = token.after(shares[name] + token(flight[name]))
            flight[name] = across(shares[name])
        elif kind == "return":
            shares[name] = token.after(shares[name] + token(flight[name]))
            flight[name] = outward(shares[name])
        elif kind == "end":
            shares[name] = token.after(settled(shares[name], token(flight[name])))
        elif kind == "embed":
            d_embed, g_emb_gain, g_emb_bias, squares, embed_blocks = embed_back(
                group,
                d_packed,
                w_qkv,
                d_r1,
                normed_emb,
                inverse_emb,
                token(row(emb_gain)),
            )
            squares, embed_blocks = token.after(squares, embed_blocks)
            flight["h"] = exchange(embed_blocks)
        elif kind == "spread":
            if name == "0":
                embed_columns = token(flight["h"]).reshape(group * token_rows, columns)
            offset = SPREAD[int(name)]
            uses = jnp.stack(table_indices(group_boxes, (plane + offset) % planes))
            part = token.after(spread_rows(token(uses), embed_columns, entries))
            flight["t" + name] = around(part, planes - offset) if offset else part
        elif step == "tables 0":
            owned = token(*[flight["t" + str(at)] for at in range(planes)])
            table_total = token.after(functools.reduce(jnp.add, owned))
            row_masks = [mask for mask in masks_one if mask >= group]
            if row_masks:
                table_total = halve(
                    relative(
                        table_total,
                        flips_of([mask // group for mask in row_masks]),
                        me // group,
                        entries * group // devices,
                        0,
                    ),
                    row_masks,
                )
            flight["u"] = exchange(table_total.reshape(group, entries // devices, columns))
        elif step == "tables 1":
            table_share = jnp.concatenate(list(token(flight["u"])), 1)
            table_share = token.after(table_share)
        elif step == "vector 0":
            vectors = [
                g_query_bias,
                g_value_bias,
                g_out_bias,
                g_attn_gain,
                g_attn_bias,
                g_in_bias,
                g_back_bias,
                g_ffn_gain,
                g_ffn_bias,
                g_emb_gain,
                g_emb_bias,
                jnp.full((devices,), jnp.sum(squares)),
            ]
            stacked = jnp.concatenate([vector.reshape(devices, -1) for vector in vectors], 1)
            stacked = token.after(token(stacked))
            flight["v1"] = lax.all_to_all(stacked, "pages", 0, 0, tiled=True)
        elif step == "vector 1":
            vector_share = token.after(jnp.sum(token(flight["v1"]), 0, keepdims=True))
            flight["v2"] = lax.ppermute(vector_share, "emb", [(0, 1), (3, 2)])
        elif step == "vector 2":
            vector_share = token.after(vector_share + token(flight["v2"]))
            flight["v3"] = lax.ppermute(vector_share, "emb", [(1, 2), (2, 1)])
        elif step == "vector 3":
            vector_share = token.after(vector_share + token(flight["v3"]))
            flight["v4"] = lax.ppermute(vector_share, "emb", [(1, 0), (2, 3)])
        elif step == "vector 4":
            middle = jnp.logical_or(plane == 1, plane == 2)
            vector_share = jnp.where(middle, vector_share, token(flight["v4"]))[0]
    for name, pieces in SPLIT.items():
        shares[name] = jnp.concatenate([shares[one] for one in pieces], 0)
    g_back = shares["back"]
    g_in = jnp.concatenate(list(shares["in"]), 1)
    g_qkv = jnp.concatenate(list(shares["q"][:3]), 1)
    g_out = shares["q"][3]

    totals = []
    first = 0
    for vector in vectors:
        length = vector.size // devices
        totals.append(vector_share[first : first + length])
        first += length
    entry_count = token_rows * model_width * devices * planes
    rms_grad = jnp.sqrt(totals[11][0] / entry_count)
    return (
        token.mark,
        d_embed,
        table_share[None],
        totals[9],
        totals[10],
        g_qkv,
        totals[0],
        totals[1],
        g_out,
        totals[2],
        totals[3],
        totals[4],
        g_in,
        totals[5],
        g_back,
        totals[6],
        totals[7],
        totals[8],
        rms_grad,
    )


def solution(mesh):
    return jax.shard_map(
        on_device,
        mesh=mesh,
        in_specs=(
            P(("pages", "emb"), None),
            P(None, ("pages", "emb")),
            P("emb", None, None),
            P(),
            P(),
            P(),
            P(),
            P(),
            P(),
            P(),
            P(),
            P(),
            P(),
            P(),
            P(),
            P(),
            P(),
            P(),
            P(("pages", "emb"), None),
        ),
        out_specs=(
            P(("pages", "emb"), None),
            P(("pages", "emb"), None),
            P("emb", "pages", None),
            P("pages"),
            P("pages"),
            P("pages", None),
            P("pages"),
            P("pages"),
            P("pages", None),
            P("pages"),
            P("pages"),
            P("pages"),
            P("pages", None),
            P("pages"),
            P("pages", None),
            P("pages"),
            P("pages"),
            P("pages"),
            P(),
        ),
        check_vma=False,
    )
```
